512 devices in a mesh: lat: 32 (over z_lo, x), lon: 16 (over y, z_hi, core).
Axes of the slice: x: 4, y: 4, z: 16 (z_hi: 2, z_lo: 8; z = z_hi * 8 + z_lo), core: 2. Of those that a mesh axis runs over, the one named last changes fastest.
Arguments:
- ocean_state: float32 [8, 48, 256, 2048], P(None, None, 'lat', 'lon'), may hold values from -6 to 6
- viscosity: float32 [47, 256, 2048], P(None, 'lat', 'lon'), may hold values from 0.02 to 20
- diffusivity: float32 [47, 256, 2048], P(None, 'lat', 'lon'), may hold values from 0.01 to 10
- wet_levels: int32 [256, 2048], P('lat', 'lon'), may hold values from 0 to 48
- storage: float32 [256, 2048], P('lat', 'lon'), may hold values from 0.2 to 2
- surface_old: float32 [256, 2048], P('lat', 'lon'), may hold values from -9 to 9
Outputs:
- mixed_state: float32 [8, 48, 256, 2048], P(None, None, 'lat', 'lon')
- surface: float32 [256, 2048], P('lat', 'lon')
The draws below stay inside these ranges and needn't reach their ends.
All inputs are finite; a program needn't handle non-finite values.
Results may differ from the reference program's by a relative error of at most 0.0003.
Values sent between devices are 32-bit elements; how exact they have to be, the bound alone decides.
No kernel may reach another device: no remote copies, remote signals or barrier semaphores. Data moves between devices by JAX's collectives and lax.ppermute only.
A program may use at most 128 MiB of HBM per device.

```python
import math
import jax
import jax.numpy as jnp

KLEV = 48
KINT = 47
ITERS = 3
NLAT = 256
NLON = 2048


def draw_wet_levels(key, part):
    key = jax.random.fold_in(key, 11)
    land_key, depth_key = jax.random.split(key)
    land_draw = jax.random.randint(land_key, (NLAT, NLON), 0, 4)
    depth_draw = jax.random.randint(depth_key, (NLAT, NLON), 1, KLEV + 1)
    levels = jnp.where(land_draw == 0, 0, depth_draw)
    levels = levels.at[0, 0].set(KLEV).at[0, 1].set(0)
    return levels.astype(jnp.int32)


def draw_surface_old(key, part):
    key = jax.random.fold_in(key, 5)
    row_ramp = 1.0 + 2.0 * jnp.arange(NLAT, dtype=jnp.float32)[:, None] / max(NLAT - 1, 1)
    base_draw = jnp.clip(jax.random.normal(key, (NLAT, NLON), jnp.float32), -3.0, 3.0)
    return base_draw * row_ramp


def block_scale(key, extent, cuts, smallest, largest):
    factor_of = 1.0
    for axis_at, parts in cuts:
        heights = jax.random.uniform(jax.random.fold_in(jax.random.fold_in(key, 6), axis_at), (parts,), jnp.float32, smallest / len(cuts), largest / len(cuts))
        factor_of = factor_of * jnp.repeat(jnp.exp(heights), extent[axis_at] // parts).reshape((-1,) + (1,) * (len(extent) - 1 - axis_at))
    return factor_of


def centred(own_key, extent, width, limit, cuts=(), kind=jnp.bfloat16):
    gain = block_scale(own_key, extent, cuts, -0.22, 0.18) if cuts else 1.0
    entries = jax.random.normal(own_key, extent, jnp.float32) * width * gain
    return jnp.minimum(jnp.maximum(entries, -limit), limit).astype(kind)


def setup_inputs(seed: int = 0) -> dict:
    seeds = jax.random.split(jax.random.key(seed), 7)
    return {
        "ocean_state": centred(seeds[0], (8, KLEV, NLAT, NLON), 1.0, 6.0, ((2, 32), (3, 16)), jnp.float32),
        "viscosity": jnp.clip(jnp.exp(math.log(20.0) - 6.9077553 * jax.random.uniform(seeds[1], (KINT, NLAT, NLON), jnp.float32) ** block_scale(seeds[1], (KINT, NLAT, NLON), ((1, 32), (2, 16)), -0.2, 0.2)), 0.02, 20.0),
        "diffusivity": jnp.clip(jnp.exp(math.log(10.0) - 6.9077553 * jax.random.uniform(seeds[2], (KINT, NLAT, NLON), jnp.float32) ** block_scale(seeds[2], (KINT, NLAT, NLON), ((1, 32), (2, 16)), -0.2, 0.2)), 0.01, 10.0),
        "wet_levels": draw_wet_levels(jax.random.fold_in(seeds[6], 71), 0),
        "storage": jnp.clip(jnp.exp(math.log(2.0) - 2.3025851 * jax.random.uniform(seeds[4], (NLAT, NLON), jnp.float32) ** block_scale(seeds[4], (NLAT, NLON), ((0, 32), (1, 16)), -0.2, 0.2)), 0.2, 2.0),
        "surface_old": draw_surface_old(jax.random.fold_in(seeds[6], 71), 0),
    }


HORIZONTAL_RATE = 0.2
FLUX_SCALE = 0.02
FACE_SCALE = 0.25


def thickness_of(levels):
    return 0.5 + jnp.arange(levels, dtype=jnp.float32) / levels


def neighbours(values, flip):
    east_side = jnp.roll(values, -1, axis=-1)
    west_side = jnp.roll(values, 1, axis=-1)
    zero_row = jnp.zeros_like(values[..., :1, :])
    south_side = jnp.concatenate([zero_row, values[..., :-1, :]], axis=-2)
    folded = values[..., -1:, ::-1] * flip
    north_side = jnp.concatenate([values[..., 1:, :], folded], axis=-2)
    return east_side, west_side, north_side, south_side


def face_counts(level_count, neighbour_set):
    return tuple(jnp.minimum(level_count, neighbour) for neighbour in neighbour_set)


def column_depth(level_count, thickness):
    level_axis = jnp.arange(thickness.shape[0], dtype=jnp.float32)[:, None, None]
    return jnp.sum(jnp.where(level_axis < level_count[None], thickness[:, None, None], 0.0), axis=0)


def depth_sum(component, level_count, thickness):
    level_axis = jnp.arange(thickness.shape[0], dtype=jnp.float32)[:, None, None]
    return jnp.sum(jnp.where(level_axis < level_count[None], thickness[:, None, None] * component, 0.0), axis=0)


def horizontal(fields, counts, neighbour_set):
    level_axis = jnp.arange(fields.shape[-3], dtype=jnp.float32)[:, None, None]
    change = jnp.zeros_like(fields)
    for face_count, neighbour in zip(counts, neighbour_set):
        change = change + jnp.where(level_axis < face_count[None], neighbour - fields, 0.0)
    return fields + HORIZONTAL_RATE * change


def couplings(coefficient, level_count, thickness):
    spacing = 2.0 / (thickness[:-1] + thickness[1:])
    interface = jnp.arange(thickness.shape[0] - 1, dtype=jnp.float32)[:, None, None]
    return jnp.where(interface + 1.0 < level_count[None], coefficient * spacing[:, None, None], 0.0)


def vertical(fields, couple, thickness):
    levels = fields.shape[1]
    zero_plane = jnp.zeros_like(couple[0])
    gain_list = []
    eliminated = []
    prev_gain = zero_plane
    prev_value = jnp.zeros_like(fields[:, 0])
    for depth_index in range(levels):
        coupling_above = couple[depth_index - 1] if depth_index > 0 else zero_plane
        coupling_below = couple[depth_index] if depth_index < levels - 1 else zero_plane
        inverse = 1.0 / (thickness[depth_index] + coupling_above + coupling_below - coupling_above * prev_gain)
        prev_gain = coupling_below * inverse
        prev_value = (thickness[depth_index] * fields[:, depth_index] + coupling_above * prev_value) * inverse
        gain_list.append(prev_gain)
        eliminated.append(prev_value)
    result = [None] * levels
    lower_value = eliminated[-1]
    result[-1] = lower_value
    for depth_index in range(levels - 2, -1, -1):
        lower_value = eliminated[depth_index] + gain_list[depth_index] * lower_value
        result[depth_index] = lower_value
    return jnp.stack(result, axis=1)


def reference(ocean_state, viscosity, diffusivity, wet_levels, storage, surface_old):
    thickness = thickness_of(ocean_state.shape[1])
    level_count = wet_levels.astype(jnp.float32)
    counts = face_counts(level_count, neighbours(level_count, 1.0))
    viscous = couplings(viscosity, level_count, thickness)
    diffusive = couplings(diffusivity, level_count, thickness)
    mixed_list = []
    for field_index in range(ocean_state.shape[0]):
        values = ocean_state[field_index]
        flip = -1.0 if field_index < 2 else 1.0
        blended = horizontal(values, counts, neighbours(values, flip))
        couple = viscous if field_index < 2 else diffusive
        mixed_list.append(vertical(blended[None], couple, thickness)[0])
    mixed_state = jnp.stack(mixed_list, axis=0)
    zonal_flux = depth_sum(mixed_state[0], counts[0], thickness)
    meridional_flux = depth_sum(mixed_state[1], counts[2], thickness)
    meridional_flux = meridional_flux.at[-1].set(0.0)
    zero_row = jnp.zeros_like(meridional_flux[:1])
    divergence = zonal_flux - jnp.roll(zonal_flux, 1, axis=-1) + meridional_flux - jnp.concatenate([zero_row, meridional_flux[:-1]], axis=0)
    ocean_mask = wet_levels > 0
    forcing = jnp.where(ocean_mask, storage * surface_old - FLUX_SCALE * divergence, 0.0)
    face_terms = tuple(FACE_SCALE * column_depth(face_count, thickness) for face_count in counts)
    diagonal = storage + face_terms[0] + face_terms[1] + face_terms[2] + face_terms[3]

    def operate(values):
        result = storage * values
        for face_term, neighbour in zip(face_terms, neighbours(values, 1.0)):
            result = result + face_term * (values - neighbour)
        return result

    surface = jnp.where(ocean_mask, surface_old, 0.0)
    residual = forcing - operate(surface)
    scaled = residual / diagonal
    direction = scaled
    product = jnp.sum(residual * scaled)
    for iteration in range(ITERS):
        image_field = operate(direction)
        step_size = product / jnp.sum(direction * image_field)
        surface = surface + step_size * direction
        residual = residual - step_size * image_field
        if iteration + 1 < ITERS:
            scaled = residual / diagonal
            next_product = jnp.sum(residual * scaled)
            direction = scaled + (next_product / product) * direction
            product = next_product
    return mixed_state, surface
```

```python
import functools

import jax
import jax.numpy as jnp
import numpy as np
from jax import lax
from jax.experimental import pallas as pl
from jax.experimental.pallas import tpu as pltpu
from jax.sharding import PartitionSpec as P

ITERS = 3
K = 48
HORIZONTAL_RATE = 0.2
FLUX_SCALE = 0.02
FACE_SCALE = 0.25
F32 = jnp.float32

PAIR_UV = 0
PAIR_VISC = 48
PAIR_SURF = 72
ROW_X = 73
ROW_SCAL = 79
LAT_TILES = 115
PL_U, PL_V, PL_VISC, PL_WET, PL_STO, PL_SUR = 0, 48, 96, 143, 144, 145
PLANES = 146
LON_WIDE = 10
LON_TILES = LON_WIDE + 3


def sub_iota():
    return lax.broadcasted_iota(jnp.int32, (8, 128), 0)


def lane_iota():
    return lax.broadcasted_iota(jnp.int32, (8, 128), 1)


def lroll(x, shift):
    return pltpu.roll(x, shift, 1)


def sroll(x, shift):
    return pltpu.roll(x, shift, 0)


def flip_lanes(x):
    return jnp.take_along_axis(x, 127 - lane_iota(), axis=1)


def flip_rows(x):
    sub = sub_iota()
    x = sroll(x, 4)
    x = jnp.where((sub & 2) == 0, sroll(x, 6), sroll(x, 2))
    return jnp.where((sub & 1) == 0, sroll(x, 7), sroll(x, 1))


def thickness_at(level):
    return 0.5 + level / 48.0


def spacing_at(level):
    return 2.0 / (thickness_at(level) + thickness_at(level + 1.0))


def depth_of(count):
    return 0.5 * count + count * (count - 1.0) * (1.0 / 96.0)


def pack_lat(flags, state, visc, wet, storage, surf, pay_a, pay_b):
    odd = flags[0]
    sub = sub_iota()
    keep = (sub < 4).astype(jnp.int32) == odd

    def pair(tile, first, second):
        rolled = sroll(second, 4)
        pay_a[tile] = jnp.where(keep, first, rolled)
        pay_b[tile] = jnp.where(keep, rolled, first)

    wet_now = wet[...].astype(F32)

    @pl.loop(0, 48, unroll=8)
    def _(k):
        pair(k, state[pl.ds(k * 8, 8), :], state[pl.ds((k + 48) * 8, 8), :])

    @pl.loop(0, 23)
    def _(m):
        pair(PAIR_VISC + m, visc[2 * m], visc[2 * m + 1])

    pair(PAIR_VISC + 23, visc[46], wet_now)
    pair(PAIR_SURF, storage[...], surf[...])
    least = jnp.broadcast_to(jnp.minimum(wet_now[3:4], wet_now[4:5]), (8, 128))
    for m in range(6):
        start = (48 + 8 * m) * 8
        row3 = state[pl.ds(start + 3, 8, stride=8), :]
        row4 = state[pl.ds(start + 4, 8, stride=8), :]
        level = (sub + 8 * m).astype(F32)
        diff = jnp.where(level < least, row3 - row4, 0.0)
        pay_a[ROW_X + m] = diff
        pay_b[ROW_X + m] = diff
    for t in range(36):
        start = (96 + 8 * t) * 8
        row0 = state[pl.ds(start, 8, stride=8), :]
        row7 = state[pl.ds(start + 7, 8, stride=8), :]
        pay_a[ROW_SCAL + t] = jnp.where(odd == 1, row0, row7)
        pay_b[ROW_SCAL + t] = jnp.where(odd == 1, row7, row0)

    @pl.when(flags[1] == 1)
    def _():
        @pl.loop(0, 48, unroll=4)
        def _(t):
            pay_b[t] = -flip_rows(flip_lanes(pay_b[t]))

        @pl.loop(48, 73)
        def _(t):
            pay_b[t] = flip_rows(flip_lanes(pay_b[t]))

        @pl.loop(73, 79)
        def _(t):
            pay_b[t] = -flip_lanes(pay_b[t])

        @pl.loop(79, 115)
        def _(t):
            pay_b[t] = flip_lanes(pay_b[t])


def pack_lon(flags, state, visc, wet, storage, surf, rec_a, rec_b, rows, row_x, far, near):
    odd = flags[0]
    odd_lon = flags[2]
    sub = sub_iota()
    lane = lane_iota()
    keep = (sub < 4).astype(jnp.int32) != odd

    def unpair(tile):
        a, b = rec_a[tile], rec_b[tile]
        return jnp.where(keep, a, b), sroll(jnp.where(keep, b, a), 4)

    @pl.loop(0, 48, unroll=8)
    def _(k):
        first, second = unpair(k)
        rows[PL_U + k] = first
        rows[PL_V + k] = second

    @pl.loop(0, 24, unroll=4)
    def _(m):
        first, second = unpair(PAIR_VISC + m)
        rows[PL_VISC + 2 * m] = first
        rows[PL_VISC + 2 * m + 1] = second

    first, second = unpair(PAIR_SURF)
    rows[PL_STO] = first
    rows[PL_SUR] = second
    for m in range(6):
        row_x[m] = jnp.where(odd == 1, rec_b[ROW_X + m], rec_a[ROW_X + m])

    wet_now = wet[...].astype(F32)

    def plane(n):
        if n < 96:
            return state[n * 8 : n * 8 + 8, :]
        if n < 143:
            return visc[n - 96]
        if n == 143:
            return wet_now
        if n == 144:
            return storage[...]
        if n == 145:
            return surf[...]
        if n < 292:
            return rows[n - 146]
        return row_x[n - 292]

    def emit(tile, planes, width):
        east = jnp.zeros((8, 128), F32)
        west = jnp.zeros((8, 128), F32)
        slots = 128 // width
        slot_of = lane // width
        for j, load in enumerate(planes):
            x = load()
            x = lroll(x, j * width) if j else x
            west = jnp.where(slot_of == j, x, west)
            east = jnp.where(slot_of == (j - 1) % slots, x, east)
        far[tile] = jnp.where(odd_lon == 1, east, west)
        near[tile] = jnp.where(odd_lon == 1, west, east)

    for tile in range(LON_WIDE):
        emit(tile, [functools.partial(plane, n) for n in range(32 * tile, min(32 * tile + 32, 298))], 4)

    def scalar(n):
        return state[(96 + n) * 8 : (96 + n) * 8 + 8, :]

    for tile in range(3):
        emit(LON_WIDE + tile, [functools.partial(scalar, n) for n in range(128 * tile, min(128 * tile + 128, 288))], 1)


def momentum(
    flags, state, visc, wet, storage, surf, rows, row_x, far, near,
    mixed, zed, moments,
    field, couple, gain, done, planes2, xs,
):
    odd_lon = flags[2]
    top = flags[1] == 1
    lane = lane_iota()
    sub = sub_iota()
    slot_of = lane // 4
    valid = jnp.logical_or(lane < 4, lane >= 124)

    def strip(n):
        tile, j = n // 32, n % 32
        a, b = far[tile], near[tile]
        mine = (slot_of == j).astype(jnp.int32) == odd_lon
        return lroll(jnp.where(mine, a, b), (128 - 4 * j) % 128)

    @pl.loop(0, 96, unroll=8)
    def _(n):
        field[n, 0] = state[pl.ds(n * 8, 8), :]
        field[n, 1] = rows[n]
        field[n, 2] = strip(n)
        field[n, 3] = strip(n + 146)

    @pl.loop(0, 6)
    def _(m):
        xs[m] = strip(m + 292)

    def four(n, own, mask):
        out = [own, rows[n], strip(n), strip(n + 146)]
        if mask:
            out[2] = jnp.where(valid, out[2], 0.0)
            out[3] = jnp.where(valid, out[3], 0.0)
        return out

    def east(q):
        return [
            lroll(jnp.where(lane == 0, q[2], q[0]), 127),
            lroll(jnp.where(lane == 0, q[3], q[1]), 127),
            lroll(jnp.where(lane == 0, q[0], q[2]), 127),
            lroll(jnp.where(lane == 0, q[1], q[3]), 127),
        ]

    def west(q):
        return [
            lroll(jnp.where(lane == 127, q[2], q[0]), 1),
            lroll(jnp.where(lane == 127, q[3], q[1]), 1),
            lroll(jnp.where(lane == 127, q[0], q[2]), 1),
            lroll(jnp.where(lane == 127, q[1], q[3]), 1),
        ]

    def north(q):
        return [
            sroll(jnp.where(sub == 0, q[1], q[0]), 7),
            sroll(jnp.where(sub == 0, q[0], q[1]), 7),
            sroll(jnp.where(sub == 0, q[3], q[2]), 7),
            sroll(jnp.where(sub == 0, q[2], q[3]), 7),
        ]

    def south(q):
        return [
            sroll(jnp.where(sub == 7, q[1], q[0]), 1),
            sroll(jnp.where(sub == 7, q[0], q[1]), 1),
            sroll(jnp.where(sub == 7, q[3], q[2]), 1),
            sroll(jnp.where(sub == 7, q[2], q[3]), 1),
        ]

    def each(fn, *lists):
        return [fn(*items) for items in zip(*lists)]

    level_count = four(PL_WET, wet[...].astype(F32), True)
    counts = [each(jnp.minimum, level_count, shift(level_count)) for shift in (east, west, north, south)]
    for i, c in enumerate(counts):
        for j in range(4):
            planes2[4 * i + j] = c[j]
    for j in range(4):
        planes2[16 + j] = level_count[j]
    ghost = jnp.logical_and(top, sub < 4)
    planes2[20] = counts[0][0]
    planes2[21] = jnp.where(ghost, counts[1][1], counts[0][1])
    planes2[22] = counts[0][2]
    planes2[23] = jnp.where(ghost, counts[1][3], counts[0][3])
    planes2[24] = counts[2][0]
    planes2[25] = jnp.where(ghost, counts[3][1], counts[2][1])
    planes2[26] = counts[2][2]
    planes2[27] = jnp.where(ghost, counts[3][3], counts[2][3])

    def blend(base, k, kf):
        q = [field[base + k, j] for j in range(4)]
        faces = [east(q), west(q), north(q), south(q)]
        change = []
        for j in range(4):
            total = None
            for i in range(4):
                term = jnp.where(kf < planes2[4 * i + j], faces[i][j] - q[j], 0.0)
                if base == PL_V and i == 2 and j in (1, 3):
                    source = row_x if j == 1 else xs
                    extra = jnp.broadcast_to(source[k // 8, pl.ds(k % 8, 1), :], (8, 128))
                    term = jnp.where(jnp.logical_and(top, sub == 3), extra, term)
                total = term if total is None else total + term
            change.append(q[j] + HORIZONTAL_RATE * total)
        return change

    zero = jnp.zeros((8, 128), F32)

    @pl.loop(0, 47, unroll=8)
    def _(k):
        couple[k, 0] = visc[k]
        couple[k, 1] = rows[PL_VISC + k]
        couple[k, 2] = strip(PL_VISC + k)
        couple[k, 3] = strip(PL_VISC + k + 146)

    for j in range(4):
        couple[47, j] = zero

    def forward(k, carry):
        above, prev_gain, prev_u, prev_v = carry
        kf = k.astype(F32)
        thick = thickness_at(kf)
        space = spacing_at(kf)
        below = [jnp.where(kf + 1.0 < planes2[16 + j], couple[k, j] * space, 0.0) for j in range(4)]
        u = blend(PL_U, k, kf)
        v = blend(PL_V, k, kf)
        new_gain, new_u, new_v = [], [], []
        for j in range(4):
            inverse = 1.0 / (thick + above[j] + below[j] - above[j] * prev_gain[j])
            new_gain.append(below[j] * inverse)
            new_u.append((thick * u[j] + above[j] * prev_u[j]) * inverse)
            new_v.append((thick * v[j] + above[j] * prev_v[j]) * inverse)
            gain[k, j] = new_gain[j]
            done[k, j] = new_u[j]
            done[k + 48, j] = new_v[j]
        return below, new_gain, new_u, new_v

    zeros = [zero] * 4
    lax.fori_loop(0, 48, forward, (zeros, zeros, zeros, zeros), unroll=2)

    def backward(i, carry):
        k = 47 - i
        kf = k.astype(F32)
        thick = thickness_at(kf)
        low_u, low_v, flux_u, flux_v = carry
        new_u, new_v, out_u, out_v = [], [], [], []
        for j in range(4):
            g = gain[k, j]
            x_u = done[k, j] + g * low_u[j]
            x_v = done[k + 48, j] + g * low_v[j]
            new_u.append(x_u)
            new_v.append(x_v)
            out_u.append(flux_u[j] + jnp.where(kf < planes2[20 + j], thick * x_u, 0.0))
            out_v.append(flux_v[j] + jnp.where(kf < planes2[24 + j], thick * x_v, 0.0))
        mixed[pl.ds(k * 8, 8), :] = new_u[0]
        mixed[pl.ds((k + 48) * 8, 8), :] = new_v[0]
        return new_u, new_v, out_u, out_v

    _, _, flux_u, flux_v = lax.fori_loop(0, 48, backward, (zeros, zeros, zeros, zeros), unroll=4)

    last = jnp.logical_and(top, sub == 7)
    first_ghost = jnp.logical_and(top, sub == 0)
    flux_v = [
        jnp.where(last, 0.0, flux_v[0]),
        jnp.where(first_ghost, 0.0, flux_v[1]),
        jnp.where(last, 0.0, flux_v[2]),
        jnp.where(first_ghost, 0.0, flux_v[3]),
    ]
    plain = each(
        lambda a, b, c, d: a - b + c - d, flux_u, west(flux_u), flux_v, south(flux_v)
    )
    mirrored = each(
        lambda a, b, c, d: a - b + c - d, east(flux_u), flux_u, north(flux_v), flux_v
    )
    divergence = [
        plain[0],
        jnp.where(ghost, mirrored[1], plain[1]),
        plain[2],
        jnp.where(ghost, mirrored[3], plain[3]),
    ]
    sto = four(PL_STO, storage[...], True)
    old = four(PL_SUR, surf[...], True)
    faces = [[FACE_SCALE * depth_of(planes2[4 * i + j]) for j in range(4)] for i in range(4)]
    diagonal = [
        jnp.maximum(sto[j] + faces[0][j] + faces[1][j] + faces[2][j] + faces[3][j], 0.1) for j in range(4)
    ]
    ocean = [planes2[16 + j] > 0.0 for j in range(4)]
    start = [jnp.where(ocean[j], old[j], 0.0) for j in range(4)]
    around = [east(start), west(start), north(start), south(start)]
    inverse = [1.0 / diagonal[j] for j in range(4)]
    basis = []
    for j in range(4):
        forcing = jnp.where(ocean[j], sto[j] * old[j] - FLUX_SCALE * divergence[j], 0.0)
        image = sto[j] * start[j]
        for i in range(4):
            image = image + faces[i][j] * (start[j] - around[i][j])
        basis.append((forcing - image) / diagonal[j])
    z0 = basis

    def spread(z):
        nb = [east(z), west(z), north(z), south(z)]
        return [
            (faces[0][j] * nb[0][j] + faces[1][j] * nb[1][j] + faces[2][j] * nb[2][j] + faces[3][j] * nb[3][j])
            * inverse[j]
            for j in range(4)
        ]

    z1 = spread(z0)
    z2 = spread(z1)
    zed[0] = start[0]
    zed[1] = z0[0]
    zed[2] = z1[0]
    zed[3] = z2[0]
    weighted = [diagonal[0] * z[0] for z in (z0, z1, z2)]
    north_weight = jnp.where(last, 1.0, 2.0)
    edge = z2[0] * (
        2.0 * faces[0][0] * east(z2)[0] + north_weight * faces[2][0] * north(z2)[0]
    )
    products = [
        weighted[0] * z0[0],
        weighted[0] * z1[0],
        weighted[1] * z1[0],
        weighted[1] * z2[0],
        weighted[2] * z2[0],
        edge,
    ]
    tile = zero
    for i, product in enumerate(products):
        total = jnp.sum(jnp.sum(product, axis=0, keepdims=True), axis=1, keepdims=True)
        tile = jnp.where(sub == i, total, tile)
    for i in range(moments.shape[0]):
        moments[i] = tile


def tracers(flags, state, diff, wet, around, rec_a, rec_b, far, near, mixed_in, out, gain, done):
    out[0 : 96 * 8, :] = mixed_in[...]
    odd = flags[0]
    odd_lon = flags[2]
    lane = lane_iota()
    sub = sub_iota()
    level_count = wet[...].astype(F32)
    counts = [around[i] for i in range(4)]
    zero = jnp.zeros((8, 128), F32)

    def forward(k, carry):
        above, prev_gain, prev = carry
        kf = k.astype(F32)
        thick = thickness_at(kf)
        coefficient = diff[jnp.minimum(k, 46)]
        below = jnp.where(kf + 1.0 < level_count, coefficient * spacing_at(kf), 0.0)
        inverse = 1.0 / (thick + above + below - above * prev_gain)
        new_gain = below * inverse
        gain[k] = new_gain
        open_face = [kf < c for c in counts]
        new = []
        for f in range(6):
            n = f * 48 + k
            q = state[pl.ds((96 + n) * 8, 8), :]
            row_a = rec_a[n // 8, pl.ds(n % 8, 1), :]
            row_b = rec_b[n // 8, pl.ds(n % 8, 1), :]
            row_n = jnp.broadcast_to(jnp.where(odd == 1, row_b, row_a), (8, 128))
            row_s = jnp.broadcast_to(jnp.where(odd == 1, row_a, row_b), (8, 128))
            j = n % 128
            a, b = far[LON_WIDE + n // 128], near[LON_WIDE + n // 128]
            side = lroll(jnp.where((lane == j).astype(jnp.int32) == odd_lon, a, b), (128 - j) % 128)
            nbs = (
                lroll(jnp.where(lane == 0, side, q), 127),
                lroll(jnp.where(lane == 127, side, q), 1),
                sroll(jnp.where(sub == 0, row_n, q), 7),
                sroll(jnp.where(sub == 7, row_s, q), 1),
            )
            change = zero
            for i in range(4):
                change = change + jnp.where(open_face[i], nbs[i] - q, 0.0)
            value = (thick * (q + HORIZONTAL_RATE * change) + above * prev[f]) * inverse
            done[n] = value
            new.append(value)
        return below, new_gain, new

    lax.fori_loop(0, 48, forward, (zero, zero, [zero] * 6), unroll=2)

    def backward(i, low):
        k = 47 - i
        g = gain[k]
        new = []
        for f in range(6):
            n = f * 48 + k
            value = done[n] + g * low[f]
            out[pl.ds((96 + n) * 8, 8), :] = value
            new.append(value)
        return new

    lax.fori_loop(0, 48, backward, [zero] * 6, unroll=4)


def finish(parts, zed, surface):
    total = parts[0]
    for i in range(1, parts.shape[0]):
        total = total + parts[i]
    nu = [jnp.broadcast_to(total[i : i + 1, :], (8, 128)) for i in range(6)]

    def inner(p, q, shift):
        out = None
        for i, a in enumerate(p):
            for j, b in enumerate(q):
                term = a * b * nu[i + j + shift]
                out = term if out is None else out + term
        return out

    one = jnp.ones((8, 128), F32)
    scaled = [one]
    direction = [one]
    product = nu[0]
    move = [jnp.zeros((8, 128), F32)] * 3
    for iteration in range(ITERS):
        curvature = inner(direction, direction, 0) - inner(direction, direction, 1)
        alpha = product / curvature
        for i, d in enumerate(direction):
            move[i] = move[i] + alpha * d
        if iteration + 1 < ITERS:
            longer = scaled + [jnp.zeros((8, 128), F32)]
            for i, d in enumerate(direction):
                longer[i] = longer[i] - alpha * d
                longer[i + 1] = longer[i + 1] + alpha * d
            scaled = longer
            following = inner(scaled, scaled, 0)
            beta = following / product
            direction = [
                scaled[i] + (beta * direction[i] if i < len(direction) else 0.0) for i in range(len(scaled))
            ]
            product = following
    surface[...] = zed[0] + move[0] * zed[1] + move[1] * zed[2] + move[2] * zed[3]


VMEM_LIMIT = 48 * 1024 * 1024


def kernel(body, outs, scratch=(), smem=1, operands=0, flops=0, nbytes=0):
    vmem = pl.BlockSpec(memory_space=pltpu.VMEM)
    return pl.pallas_call(
        body,
        out_shape=[jax.ShapeDtypeStruct(s, F32) for s in outs],
        in_specs=[pl.BlockSpec(memory_space=pltpu.SMEM)] * smem + [vmem] * operands,
        out_specs=[vmem] * len(outs),
        scratch_shapes=[pltpu.VMEM(s, F32) for s in scratch],
        compiler_params=pltpu.CompilerParams(vmem_limit_bytes=VMEM_LIMIT),
        cost_estimate=pl.CostEstimate(flops=flops, bytes_accessed=nbytes, transcendentals=0),
    )


def lat_pairs(lat, lon):
    first, second = [], []
    for l in range(lat):
        for p in range(lon):
            here = l * lon + p
            first.append((here, (l ^ 1) * lon + p))
            if l == lat - 1:
                second.append((here, l * lon + lon - 1 - p))
            elif l % 2 == 1:
                second.append((here, here + lon))
            elif l > 0:
                second.append((here, here - lon))
    return first, second


def lon_pairs(lon):
    far, near = [], []
    for p in range(lon):
        step = 1 if p % 2 else -1
        far.append((p, (p + step) % lon))
        near.append((p, p ^ 1))
    return far, near


def make_local(mesh_shape):
    lat, lon = mesh_shape["lat"], mesh_shape["lon"]
    pairs_a, pairs_b = lat_pairs(lat, lon)
    pairs_far, pairs_near = lon_pairs(lon)
    both = ("lat", "lon")
    stages = reduction_stages(lat, lon)

    def local(ocean_state, viscosity, diffusivity, wet_levels, storage, surface_old):
        band = lax.axis_index("lat")
        place = lax.axis_index("lon")
        flags = jnp.stack([band % 2, (band == lat - 1).astype(jnp.int32), place % 2]).astype(jnp.int32)
        state = ocean_state.reshape(8 * K * 8, 128)
        fixed = (viscosity, wet_levels, storage, surface_old)
        pay_a, pay_b = kernel(pack_lat, [(LAT_TILES, 8, 128)] * 2, operands=5)(flags, state, *fixed)
        rec_b = lax.ppermute(pay_b, both, pairs_b)
        rec_a = lax.ppermute(pay_a, both, pairs_a)
        rows, row_x, pay_far, pay_near = kernel(
            pack_lon,
            [(PLANES, 8, 128), (6, 8, 128), (LON_TILES, 8, 128), (LON_TILES, 8, 128)],
            operands=7,
        )(flags, state, *fixed, rec_a, rec_b)
        rec_far = lax.ppermute(pay_far, "lon", pairs_far)
        rec_near = lax.ppermute(pay_near, "lon", pairs_near)
        mixed, zed, around, moments = kernel(
            momentum_entry,
            [(2 * K * 8, 128), (4, 8, 128), (4, 8, 128), (stages[0][1], 8, 128)],
            scratch=[(96, 4, 8, 128), (48, 4, 8, 128), (48, 4, 8, 128), (96, 4, 8, 128), (28, 8, 128), (6, 8, 128)],
            operands=9,
        )(flags, state, *fixed, rows, row_x, rec_far, rec_near)
        parts = moments
        for i, (groups, size, following) in enumerate(stages):
            if i:
                parts = jnp.broadcast_to(jnp.sum(parts, axis=0)[None], (size, 8, 128))
            parts = lax.all_to_all(parts, both, 0, 0, axis_index_groups=groups, tiled=True)
        (mixed,) = kernel(
            tracers,
            [(8 * K * 8, 128)],
            scratch=[(48, 8, 128), (288, 8, 128)],
            operands=9,
            flops=20_000_000,
            nbytes=6_000_000,
        )(
            flags, state, diffusivity, wet_levels, around,
            rec_a[ROW_SCAL:], rec_b[ROW_SCAL:], rec_far, rec_near, mixed,
        )
        (surface,) = kernel(finish, [(8, 128)], smem=0, operands=2)(parts, zed)
        return mixed.reshape(8, K, 8, 128), surface

    return local


def momentum_entry(*refs):
    inputs, outputs, scratch = refs[:10], refs[10:14], refs[14:]
    mixed, zed, around, moments = outputs
    momentum(*inputs, mixed, zed, moments, *scratch)
    planes2 = scratch[4]
    for i in range(4):
        around[i] = planes2[4 * i]


def reduction_stages(lat, lon):
    index = np.arange(lat * lon)
    if lat == 32 and lon == 16:
        grid = index.reshape(8, 4, 4, 2, 2)
        along_z = grid.transpose(1, 2, 4, 3, 0).reshape(32, 16)
        rest = grid.transpose(0, 3, 1, 2, 4).reshape(16, 32)
    else:
        grid = index.reshape(lat, lon)
        along_z, rest = grid.T, grid
    return [(g.tolist(), g.shape[1], None) for g in (along_z, rest)]


def solution(mesh):
    placed = (
        P(None, None, "lat", "lon"),
        P(None, "lat", "lon"),
        P(None, "lat", "lon"),
        P("lat", "lon"),
        P("lat", "lon"),
        P("lat", "lon"),
    )
    return jax.shard_map(
        make_local(dict(mesh.shape)),
        mesh=mesh,
        in_specs=placed,
        out_specs=(P(None, None, "lat", "lon"), P("lat", "lon")),
        check_vma=False,
    )
```

```python
import functools

import jax
import jax.numpy as jnp
import numpy as np
from jax import lax
from jax.experimental import pallas as pl
from jax.experimental.pallas import tpu as pltpu
from jax.sharding import PartitionSpec as P

ITERS = 3
K = 48
HORIZONTAL_RATE = 0.2
FLUX_SCALE = 0.02
FACE_SCALE = 0.25
F32 = jnp.float32

PAIR_UV = 0
PAIR_VISC = 48
PAIR_SURF = 72
ROW_X = 73
LAT_TILES = 79
ROW_TILES = 36
PL_U, PL_V, PL_VISC, PL_WET, PL_STO, PL_SUR = 0, 48, 96, 143, 144, 145
PLANES = 146
LON_WIDE = 10
LON_TILES = LON_WIDE + 3
CHUNK = 8


def sub_iota():
    return lax.broadcasted_iota(jnp.int32, (8, 128), 0)


def lane_iota():
    return lax.broadcasted_iota(jnp.int32, (8, 128), 1)


def lroll(x, shift):
    return pltpu.roll(x, shift, 1)


def sroll(x, shift):
    return pltpu.roll(x, shift, 0)


def flip_lanes(x):
    return jnp.take_along_axis(x, 127 - lane_iota(), axis=1)


def flip_rows(x):
    sub = sub_iota()
    x = sroll(x, 4)
    x = jnp.where((sub & 2) == 0, sroll(x, 6), sroll(x, 2))
    return jnp.where((sub & 1) == 0, sroll(x, 7), sroll(x, 1))


def thickness_at(level):
    return 0.5 + level * (1.0 / 48.0)


def spacing_at(level):
    return 96.0 / jnp.full((8, 128), 49.0 + 2.0 * level, F32)


def depth_of(count):
    return 0.5 * count + count * (count - 1.0) * (1.0 / 96.0)


def pack_lat(
    flags, state_any, visc_any, wet_any, storage_any, surf_any, pay_b, pay_a, state, visc, flat, wet, sems,
):
    half = 48 * 8
    copies = [
        pltpu.make_async_copy(state_any.at[pl.ds(0, half)], state.at[pl.ds(0, half)], sems.at[0]),
        pltpu.make_async_copy(state_any.at[pl.ds(half, half)], state.at[pl.ds(half, half)], sems.at[1]),
        pltpu.make_async_copy(visc_any, visc, sems.at[2]),
        pltpu.make_async_copy(wet_any, wet, sems.at[3]),
        pltpu.make_async_copy(storage_any, flat.at[1], sems.at[4]),
        pltpu.make_async_copy(surf_any, flat.at[2], sems.at[5]),
    ]
    for copy in copies:
        copy.start()
    for copy in copies:
        copy.wait()
    flat[0] = wet[...].astype(F32)
    odd = flags[0]
    sub = sub_iota()
    keep = (sub < 4).astype(jnp.int32) == odd
    wet_now = flat[0]
    least = jnp.broadcast_to(jnp.minimum(wet_now[3:4], wet_now[4:5]), (8, 128))

    def pairs():
        for k in range(48):
            yield k, state[k * 8 : k * 8 + 8, :], state[(k + 48) * 8 : (k + 48) * 8 + 8, :], -1.0
        for m in range(23):
            yield PAIR_VISC + m, visc[2 * m], visc[2 * m + 1], 1.0
        yield PAIR_VISC + 23, visc[46], wet_now, 1.0
        yield PAIR_SURF, flat[1], flat[2], 1.0

    def crossed():
        for m in range(6):
            start = (48 + 8 * m) * 8
            row3 = state[pl.ds(start + 3, 8, stride=8), :]
            row4 = state[pl.ds(start + 4, 8, stride=8), :]
            level = (sub + 8 * m).astype(F32)
            yield ROW_X + m, jnp.where(level < least, row3 - row4, 0.0)

    @pl.when(flags[1] == 0)
    def _():
        for tile, first, second, _ in pairs():
            rolled = sroll(second, 4)
            pay_a[tile] = jnp.where(keep, first, rolled)
            pay_b[tile] = jnp.where(keep, rolled, first)
        for tile, diff in crossed():
            pay_a[tile] = diff
            pay_b[tile] = diff

    @pl.when(flags[1] == 1)
    def _():
        for tile, first, second, sign in pairs():
            rolled = sroll(second, 4)
            pay_a[tile] = jnp.where(keep, first, rolled)
            turned = flip_rows(flip_lanes(jnp.where(keep, rolled, first)))
            pay_b[tile] = -turned if sign < 0 else turned
        for tile, diff in crossed():
            pay_a[tile] = diff
            pay_b[tile] = -flip_lanes(diff)


def pack_tracers(flags, state_any, pay_b, pay_a, far, near, tracer, sems):
    half = 144 * 8
    copies = [
        pltpu.make_async_copy(
            state_any.at[pl.ds((96 + 144 * i) * 8, half)], tracer.at[pl.ds(i * half, half)], sems.at[i]
        )
        for i in range(2)
    ]
    for copy in copies:
        copy.start()
    for copy in copies:
        copy.wait()
    odd = flags[0]
    odd_lon = flags[2]
    lane = lane_iota()

    def rows_of(t):
        start = 8 * t * 8
        return tracer[pl.ds(start, 8, stride=8), :], tracer[pl.ds(start + 7, 8, stride=8), :]

    for t in range(ROW_TILES):
        row0, row7 = rows_of(t)
        pay_a[t] = jnp.where(odd == 1, row0, row7)
        pay_b[t] = jnp.where(odd == 1, row7, row0)

    @pl.when(flags[1] == 1)
    def _():
        for t in range(ROW_TILES):
            pay_b[t] = flip_lanes(rows_of(t)[1])

    def scalar(n):
        return tracer[n * 8 : n * 8 + 8, :]

    for tile in range(3):
        planes = [functools.partial(scalar, n) for n in range(128 * tile, min(128 * tile + 128, 288))]
        east, west = pack_columns(lane, planes, 1)
        far[tile] = jnp.where(odd_lon == 1, east, west)
        near[tile] = jnp.where(odd_lon == 1, west, east)


def pack_columns(lane, planes, width):
    east = jnp.zeros((8, 128), F32)
    west = jnp.zeros((8, 128), F32)
    slots = 128 // width
    slot_of = lane // width
    for j, load in enumerate(planes):
        x = load()
        x = lroll(x, j * width) if j else x
        west = jnp.where(slot_of == j, x, west)
        east = jnp.where(slot_of == (j - 1) % slots, x, east)
    return east, west


def lon_planes(state, visc, flat, rows, row_x):
    def plane(n):
        if n < 96:
            return state[n * 8 : n * 8 + 8, :]
        if n < 143:
            return visc[n - 96]
        if n < 146:
            return flat[n - 143]
        if n < 292:
            return rows[n - 146]
        return row_x[n - 292]

    lane = lane_iota()
    for tile in range(LON_WIDE):
        planes = [functools.partial(plane, n) for n in range(32 * tile, min(32 * tile + 32, 298))]
        yield tile, pack_columns(lane, planes, 4)


def pack_lon(
    flags, state, visc, flat, rec_b, rec_a, far_tracers, near_tracers, rows, row_x, far, near
):
    odd = flags[0]
    odd_lon = flags[2]
    sub = sub_iota()
    keep = (sub < 4).astype(jnp.int32) != odd

    def unpair(tile):
        a, b = rec_a[tile], rec_b[tile]
        return jnp.where(keep, a, b), sroll(jnp.where(keep, b, a), 4)

    for k in range(48):
        first, second = unpair(k)
        rows[PL_U + k] = first
        rows[PL_V + k] = second
    for m in range(24):
        first, second = unpair(PAIR_VISC + m)
        rows[PL_VISC + 2 * m] = first
        rows[PL_VISC + 2 * m + 1] = second
    first, second = unpair(PAIR_SURF)
    rows[PL_STO] = first
    rows[PL_SUR] = second
    for m in range(6):
        row_x[m] = jnp.where(odd == 1, rec_b[ROW_X + m], rec_a[ROW_X + m])
    for tile, (east, west) in lon_planes(state, visc, flat, rows, row_x):
        far[tile] = jnp.where(odd_lon == 1, east, west)
        near[tile] = jnp.where(odd_lon == 1, west, east)
    for tile in range(3):
        far[LON_WIDE + tile] = far_tracers[tile]
        near[LON_WIDE + tile] = near_tracers[tile]


def momentum(
    flags, state, visc, flat, rows, row_x, far, near,
    mixed, zed, moments,
    gain, done, planes2, xs,
):
    odd_lon = flags[2]
    top = flags[1] == 1
    lane = lane_iota()
    sub = sub_iota()
    slot_of = lane // 4
    valid = jnp.logical_or(lane < 4, lane >= 124)

    def strip_at(tile, j):
        a, b = far[tile], near[tile]
        mine = (slot_of == j).astype(jnp.int32) == odd_lon
        return lroll(jnp.where(mine, a, b), (128 - 4 * j) % 128)

    def strip(n):
        return strip_at(n // 32, n % 32)

    def strip_in(chunk, first, i):
        n = first + CHUNK * chunk + i
        return strip_at(n // 32, n % 32)

    for m in range(6):
        xs[m] = strip(m + 292)

    def four(n, own, mask):
        out = [own, rows[n], strip(n), strip(n + 146)]
        if mask:
            out[2] = jnp.where(valid, out[2], 0.0)
            out[3] = jnp.where(valid, out[3], 0.0)
        return out

    def east(q):
        return [
            lroll(jnp.where(lane == 0, q[2], q[0]), 127),
            lroll(jnp.where(lane == 0, q[3], q[1]), 127),
            lroll(jnp.where(lane == 0, q[0], q[2]), 127),
            lroll(jnp.where(lane == 0, q[1], q[3]), 127),
        ]

    def west(q):
        return [
            lroll(jnp.where(lane == 127, q[2], q[0]), 1),
            lroll(jnp.where(lane == 127, q[3], q[1]), 1),
            lroll(jnp.where(lane == 127, q[0], q[2]), 1),
            lroll(jnp.where(lane == 127, q[1], q[3]), 1),
        ]

    def north(q):
        return [
            sroll(jnp.where(sub == 0, q[1], q[0]), 7),
            sroll(jnp.where(sub == 0, q[0], q[1]), 7),
            sroll(jnp.where(sub == 0, q[3], q[2]), 7),
            sroll(jnp.where(sub == 0, q[2], q[3]), 7),
        ]

    def south(q):
        return [
            sroll(jnp.where(sub == 7, q[1], q[0]), 1),
            sroll(jnp.where(sub == 7, q[0], q[1]), 1),
            sroll(jnp.where(sub == 7, q[3], q[2]), 1),
            sroll(jnp.where(sub == 7, q[2], q[3]), 1),
        ]

    def each(fn, *lists):
        return [fn(*items) for items in zip(*lists)]

    level_count = four(PL_WET, flat[0], True)
    counts = [each(jnp.minimum, level_count, shift(level_count)) for shift in (east, west, north, south)]
    for i, c in enumerate(counts):
        for j in range(4):
            planes2[4 * i + j] = c[j]
    for j in range(4):
        planes2[16 + j] = level_count[j]
    ghost = jnp.logical_and(top, sub < 4)
    planes2[20] = counts[0][0]
    planes2[21] = jnp.where(ghost, counts[1][1], counts[0][1])
    planes2[22] = counts[0][2]
    planes2[23] = jnp.where(ghost, counts[1][3], counts[0][3])
    planes2[24] = counts[2][0]
    planes2[25] = jnp.where(ghost, counts[3][1], counts[2][1])
    planes2[26] = counts[2][2]
    planes2[27] = jnp.where(ghost, counts[3][3], counts[2][3])

    zero = jnp.zeros((8, 128), F32)
    cross = jnp.logical_and(top, sub == 3)

    def blend(base, chunk, i, open_east, open_north):
        n = base + CHUNK * chunk + i
        q = [state[pl.ds(n * 8, 8), :], rows[n], strip_in(chunk, base, i), strip_in(chunk, base + 146, i)]
        over_east = each(lambda o, a, b: jnp.where(o, a - b, 0.0), open_east, east(q), q)
        over_north = each(lambda o, a, b: jnp.where(o, a - b, 0.0), open_north, north(q), q)
        if base == PL_V:
            for j, source in ((1, row_x), (3, xs)):
                extra = jnp.broadcast_to(source[chunk, i : i + 1, :], (8, 128))
                over_north[j] = jnp.where(cross, extra, over_north[j])
        return each(
            lambda c, a, b, d, e: c + HORIZONTAL_RATE * (a - b + d - e),
            q, over_east, west(over_east), over_north, south(over_north),
        )

    def forward(chunk, carry):
        above, prev_gain, prev_u, prev_v = carry
        for i in range(CHUNK):
            k = CHUNK * chunk + i
            kf = k.astype(F32)
            thick = thickness_at(kf)
            space = spacing_at(kf)
            coefficient = [
                visc[jnp.minimum(k, 46)],
                rows[PL_VISC + k],
                strip_in(chunk, PL_VISC, i),
                strip_in(chunk, PL_VISC + 146, i),
            ]
            below = [jnp.where(kf + 1.0 < planes2[16 + j], coefficient[j] * space, 0.0) for j in range(4)]
            open_east = [kf < planes2[j] for j in range(4)]
            open_north = [kf < planes2[8 + j] for j in range(4)]
            u = blend(PL_U, chunk, i, open_east, open_north)
            v = blend(PL_V, chunk, i, open_east, open_north)
            new_gain, new_u, new_v = [], [], []
            for j in range(4):
                inverse = 1.0 / (thick + above[j] + below[j] - above[j] * prev_gain[j])
                new_gain.append(below[j] * inverse)
                new_u.append((thick * u[j] + above[j] * prev_u[j]) * inverse)
                new_v.append((thick * v[j] + above[j] * prev_v[j]) * inverse)
                gain[chunk, i, j] = new_gain[j]
                done[0, chunk, i, j] = new_u[j]
                done[1, chunk, i, j] = new_v[j]
            above, prev_gain, prev_u, prev_v = below, new_gain, new_u, new_v
        return above, prev_gain, prev_u, prev_v

    zeros = [zero] * 4
    lax.fori_loop(0, K // CHUNK, forward, (zeros, zeros, zeros, zeros))

    def backward(step, carry):
        chunk = K // CHUNK - 1 - step
        low_u, low_v, flux_u, flux_v = carry
        for i in reversed(range(CHUNK)):
            k = CHUNK * chunk + i
            kf = k.astype(F32)
            thick = thickness_at(kf)
            new_u, new_v, out_u, out_v = [], [], [], []
            for j in range(4):
                g = gain[chunk, i, j]
                x_u = done[0, chunk, i, j] + g * low_u[j]
                x_v = done[1, chunk, i, j] + g * low_v[j]
                new_u.append(x_u)
                new_v.append(x_v)
                out_u.append(flux_u[j] + jnp.where(kf < planes2[20 + j], thick * x_u, 0.0))
                out_v.append(flux_v[j] + jnp.where(kf < planes2[24 + j], thick * x_v, 0.0))
            mixed[pl.ds(k * 8, 8), :] = new_u[0]
            mixed[pl.ds((k + 48) * 8, 8), :] = new_v[0]
            low_u, low_v, flux_u, flux_v = new_u, new_v, out_u, out_v
        return low_u, low_v, flux_u, flux_v

    _, _, flux_u, flux_v = lax.fori_loop(0, K // CHUNK, backward, (zeros, zeros, zeros, zeros))

    last = jnp.logical_and(top, sub == 7)
    first_ghost = jnp.logical_and(top, sub == 0)
    flux_v = [
        jnp.where(last, 0.0, flux_v[0]),
        jnp.where(first_ghost, 0.0, flux_v[1]),
        jnp.where(last, 0.0, flux_v[2]),
        jnp.where(first_ghost, 0.0, flux_v[3]),
    ]
    plain = each(
        lambda a, b, c, d: a - b + c - d, flux_u, west(flux_u), flux_v, south(flux_v)
    )
    mirrored = each(
        lambda a, b, c, d: a - b + c - d, east(flux_u), flux_u, north(flux_v), flux_v
    )
    divergence = [
        plain[0],
        jnp.where(ghost, mirrored[1], plain[1]),
        plain[2],
        jnp.where(ghost, mirrored[3], plain[3]),
    ]
    sto = four(PL_STO, flat[1], True)
    old = four(PL_SUR, flat[2], True)
    faces = [[FACE_SCALE * depth_of(planes2[4 * i + j]) for j in range(4)] for i in range(4)]
    diagonal = [
        jnp.maximum(sto[j] + faces[0][j] + faces[1][j] + faces[2][j] + faces[3][j], 0.1) for j in range(4)
    ]
    ocean = [planes2[16 + j] > 0.0 for j in range(4)]
    start = [jnp.where(ocean[j], old[j], 0.0) for j in range(4)]
    around = [east(start), west(start), north(start), south(start)]
    inverse = [1.0 / diagonal[j] for j in range(4)]
    basis = []
    for j in range(4):
        forcing = jnp.where(ocean[j], sto[j] * old[j] - FLUX_SCALE * divergence[j], 0.0)
        image = sto[j] * start[j]
        for i in range(4):
            image = image + faces[i][j] * (start[j] - around[i][j])
        basis.append((forcing - image) / diagonal[j])
    z0 = basis

    def spread(z):
        nb = [east(z), west(z), north(z), south(z)]
        return [
            (faces[0][j] * nb[0][j] + faces[1][j] * nb[1][j] + faces[2][j] * nb[2][j] + faces[3][j] * nb[3][j])
            * inverse[j]
            for j in range(4)
        ]

    z1 = spread(z0)
    z2 = spread(z1)
    zed[0] = start[0]
    zed[1] = z0[0]
    zed[2] = z1[0]
    zed[3] = z2[0]
    weighted = [diagonal[0] * z[0] for z in (z0, z1, z2)]
    north_weight = jnp.where(last, 1.0, 2.0)
    edge = z2[0] * (
        2.0 * faces[0][0] * east(z2)[0] + north_weight * faces[2][0] * north(z2)[0]
    )
    products = [
        weighted[0] * z0[0],
        weighted[0] * z1[0],
        weighted[1] * z1[0],
        weighted[1] * z2[0],
        weighted[2] * z2[0],
        edge,
    ]
    tile = zero
    for i, product in enumerate(products):
        total = jnp.sum(jnp.sum(product, axis=0, keepdims=True), axis=1, keepdims=True)
        tile = jnp.where(sub == i, total, tile)
    for i in range(moments.shape[0]):
        moments[i] = tile


def tracers_down(flags, state, diff, flat, around, rec_b, rec_a, far, near, gain, done):
    odd = flags[0]
    odd_lon = flags[2]
    lane = lane_iota()
    sub = sub_iota()
    level_count = flat[0]
    zero = jnp.zeros((8, 128), F32)

    def forward(chunk, carry):
        above, prev_gain, prev = carry
        for i in range(CHUNK):
            k = CHUNK * chunk + i
            kf = k.astype(F32)
            thick = thickness_at(kf)
            coefficient = diff[jnp.minimum(k, 46)]
            below = jnp.where(kf + 1.0 < level_count, coefficient * spacing_at(kf), 0.0)
            inverse = 1.0 / (thick + above + below - above * prev_gain)
            new_gain = below * inverse
            gain[chunk, i] = new_gain
            open_face = [kf < around[face] for face in range(4)]
            new = []
            for f in range(6):
                first = f * 48 + CHUNK * chunk
                q = state[pl.ds((first + i) * 8, 8), :]
                row_a = rec_a[f * 6 + chunk, i : i + 1, :]
                row_b = rec_b[f * 6 + chunk, i : i + 1, :]
                row_n = jnp.broadcast_to(jnp.where(odd == 1, row_b, row_a), (8, 128))
                row_s = jnp.broadcast_to(jnp.where(odd == 1, row_a, row_b), (8, 128))
                tile, j = first // 128, first % 128 + i
                a, b = far[LON_WIDE + tile], near[LON_WIDE + tile]
                side = lroll(jnp.where((lane == j).astype(jnp.int32) == odd_lon, a, b), (128 - j) % 128)
                change = jnp.where(open_face[0], lroll(jnp.where(lane == 0, side, q), 127) - q, 0.0)
                change += jnp.where(open_face[1], lroll(jnp.where(lane == 127, side, q), 1) - q, 0.0)
                change += jnp.where(open_face[2], sroll(jnp.where(sub == 0, row_n, q), 7) - q, 0.0)
                change += jnp.where(open_face[3], sroll(jnp.where(sub == 7, row_s, q), 1) - q, 0.0)
                value = (thick * (q + HORIZONTAL_RATE * change) + above * prev[f]) * inverse
                done[f, chunk, i] = value
                new.append(value)
            above, prev_gain, prev = below, new_gain, new
        return above, prev_gain, prev

    lax.fori_loop(0, K // CHUNK, forward, (zero, zero, [zero] * 6))


def tracers_up(gain, done, mixed_in, after, out):
    del after
    out[0 : 96 * 8, :] = mixed_in[...]
    zero = jnp.zeros((8, 128), F32)

    def backward(step, low):
        chunk = K // CHUNK - 1 - step
        for i in reversed(range(CHUNK)):
            g = gain[chunk, i]
            low = [done[f, chunk, i] + g * low[f] for f in range(6)]
            for f in range(6):
                out[pl.ds((96 + f * 48 + CHUNK * chunk + i) * 8, 8), :] = low[f]
        return low

    lax.fori_loop(0, K // CHUNK, backward, [zero] * 6)


def combine(parts, after, out):
    del after
    total = parts[0]
    for i in range(1, parts.shape[0]):
        total = total + parts[i]
    for i in range(out.shape[0]):
        out[i] = total


def finish(parts, zed, surface):
    total = parts[0]
    for i in range(1, parts.shape[0]):
        total = total + parts[i]
    nu = [jnp.broadcast_to(total[i : i + 1, :], (8, 128)) for i in range(6)]

    def inner(p, q, shift):
        out = None
        for i, a in enumerate(p):
            for j, b in enumerate(q):
                term = a * b * nu[i + j + shift]
                out = term if out is None else out + term
        return out

    one = jnp.ones((8, 128), F32)
    scaled = [one]
    direction = [one]
    product = nu[0]
    move = [jnp.zeros((8, 128), F32)] * 3
    for iteration in range(ITERS):
        curvature = inner(direction, direction, 0) - inner(direction, direction, 1)
        alpha = product / curvature
        for i, d in enumerate(direction):
            move[i] = move[i] + alpha * d
        if iteration + 1 < ITERS:
            longer = scaled + [jnp.zeros((8, 128), F32)]
            for i, d in enumerate(direction):
                longer[i] = longer[i] - alpha * d
                longer[i + 1] = longer[i + 1] + alpha * d
            scaled = longer
            following = inner(scaled, scaled, 0)
            beta = following / product
            direction = [
                scaled[i] + (beta * direction[i] if i < len(direction) else 0.0) for i in range(len(scaled))
            ]
            product = following
    surface[...] = zed[0] + move[0] * zed[1] + move[1] * zed[2] + move[2] * zed[3]


VMEM_LIMIT = 24 * 1024 * 1024
FIRST_LIMIT = 60 * 1024 * 1024
SMEM = pl.BlockSpec(memory_space=pltpu.SMEM)
VMEM = pl.BlockSpec(memory_space=pltpu.VMEM)
ANY = pl.BlockSpec(memory_space=pl.ANY)


def kernel(body, ins, outs, scratch=(), flops=0, nbytes=0, limit=VMEM_LIMIT):
    return pl.pallas_call(
        body,
        out_shape=[jax.ShapeDtypeStruct(s, F32) for s in outs],
        in_specs=ins,
        out_specs=[VMEM] * len(outs),
        scratch_shapes=[pltpu.VMEM(s, F32) if isinstance(s, tuple) else s for s in scratch],
        compiler_params=pltpu.CompilerParams(vmem_limit_bytes=limit),
        cost_estimate=pl.CostEstimate(flops=flops, bytes_accessed=nbytes, transcendentals=0),
    )


def lat_pairs(lat, lon):
    first, second = [], []
    for l in range(lat):
        for p in range(lon):
            here = l * lon + p
            first.append((here, (l ^ 1) * lon + p))
            if l == lat - 1:
                second.append((here, l * lon + lon - 1 - p))
            elif l % 2 == 1:
                second.append((here, here + lon))
            elif l > 0:
                second.append((here, here - lon))
    return first, second


def lon_pairs(lon):
    far, near = [], []
    for p in range(lon):
        step = 1 if p % 2 else -1
        far.append((p, (p + step) % lon))
        near.append((p, p ^ 1))
    return far, near


def make_local(mesh_shape):
    lat, lon = mesh_shape["lat"], mesh_shape["lon"]
    pairs_a, pairs_b = lat_pairs(lat, lon)
    pairs_far, pairs_near = lon_pairs(lon)
    both = ("lat", "lon")
    stages = reduction_stages(lat, lon)

    def local(ocean_state, viscosity, diffusivity, wet_levels, storage, surface_old):
        band = lax.axis_index("lat")
        place = lax.axis_index("lon")
        flags = jnp.stack([band % 2, (band == lat - 1).astype(jnp.int32), place % 2]).astype(jnp.int32)
        state = ocean_state.reshape(8 * K * 8, 128)
        pay_b, pay_a, uv, visc, flat = kernel(
            pack_lat,
            [SMEM] + [ANY] * 5,
            [(LAT_TILES, 8, 128)] * 2 + [(96 * 8, 128), (47, 8, 128), (3, 8, 128)],
            scratch=[pltpu.VMEM((8, 128), jnp.int32), pltpu.SemaphoreType.DMA((6,))],
            limit=FIRST_LIMIT,
        )(flags, state, viscosity, wet_levels, storage, surface_old)
        own = (uv, visc, flat)
        rec_b = lax.ppermute(pay_b, both, pairs_b)
        rec_a = lax.ppermute(pay_a, both, pairs_a)
        row_b, row_a, far_tracers, near_tracers, tracer = kernel(
            pack_tracers,
            [SMEM, ANY],
            [(ROW_TILES, 8, 128)] * 2 + [(3, 8, 128)] * 2 + [(288 * 8, 128)],
            scratch=[pltpu.SemaphoreType.DMA((2,))],
            flops=1_000_000,
            nbytes=2_000_000,
        )(flags, state)
        rec_row_b = lax.ppermute(row_b, both, pairs_b)
        rec_row_a = lax.ppermute(row_a, both, pairs_a)
        rows, row_x, pay_far, pay_near = kernel(
            pack_lon,
            [SMEM] + [VMEM] * 7,
            [(PLANES, 8, 128), (6, 8, 128), (LON_TILES, 8, 128), (LON_TILES, 8, 128)],
        )(flags, *own, rec_b, rec_a, far_tracers, near_tracers)
        rec_far = lax.ppermute(pay_far, "lon", pairs_far)
        rec_near = lax.ppermute(pay_near, "lon", pairs_near)
        chunked = (K // CHUNK, CHUNK)
        mixed, zed, around, moments = kernel(
            momentum_entry,
            [SMEM] + [VMEM] * 7 + [ANY] * 2,
            [(2 * K * 8, 128), (4, 8, 128), (4, 8, 128), (stages[0][1], 8, 128)],
            scratch=[(*chunked, 4, 8, 128), (2, *chunked, 4, 8, 128), (28, 8, 128), (6, 8, 128)],
        )(flags, *own, rows, row_x, rec_far, rec_near, rec_row_b, rec_row_a)
        (first_groups, _), (second_groups, second_size) = stages
        parts = lax.all_to_all(moments, both, 0, 0, axis_index_groups=first_groups, tiled=True)
        gain, done = kernel(
            tracers_down,
            [SMEM] + [VMEM] * 8,
            [(*chunked, 8, 128), (6, *chunked, 8, 128)],
            flops=10_000_000,
            nbytes=6_000_000,
        )(flags, tracer, diffusivity, flat, around, rec_row_b, rec_row_a, rec_far, rec_near)
        (parts,) = kernel(combine, [VMEM, ANY], [(second_size, 8, 128)])(parts, gain)
        sent = parts
        parts = lax.all_to_all(parts, both, 0, 0, axis_index_groups=second_groups, tiled=True)
        (mixed,) = kernel(
            tracers_up, [VMEM] * 3 + [ANY], [(8 * K * 8, 128)], flops=10_000_000, nbytes=6_000_000
        )(gain, done, mixed, sent)
        (surface,) = kernel(finish, [VMEM] * 2, [(8, 128)])(parts, zed)
        return mixed.reshape(8, K, 8, 128), surface

    return local


def momentum_entry(*refs):
    inputs, outputs, scratch = refs[:8], refs[10:14], refs[14:]
    mixed, zed, around, moments = outputs
    momentum(*inputs, mixed, zed, moments, *scratch)
    counts = scratch[2]
    for face in range(4):
        around[face] = counts[4 * face]


def reduction_stages(lat, lon):
    index = np.arange(lat * lon)
    if lat == 32 and lon == 16:
        grid = index.reshape(8, 4, 4, 2, 2)
        along_z = grid.transpose(1, 2, 4, 3, 0).reshape(32, 16)
        rest = grid.transpose(0, 3, 1, 2, 4).reshape(16, 32)
    else:
        grid = index.reshape(lat, lon)
        along_z, rest = grid.T, grid
    return [(g.tolist(), g.shape[1]) for g in (along_z, rest)]


def solution(mesh):
    placed = (
        P(None, None, "lat", "lon"),
        P(None, "lat", "lon"),
        P(None, "lat", "lon"),
        P("lat", "lon"),
        P("lat", "lon"),
        P("lat", "lon"),
    )
    return jax.shard_map(
        make_local(dict(mesh.shape)),
        mesh=mesh,
        in_specs=placed,
        out_specs=(P(None, None, "lat", "lon"), P("lat", "lon")),
        check_vma=False,
    )
```

```python
import functools

import jax
import jax.numpy as jnp
import numpy as np
from jax import lax
from jax.experimental import pallas as pl
from jax.experimental.pallas import tpu as pltpu
from jax.sharding import PartitionSpec as P

ITERS = 3
K = 48
HORIZONTAL_RATE = 0.2
FLUX_SCALE = 0.02
FACE_SCALE = 0.25
F32 = jnp.float32

PAIR_UV = 0
PAIR_VISC = 48
PAIR_SURF = 72
ROW_X = 73
LAT_TILES = 79
ROW_TILES = 36
PL_U, PL_V, PL_VISC, PL_WET, PL_STO, PL_SUR = 0, 48, 96, 143, 144, 145
PLANES = 146
HALO, CROSS = 152, 298
LON_WIDE = 10
LON_TILES = LON_WIDE + 3
CHUNK = 8
ZED, AROUND = 96, 100


def whereabouts():
    band = lax.axis_index("lat")
    return lax.rem(band, 2), band == lax.axis_size("lat") - 1, lax.rem(lax.axis_index("lon"), 2)


def sub_iota():
    return lax.broadcasted_iota(jnp.int32, (8, 128), 0)


def lane_iota():
    return lax.broadcasted_iota(jnp.int32, (8, 128), 1)


def lroll(x, shift):
    return pltpu.roll(x, shift, 1)


def sroll(x, shift):
    return pltpu.roll(x, shift, 0)


def flip_lanes(x):
    return jnp.take_along_axis(x, 127 - lane_iota(), axis=1)


def flip_rows(x):
    sub = sub_iota()
    x = sroll(x, 4)
    x = jnp.where((sub & 2) == 0, sroll(x, 6), sroll(x, 2))
    return jnp.where((sub & 1) == 0, sroll(x, 7), sroll(x, 1))


def thickness_at(level):
    return 0.5 + level * (1.0 / 48.0)


def spacing_at(level):
    return 96.0 / jnp.full((8, 128), 49.0 + 2.0 * level, F32)


def depth_of(count):
    return 0.5 * count + count * (count - 1.0) * (1.0 / 96.0)


def pack_lat(
    state_any, visc_any, wet_any, storage_any, surf_any,
    out_b, out_a, out_state, out_visc, out_flat,
    pay_b, pay_a, state, visc, flat, wet, sems, out_sems,
):
    odd, top, _ = whereabouts()
    half = 48 * 8
    copies = [
        pltpu.make_async_copy(state_any.at[pl.ds(0, half)], state.at[pl.ds(0, half)], sems.at[0]),
        pltpu.make_async_copy(state_any.at[pl.ds(half, half)], state.at[pl.ds(half, half)], sems.at[1]),
        pltpu.make_async_copy(visc_any, visc, sems.at[2]),
        pltpu.make_async_copy(wet_any, wet, sems.at[3]),
        pltpu.make_async_copy(storage_any, flat.at[1], sems.at[4]),
        pltpu.make_async_copy(surf_any, flat.at[2], sems.at[5]),
    ]
    for copy in copies:
        copy.start()
    sub = sub_iota()
    keep = (sub < 4).astype(jnp.int32) == odd

    def pack(tiles):
        @pl.when(jnp.logical_not(top))
        def _():
            for tile, first, second, _ in tiles():
                rolled = sroll(second, 4)
                pay_a[tile] = jnp.where(keep, first, rolled)
                pay_b[tile] = jnp.where(keep, rolled, first)

        @pl.when(top)
        def _():
            for tile, first, second, sign in tiles():
                rolled = sroll(second, 4)
                pay_a[tile] = jnp.where(keep, first, rolled)
                turned = flip_rows(flip_lanes(jnp.where(keep, rolled, first)))
                pay_b[tile] = -turned if sign < 0 else turned

    def velocities():
        for k in range(48):
            yield k, state[k * 8 : k * 8 + 8, :], state[(k + 48) * 8 : (k + 48) * 8 + 8, :], -1.0

    def others():
        for m in range(23):
            yield PAIR_VISC + m, visc[2 * m], visc[2 * m + 1], 1.0
        yield PAIR_VISC + 23, visc[46], flat[0], 1.0
        yield PAIR_SURF, flat[1], flat[2], 1.0

    def send(source, target, sem):
        copy = pltpu.make_async_copy(source, target, out_sems.at[sem])
        copy.start()
        return copy

    copies[0].wait()
    copies[1].wait()
    leaving = [send(state, out_state, 0)]
    pack(velocities)
    first = pl.ds(0, PAIR_VISC)
    leaving += [send(pay_b.at[first], out_b.at[first], 1), send(pay_a.at[first], out_a.at[first], 2)]
    for copy in copies[2:]:
        copy.wait()
    flat[0] = wet[...].astype(F32)
    leaving += [send(visc, out_visc, 3), send(flat, out_flat, 4)]
    pack(others)
    least = jnp.broadcast_to(jnp.minimum(flat[0, 3:4, :], flat[0, 4:5, :]), (8, 128))
    for m in range(6):
        start = (48 + 8 * m) * 8
        row3 = state[pl.ds(start + 3, 8, stride=8), :]
        row4 = state[pl.ds(start + 4, 8, stride=8), :]
        level = (sub + 8 * m).astype(F32)
        diff = jnp.where(level < least, row3 - row4, 0.0)
        pay_a[ROW_X + m] = diff
        pay_b[ROW_X + m] = -flip_lanes(diff)
    rest = pl.ds(PAIR_VISC, LAT_TILES - PAIR_VISC)
    leaving += [send(pay_b.at[rest], out_b.at[rest], 5), send(pay_a.at[rest], out_a.at[rest], 6)]
    for copy in leaving:
        copy.wait()


def pack_tracers(state_any, pay_b, pay_a, far, near, tracer, sems):
    half = 144 * 8
    copies = [
        pltpu.make_async_copy(
            state_any.at[pl.ds((96 + 144 * i) * 8, half)], tracer.at[pl.ds(i * half, half)], sems.at[i]
        )
        for i in range(2)
    ]
    for copy in copies:
        copy.start()
    for copy in copies:
        copy.wait()
    odd, top, odd_lon = whereabouts()
    lane = lane_iota()

    def rows_of(t):
        start = 8 * t * 8
        return tracer[pl.ds(start, 8, stride=8), :], tracer[pl.ds(start + 7, 8, stride=8), :]

    for t in range(ROW_TILES):
        row0, row7 = rows_of(t)
        pay_a[t] = jnp.where(odd == 1, row0, row7)
        pay_b[t] = jnp.where(odd == 1, row7, row0)

    @pl.when(top)
    def _():
        for t in range(ROW_TILES):
            pay_b[t] = flip_lanes(rows_of(t)[1])

    def scalar(n):
        return tracer[n * 8 : n * 8 + 8, :]

    for tile in range(3):
        planes = [functools.partial(scalar, n) for n in range(128 * tile, min(128 * tile + 128, 288))]
        east, west = pack_columns(lane, planes, 1)
        far[tile] = jnp.where(odd_lon == 1, east, west)
        near[tile] = jnp.where(odd_lon == 1, west, east)


def pack_columns(lane, planes, width):
    east = jnp.zeros((8, 128), F32)
    west = jnp.zeros((8, 128), F32)
    slots = 128 // width
    slot_of = lane // width
    for j, load in enumerate(planes):
        x = load()
        x = lroll(x, j * width) if j else x
        west = jnp.where(slot_of == j, x, west)
        east = jnp.where(slot_of == (j - 1) % slots, x, east)
    return east, west


def lon_planes(state, visc, flat, rows, row_x):
    def plane(n):
        if n < 96:
            return state[n * 8 : n * 8 + 8, :]
        if n < 143:
            return visc[n - 96]
        if n < 146:
            return flat[n - 143]
        if n < HALO:
            return flat[0]
        if n < CROSS:
            return rows[n - HALO]
        return row_x[n - CROSS]

    lane = lane_iota()
    for tile in range(LON_WIDE):
        planes = [functools.partial(plane, n) for n in range(32 * tile, min(32 * tile + 32, CROSS + 6))]
        east, west = pack_columns(lane, planes, 4)
        yield tile, (lroll(east, 64), west)


def pack_lon(
    state, visc, flat, rec_b, rec_a, far_tracers, near_tracers, rows, row_x, far, near
):
    odd, _, odd_lon = whereabouts()
    sub = sub_iota()
    keep = (sub < 4).astype(jnp.int32) != odd

    def unpair(tile):
        a, b = rec_a[tile], rec_b[tile]
        return jnp.where(keep, a, b), sroll(jnp.where(keep, b, a), 4)

    for k in range(48):
        first, second = unpair(k)
        rows[PL_U + k] = first
        rows[PL_V + k] = second
    for m in range(24):
        first, second = unpair(PAIR_VISC + m)
        rows[PL_VISC + 2 * m] = first
        rows[PL_VISC + 2 * m + 1] = second
    first, second = unpair(PAIR_SURF)
    rows[PL_STO] = first
    rows[PL_SUR] = second
    for m in range(6):
        row_x[m] = jnp.where(odd == 1, rec_b[ROW_X + m], rec_a[ROW_X + m])
    for tile, (east, west) in lon_planes(state, visc, flat, rows, row_x):
        far[tile] = jnp.where(odd_lon == 1, east, west)
        near[tile] = jnp.where(odd_lon == 1, west, east)
    for tile in range(3):
        far[LON_WIDE + tile] = far_tracers[tile]
        near[LON_WIDE + tile] = near_tracers[tile]


def each(fn, *lists):
    return [fn(*items) for items in zip(*lists)]


def north_pair(q):
    sub = sub_iota()
    return [sroll(jnp.where(sub == 0, q[1], q[0]), 7), sroll(jnp.where(sub == 0, q[0], q[1]), 7)]


def south_pair(q):
    sub = sub_iota()
    return [sroll(jnp.where(sub == 7, q[1], q[0]), 1), sroll(jnp.where(sub == 7, q[0], q[1]), 1)]


def east_within(q):
    return [lroll(x, 127) for x in q]


def west_within(q):
    return [lroll(x, 1) for x in q]


def columns(load, cross_row, coefficient_at, level_count, top, counts, gain, done, keep):
    sub = sub_iota()
    zero = jnp.zeros((8, 128), F32)
    cross = jnp.logical_and(top, sub == 3)
    ghost = jnp.logical_and(top, sub < 4)
    face_east = each(jnp.minimum, level_count, east_within(level_count))
    face_west = each(jnp.minimum, level_count, west_within(level_count))
    face_north = each(jnp.minimum, level_count, north_pair(level_count))
    face_south = each(jnp.minimum, level_count, south_pair(level_count))
    sums = [
        face_east[0], jnp.where(ghost, face_west[1], face_east[1]),
        face_north[0], jnp.where(ghost, face_south[1], face_north[1]),
    ]
    for i, tile in enumerate(face_east + face_north + level_count + sums):
        counts[i] = tile

    def blend(field, chunk, i, open_east, open_north):
        q = load(field, chunk, i)
        over_east = each(lambda o, a, b: jnp.where(o, a - b, 0.0), open_east, east_within(q), q)
        over_north = each(lambda o, a, b: jnp.where(o, a - b, 0.0), open_north, north_pair(q), q)
        if field == 1:
            over_north[1] = jnp.where(cross, cross_row(chunk, i), over_north[1])
        return each(
            lambda c, a, b, d, e: c + HORIZONTAL_RATE * (a - b + d - e),
            q, over_east, west_within(over_east), over_north, south_pair(over_north),
        )

    def forward(chunk, carry):
        above, prev_gain, prev = carry
        for i in range(CHUNK):
            kf = (CHUNK * chunk + i).astype(F32)
            thick = thickness_at(kf)
            space = spacing_at(kf)
            coefficient = coefficient_at(chunk, i)
            below = [jnp.where(kf + 1.0 < counts[4 + j], coefficient[j] * space, 0.0) for j in range(2)]
            open_east = [kf < counts[j] for j in range(2)]
            open_north = [kf < counts[2 + j] for j in range(2)]
            inverse = [1.0 / (thick + above[j] + below[j] - above[j] * prev_gain[j]) for j in range(2)]
            new_gain = [below[j] * inverse[j] for j in range(2)]
            new = []
            for field in range(2):
                value = blend(field, chunk, i, open_east, open_north)
                new.append([(thick * value[j] + above[j] * prev[field][j]) * inverse[j] for j in range(2)])
            for j in range(2):
                gain[chunk, i, j] = new_gain[j]
                done[0, chunk, i, j] = new[0][j]
                done[1, chunk, i, j] = new[1][j]
            above, prev_gain, prev = below, new_gain, new
        return above, prev_gain, prev

    zeros = [zero, zero]
    lax.fori_loop(0, K // CHUNK, forward, (zeros, zeros, [zeros, zeros]))

    def backward(step, carry):
        chunk = K // CHUNK - 1 - step
        low, flux = carry
        for i in reversed(range(CHUNK)):
            k = CHUNK * chunk + i
            kf = k.astype(F32)
            thick = thickness_at(kf)
            low = [
                [done[field, chunk, i, j] + gain[chunk, i, j] * low[field][j] for j in range(2)] for field in range(2)
            ]
            flux = [
                [
                    flux[field][j] + jnp.where(kf < counts[6 + 2 * field + j], thick * low[field][j], 0.0)
                    for j in range(2)
                ]
                for field in range(2)
            ]
            for field in range(2):
                keep(field, k, low[field][0])
        return low, flux

    _, flux = lax.fori_loop(0, K // CHUNK, backward, ([zeros, zeros], [zeros, zeros]))
    return flux


def momentum_inner(state, visc, flat, rows, row_x, mixed, flux_out, gain, done, counts):
    _, top, _ = whereabouts()

    def load(field, chunk, i):
        n = 48 * field + CHUNK * chunk + i
        return [state[pl.ds(n * 8, 8), :], rows[n]]

    def coefficient_at(chunk, i):
        k = CHUNK * chunk + i
        return [visc[jnp.minimum(k, 46)], rows[PL_VISC + k]]

    def cross_row(chunk, i):
        return jnp.broadcast_to(row_x[chunk, i : i + 1, :], (8, 128))

    def keep(field, k, tile):
        mixed[48 * field + k] = tile

    flux = columns(load, cross_row, coefficient_at, [flat[0], rows[PL_WET]], top, counts, gain, done, keep)
    for field in range(2):
        for j in range(2):
            flux_out[2 * field + j] = flux[field][j]


def momentum(
    state, visc, flat, rows, row_x, flux_inner, far, near,
    mixed, moments,
    gain, done, counts, planes2, xs,
):
    _, top, odd_lon = whereabouts()
    lane = lane_iota()
    sub = sub_iota()
    slot_of = lane // 4
    from_halo = jnp.logical_or(lane < 4, slot_of == 15)
    from_start = slot_of == 16
    zero = jnp.zeros((8, 128), F32)

    def strip_at(tile, j):
        a, b = far[tile], near[tile]
        mine = (slot_of == j).astype(jnp.int32) == odd_lon
        return lroll(jnp.where(mine, a, b), (128 - 4 * j) & 127)

    def strip(n):
        return strip_at(n // 32, n % 32)

    def around_edges(own, halo):
        return jnp.where(from_halo, halo, jnp.where(from_start, lroll(own, 64), own))

    def edges_at(own, chunk, first, i):
        base = first + CHUNK * chunk
        return around_edges(own, strip_at(base >> 5, (base & 31) + i))

    def spread_out(x):
        return jnp.where(lane < 64, x, lroll(x, 64))

    for m in range(6):
        xs[m] = around_edges(row_x[m], strip(m + CROSS))

    def load(field, chunk, i):
        n = 48 * field + CHUNK * chunk + i
        return [
            edges_at(state[pl.ds(n * 8, 8), :], chunk, 48 * field, i),
            edges_at(rows[n], chunk, 48 * field + HALO, i),
        ]

    def coefficient_at(chunk, i):
        k = CHUNK * chunk + i
        return [
            edges_at(visc[jnp.minimum(k, 46)], chunk, PL_VISC, i),
            edges_at(rows[PL_VISC + k], chunk, PL_VISC + HALO, i),
        ]

    def cross_row(chunk, i):
        return jnp.broadcast_to(xs[chunk, i : i + 1, :], (8, 128))

    def keep(field, k, tile):
        mixed[48 * field + k] = tile

    here = jnp.logical_or(from_halo, jnp.logical_or(from_start, lane >= 124))
    wet_edges = [
        jnp.where(here, around_edges(flat[0], strip(PL_WET)), 0.0),
        jnp.where(here, around_edges(rows[PL_WET], strip(PL_WET + HALO)), 0.0),
    ]
    edge_flux = columns(load, cross_row, coefficient_at, wet_edges, top, counts, gain, done, keep)

    def put_together(inner, edge):
        own = [
            jnp.where(lane == 127, e, jnp.where(lane == 0, lroll(e, 64), q)) for q, e in zip(inner, edge)
        ]
        return own + [spread_out(e) for e in edge]

    flux_u = put_together([flux_inner[0], flux_inner[1]], edge_flux[0])
    flux_v = put_together([flux_inner[2], flux_inner[3]], edge_flux[1])

    valid = jnp.logical_or(lane < 4, lane >= 124)

    def four(n, own):
        halo = [jnp.where(valid, spread_out(strip(m)), 0.0) for m in (n, n + HALO)]
        return [own, rows[n]] + halo

    def east(q):
        return [
            lroll(jnp.where(lane == 0, q[2], q[0]), 127),
            lroll(jnp.where(lane == 0, q[3], q[1]), 127),
            lroll(jnp.where(lane == 0, q[0], q[2]), 127),
            lroll(jnp.where(lane == 0, q[1], q[3]), 127),
        ]

    def west(q):
        return [
            lroll(jnp.where(lane == 127, q[2], q[0]), 1),
            lroll(jnp.where(lane == 127, q[3], q[1]), 1),
            lroll(jnp.where(lane == 127, q[0], q[2]), 1),
            lroll(jnp.where(lane == 127, q[1], q[3]), 1),
        ]

    def north(q):
        return north_pair(q[:2]) + north_pair(q[2:])

    def south(q):
        return south_pair(q[:2]) + south_pair(q[2:])

    level_count = four(PL_WET, flat[0])
    around = [each(jnp.minimum, level_count, shift(level_count)) for shift in (east, west, north, south)]
    for i, c in enumerate(around):
        for j in range(4):
            planes2[4 * i + j] = c[j]
    for j in range(4):
        planes2[16 + j] = level_count[j]
    ghost = jnp.logical_and(top, sub < 4)

    last = jnp.logical_and(top, sub == 7)
    first_ghost = jnp.logical_and(top, sub == 0)
    flux_v = [
        jnp.where(last, 0.0, flux_v[0]),
        jnp.where(first_ghost, 0.0, flux_v[1]),
        jnp.where(last, 0.0, flux_v[2]),
        jnp.where(first_ghost, 0.0, flux_v[3]),
    ]
    plain = each(
        lambda a, b, c, d: a - b + c - d, flux_u, west(flux_u), flux_v, south(flux_v)
    )
    mirrored = each(
        lambda a, b, c, d: a - b + c - d, east(flux_u), flux_u, north(flux_v), flux_v
    )
    divergence = [
        plain[0],
        jnp.where(ghost, mirrored[1], plain[1]),
        plain[2],
        jnp.where(ghost, mirrored[3], plain[3]),
    ]
    sto = four(PL_STO, flat[1])
    old = four(PL_SUR, flat[2])
    faces = [[FACE_SCALE * depth_of(planes2[4 * i + j]) for j in range(4)] for i in range(4)]
    diagonal = [
        jnp.maximum(sto[j] + faces[0][j] + faces[1][j] + faces[2][j] + faces[3][j], 0.1) for j in range(4)
    ]
    ocean = [planes2[16 + j] > 0.0 for j in range(4)]
    start = [jnp.where(ocean[j], old[j], 0.0) for j in range(4)]
    around = [east(start), west(start), north(start), south(start)]
    inverse = [1.0 / diagonal[j] for j in range(4)]
    basis = []
    for j in range(4):
        forcing = jnp.where(ocean[j], sto[j] * old[j] - FLUX_SCALE * divergence[j], 0.0)
        image = sto[j] * start[j]
        for i in range(4):
            image = image + faces[i][j] * (start[j] - around[i][j])
        basis.append((forcing - image) / diagonal[j])
    z0 = basis

    def spread(z):
        nb = [east(z), west(z), north(z), south(z)]
        return [
            (faces[0][j] * nb[0][j] + faces[1][j] * nb[1][j] + faces[2][j] * nb[2][j] + faces[3][j] * nb[3][j])
            * inverse[j]
            for j in range(4)
        ]

    z1 = spread(z0)
    z2 = spread(z1)
    mixed[ZED + 0] = start[0]
    mixed[ZED + 1] = z0[0]
    mixed[ZED + 2] = z1[0]
    mixed[ZED + 3] = z2[0]
    weighted = [diagonal[0] * z[0] for z in (z0, z1, z2)]
    north_weight = jnp.where(last, 1.0, 2.0)
    edge = z2[0] * (
        2.0 * faces[0][0] * east(z2)[0] + north_weight * faces[2][0] * north(z2)[0]
    )
    products = [
        weighted[0] * z0[0],
        weighted[0] * z1[0],
        weighted[1] * z1[0],
        weighted[1] * z2[0],
        weighted[2] * z2[0],
        edge,
    ]
    row = jnp.zeros((1, 128), F32)
    for i, product in enumerate(products):
        total = jnp.sum(jnp.sum(product, axis=0, keepdims=True), axis=1, keepdims=True)
        row = jnp.where(lane[:1] == i, total, row)
    moments[...] = jnp.broadcast_to(row, moments.shape)


def tracers_down(state, diff, flat, mixed, rec_b, rec_a, far, near, gain, done):
    odd, _, odd_lon = whereabouts()
    lane = lane_iota()
    sub = sub_iota()
    level_count = flat[0]
    zero = jnp.zeros((8, 128), F32)

    def forward(chunk, carry):
        above, prev_gain, prev = carry
        for i in range(CHUNK):
            k = CHUNK * chunk + i
            kf = k.astype(F32)
            thick = thickness_at(kf)
            coefficient = diff[jnp.minimum(k, 46)]
            below = jnp.where(kf + 1.0 < level_count, coefficient * spacing_at(kf), 0.0)
            inverse = 1.0 / (thick + above + below - above * prev_gain)
            new_gain = below * inverse
            gain[chunk, i] = new_gain
            open_face = [kf < mixed[AROUND + face] for face in range(4)]
            new = []
            for f in range(6):
                first = f * 48 + CHUNK * chunk
                q = state[pl.ds((first + i) * 8, 8), :]
                row_a = rec_a[f * 6 + chunk, i : i + 1, :]
                row_b = rec_b[f * 6 + chunk, i : i + 1, :]
                row_n = jnp.broadcast_to(jnp.where(odd == 1, row_b, row_a), (8, 128))
                row_s = jnp.broadcast_to(jnp.where(odd == 1, row_a, row_b), (8, 128))
                tile, j = first >> 7, (first & 127) + i
                a, b = far[LON_WIDE + tile], near[LON_WIDE + tile]
                side = lroll(jnp.where((lane == j).astype(jnp.int32) == odd_lon, a, b), (128 - j) & 127)
                change = jnp.where(open_face[0], lroll(jnp.where(lane == 0, side, q), 127) - q, 0.0)
                change += jnp.where(open_face[1], lroll(jnp.where(lane == 127, side, q), 1) - q, 0.0)
                change += jnp.where(open_face[2], sroll(jnp.where(sub == 0, row_n, q), 7) - q, 0.0)
                change += jnp.where(open_face[3], sroll(jnp.where(sub == 7, row_s, q), 1) - q, 0.0)
                value = (thick * (q + HORIZONTAL_RATE * change) + above * prev[f]) * inverse
                done[f, chunk, i] = value
                new.append(value)
            above, prev_gain, prev = below, new_gain, new
        return above, prev_gain, prev

    lax.fori_loop(0, K // CHUNK, forward, (zero, zero, [zero] * 6))


def tracers_up(gain, done, inner, mixed, after, out):
    del after
    lane = lane_iota()
    for n in range(96):
        edge = mixed[n]
        out[n] = jnp.where(lane == 127, edge, jnp.where(lane == 0, lroll(edge, 64), inner[n]))
    zero = jnp.zeros((8, 128), F32)

    def backward(step, low):
        chunk = K // CHUNK - 1 - step
        for i in reversed(range(CHUNK)):
            g = gain[chunk, i]
            low = [done[f, chunk, i] + g * low[f] for f in range(6)]
            for f in range(6):
                out[96 + f * 48 + CHUNK * chunk + i] = low[f]
        return low

    lax.fori_loop(0, K // CHUNK, backward, [zero] * 6)


def combine(parts, after, out):
    del after
    out[...] = jnp.broadcast_to(jnp.sum(parts[...], axis=0, keepdims=True), out.shape)


def finish(parts, mixed, surface):
    total = jnp.sum(parts[...], axis=0, keepdims=True)
    nu = [jnp.broadcast_to(total[:, i : i + 1], (8, 128)) for i in range(6)]

    def inner(p, q, shift):
        out = None
        for i, a in enumerate(p):
            for j, b in enumerate(q):
                term = a * b * nu[i + j + shift]
                out = term if out is None else out + term
        return out

    one = jnp.ones((8, 128), F32)
    scaled = [one]
    direction = [one]
    product = nu[0]
    move = [jnp.zeros((8, 128), F32)] * 3
    for iteration in range(ITERS):
        curvature = inner(direction, direction, 0) - inner(direction, direction, 1)
        alpha = product / curvature
        for i, d in enumerate(direction):
            move[i] = move[i] + alpha * d
        if iteration + 1 < ITERS:
            longer = scaled + [jnp.zeros((8, 128), F32)]
            for i, d in enumerate(direction):
                longer[i] = longer[i] - alpha * d
                longer[i + 1] = longer[i + 1] + alpha * d
            scaled = longer
            following = inner(scaled, scaled, 0)
            beta = following / product
            direction = [
                scaled[i] + (beta * direction[i] if i < len(direction) else 0.0) for i in range(len(scaled))
            ]
            product = following
    surface[...] = sum((move[i] * mixed[ZED + 1 + i] for i in range(3)), mixed[ZED])


VMEM_LIMIT = 24 * 1024 * 1024
FIRST_LIMIT = 60 * 1024 * 1024
VMEM = pl.BlockSpec(memory_space=pltpu.VMEM)
ANY = pl.BlockSpec(memory_space=pl.ANY)


def kernel(body, ins, outs, scratch=(), flops=0, nbytes=0, limit=VMEM_LIMIT, out_spec=VMEM):
    return pl.pallas_call(
        body,
        out_shape=[jax.ShapeDtypeStruct(s, F32) for s in outs],
        in_specs=ins,
        out_specs=[out_spec] * len(outs),
        scratch_shapes=[pltpu.VMEM(s, F32) if isinstance(s, tuple) else s for s in scratch],
        compiler_params=pltpu.CompilerParams(vmem_limit_bytes=limit),
        cost_estimate=pl.CostEstimate(flops=flops, bytes_accessed=nbytes, transcendentals=0),
    )


def lat_pairs(lat, lon):
    first, second = [], []
    for l in range(lat):
        for p in range(lon):
            here = l * lon + p
            first.append((here, (l ^ 1) * lon + p))
            if l == lat - 1:
                second.append((here, l * lon + lon - 1 - p))
            elif l % 2 == 1:
                second.append((here, here + lon))
            elif l > 0:
                second.append((here, here - lon))
    return first, second


def lon_pairs(lon):
    far, near = [], []
    for p in range(lon):
        step = 1 if p % 2 else -1
        far.append((p, (p + step) % lon))
        near.append((p, p ^ 1))
    return far, near


def make_local(mesh_shape):
    lat, lon = mesh_shape["lat"], mesh_shape["lon"]
    pairs_a, pairs_b = lat_pairs(lat, lon)
    pairs_far, pairs_near = lon_pairs(lon)
    both = ("lat", "lon")
    stages = reduction_stages(lat, lon)

    def local(ocean_state, viscosity, diffusivity, wet_levels, storage, surface_old):
        state = ocean_state.reshape(8 * K * 8, 128)
        pay_b, pay_a, uv, visc, flat = kernel(
            pack_lat,
            [ANY] * 5,
            [(LAT_TILES, 8, 128)] * 2 + [(96 * 8, 128), (47, 8, 128), (3, 8, 128)],
            scratch=[(LAT_TILES, 8, 128)] * 2 + [
                (96 * 8, 128), (47, 8, 128), (3, 8, 128),
                pltpu.VMEM((8, 128), jnp.int32), pltpu.SemaphoreType.DMA((6,)), pltpu.SemaphoreType.DMA((7,)),
            ],
            out_spec=ANY,
            limit=FIRST_LIMIT,
        )(state, viscosity, wet_levels, storage, surface_old)
        own = (uv, visc, flat)
        rec_b = lax.ppermute(pay_b, both, pairs_b)
        rec_a = lax.ppermute(pay_a, both, pairs_a)
        row_b, row_a, far_tracers, near_tracers, tracer = kernel(
            pack_tracers,
            [ANY],
            [(ROW_TILES, 8, 128)] * 2 + [(3, 8, 128)] * 2 + [(288 * 8, 128)],
            scratch=[pltpu.SemaphoreType.DMA((2,))],
            flops=1_000_000,
            nbytes=2_000_000,
        )(state)
        rec_row_b = lax.ppermute(row_b, both, pairs_b)
        rec_row_a = lax.ppermute(row_a, both, pairs_a)
        rows, row_x, pay_far, pay_near = kernel(
            pack_lon,
            [VMEM] * 7,
            [(PLANES, 8, 128), (6, 8, 128), (LON_TILES, 8, 128), (LON_TILES, 8, 128)],
        )(*own, rec_b, rec_a, far_tracers, near_tracers)
        rec_far = lax.ppermute(pay_far, "lon", pairs_far)
        rec_near = lax.ppermute(pay_near, "lon", pairs_near)
        chunked = (K // CHUNK, CHUNK)
        scratch = [(*chunked, 2, 8, 128), (2, *chunked, 2, 8, 128), (10, 8, 128)]
        inner, flux_inner = kernel(
            momentum_inner,
            [VMEM] * 5,
            [(2 * K, 8, 128), (4, 8, 128)],
            scratch=scratch,
            flops=10_000_000,
            nbytes=6_000_000,
        )(*own, rows, row_x)
        mixed, moments = kernel(
            momentum_entry,
            [VMEM] * 8 + [ANY] * 2,
            [(2 * K + 8, 8, 128), (stages[0][1], 128)],
            scratch=scratch + [(20, 8, 128), (6, 8, 128)],
        )(*own, rows, row_x, flux_inner, rec_far, rec_near, rec_row_b, rec_row_a)
        (first_groups, _), (second_groups, second_size) = stages
        parts = lax.all_to_all(moments, both, 0, 0, axis_index_groups=first_groups, tiled=True)
        gain, done = kernel(
            tracers_down,
            [VMEM] * 8,
            [(*chunked, 8, 128), (6, *chunked, 8, 128)],
            flops=10_000_000,
            nbytes=6_000_000,
        )(tracer, diffusivity, flat, mixed, rec_row_b, rec_row_a, rec_far, rec_near)
        (parts,) = kernel(combine, [VMEM, ANY], [(second_size, 128)])(parts, gain)
        sent = parts
        parts = lax.all_to_all(parts, both, 0, 0, axis_index_groups=second_groups, tiled=True)
        (state_out,) = kernel(
            tracers_up, [VMEM] * 4 + [ANY], [(8 * K, 8, 128)], flops=10_000_000, nbytes=6_000_000
        )(gain, done, inner, mixed, sent)
        (surface,) = kernel(finish, [VMEM] * 2, [(8, 128)])(parts, mixed)
        return state_out.reshape(8, K, 8, 128), surface

    return local


def momentum_entry(*refs):
    inputs, outputs, scratch = refs[:8], refs[10:12], refs[12:]
    mixed, moments = outputs
    momentum(*inputs, mixed, moments, *scratch)
    planes2 = scratch[3]
    for face in range(4):
        mixed[AROUND + face] = planes2[4 * face]


def reduction_stages(lat, lon):
    index = np.arange(lat * lon)
    if lat == 32 and lon == 16:
        grid = index.reshape(8, 4, 4, 2, 2)
        along_z = grid.transpose(1, 2, 4, 3, 0).reshape(32, 16)
        rest = grid.transpose(0, 3, 1, 2, 4).reshape(16, 32)
    else:
        grid = index.reshape(lat, lon)
        along_z, rest = grid.T, grid
    return [(g.tolist(), g.shape[1]) for g in (along_z, rest)]


def solution(mesh):
    placed = (
        P(None, None, "lat", "lon"),
        P(None, "lat", "lon"),
        P(None, "lat", "lon"),
        P("lat", "lon"),
        P("lat", "lon"),
        P("lat", "lon"),
    )
    return jax.shard_map(
        make_local(dict(mesh.shape)),
        mesh=mesh,
        in_specs=placed,
        out_specs=(P(None, None, "lat", "lon"), P("lat", "lon")),
        check_vma=False,
    )
```

```python
import functools

import jax
import jax.numpy as jnp
import numpy as np
from jax import lax
from jax.experimental import pallas as pl
from jax.experimental.pallas import tpu as pltpu
from jax.sharding import PartitionSpec as P

ITERS = 3
K = 48
HORIZONTAL_RATE = 0.2
FLUX_SCALE = 0.02
FACE_SCALE = 0.25
F32 = jnp.float32

PAIR_UV = 0
PAIR_VISC = 48
PAIR_SURF = 72
ROW_X = 73
LAT_TILES = 79
ROW_TILES = 36
PL_U, PL_V, PL_VISC, PL_WET, PL_STO, PL_SUR = 0, 48, 96, 143, 144, 145
PLANES = 146
HALO, CROSS = 152, 298
LON_WIDE = 10
LON_TILES = LON_WIDE + 3
CHUNK = 8
ZED, AROUND = 96, 100


def whereabouts():
    band = lax.axis_index("lat")
    return lax.rem(band, 2), band == lax.axis_size("lat") - 1, lax.rem(lax.axis_index("lon"), 2)


def sub_iota():
    return lax.broadcasted_iota(jnp.int32, (8, 128), 0)


def lane_iota():
    return lax.broadcasted_iota(jnp.int32, (8, 128), 1)


def lroll(x, shift):
    return pltpu.roll(x, shift, 1)


def sroll(x, shift):
    return pltpu.roll(x, shift, 0)


def flip_lanes(x):
    return jnp.take_along_axis(x, 127 - lane_iota(), axis=1)


def flip_rows(x):
    sub = sub_iota()
    x = sroll(x, 4)
    x = jnp.where((sub & 2) == 0, sroll(x, 6), sroll(x, 2))
    return jnp.where((sub & 1) == 0, sroll(x, 7), sroll(x, 1))


def thickness_at(level):
    return 0.5 + level * (1.0 / 48.0)


def spacing_at(level):
    return 96.0 / jnp.full((8, 128), 49.0 + 2.0 * level, F32)


def depth_of(count):
    return 0.5 * count + count * (count - 1.0) * (1.0 / 96.0)


def pack_lat(
    state_any, visc_any, wet_any, storage_any, surf_any,
    out_b, out_a, out_state, out_visc, out_flat,
    pay_b, pay_a, state, visc, flat, wet, sems, out_sems,
):
    odd, top, _ = whereabouts()
    half = 48 * 8
    copies = [
        pltpu.make_async_copy(state_any.at[pl.ds(0, half)], state.at[pl.ds(0, half)], sems.at[0]),
        pltpu.make_async_copy(state_any.at[pl.ds(half, half)], state.at[pl.ds(half, half)], sems.at[1]),
        pltpu.make_async_copy(visc_any, visc, sems.at[2]),
        pltpu.make_async_copy(wet_any, wet, sems.at[3]),
        pltpu.make_async_copy(storage_any, flat.at[1], sems.at[4]),
        pltpu.make_async_copy(surf_any, flat.at[2], sems.at[5]),
    ]
    for copy in copies:
        copy.start()
    sub = sub_iota()
    keep = (sub < 4).astype(jnp.int32) == odd

    def pack(tiles):
        @pl.when(jnp.logical_not(top))
        def _():
            for tile, first, second, _ in tiles():
                rolled = sroll(second, 4)
                pay_a[tile] = jnp.where(keep, first, rolled)
                pay_b[tile] = jnp.where(keep, rolled, first)

        @pl.when(top)
        def _():
            for tile, first, second, sign in tiles():
                rolled = sroll(second, 4)
                pay_a[tile] = jnp.where(keep, first, rolled)
                turned = flip_rows(flip_lanes(jnp.where(keep, rolled, first)))
                pay_b[tile] = -turned if sign < 0 else turned

    def velocities():
        for k in range(48):
            yield k, state[k * 8 : k * 8 + 8, :], state[(k + 48) * 8 : (k + 48) * 8 + 8, :], -1.0

    def others():
        for m in range(23):
            yield PAIR_VISC + m, visc[2 * m], visc[2 * m + 1], 1.0
        yield PAIR_VISC + 23, visc[46], flat[0], 1.0
        yield PAIR_SURF, flat[1], flat[2], 1.0

    def send(source, target, sem):
        copy = pltpu.make_async_copy(source, target, out_sems.at[sem])
        copy.start()
        return copy

    copies[0].wait()
    copies[1].wait()
    leaving = [send(state, out_state, 0)]
    pack(velocities)
    first = pl.ds(0, PAIR_VISC)
    leaving += [send(pay_b.at[first], out_b.at[first], 1), send(pay_a.at[first], out_a.at[first], 2)]
    for copy in copies[2:]:
        copy.wait()
    flat[0] = wet[...].astype(F32)
    leaving += [send(visc, out_visc, 3), send(flat, out_flat, 4)]
    pack(others)
    least = jnp.broadcast_to(jnp.minimum(flat[0, 3:4, :], flat[0, 4:5, :]), (8, 128))
    for m in range(6):
        start = (48 + 8 * m) * 8
        row3 = state[pl.ds(start + 3, 8, stride=8), :]
        row4 = state[pl.ds(start + 4, 8, stride=8), :]
        level = (sub + 8 * m).astype(F32)
        diff = jnp.where(level < least, row3 - row4, 0.0)
        pay_b[ROW_X + m] = -flip_lanes(diff)
    rest_b, rest_a = (pl.ds(PAIR_VISC, count - PAIR_VISC) for count in (LAT_TILES, ROW_X))
    leaving += [send(pay_b.at[rest_b], out_b.at[rest_b], 5), send(pay_a.at[rest_a], out_a.at[rest_a], 6)]
    for copy in leaving:
        copy.wait()


def pack_tracers(state_any, pay_b, pay_a, far, near, tracer, sems):
    half = 144 * 8
    copies = [
        pltpu.make_async_copy(
            state_any.at[pl.ds((96 + 144 * i) * 8, half)], tracer.at[pl.ds(i * half, half)], sems.at[i]
        )
        for i in range(2)
    ]
    for copy in copies:
        copy.start()
    for copy in copies:
        copy.wait()
    odd, top, odd_lon = whereabouts()
    lane = lane_iota()

    def rows_of(t):
        start = 8 * t * 8
        return tracer[pl.ds(start, 8, stride=8), :], tracer[pl.ds(start + 7, 8, stride=8), :]

    for t in range(ROW_TILES):
        row0, row7 = rows_of(t)
        pay_a[t] = jnp.where(odd == 1, row0, row7)
        pay_b[t] = jnp.where(odd == 1, row7, row0)

    @pl.when(top)
    def _():
        for t in range(ROW_TILES):
            pay_b[t] = flip_lanes(rows_of(t)[1])

    def scalar(n):
        return tracer[n * 8 : n * 8 + 8, :]

    for tile in range(3):
        planes = [functools.partial(scalar, n) for n in range(128 * tile, min(128 * tile + 128, 288))]
        east, west = pack_columns(lane, planes, 1)
        far[tile] = jnp.where(odd_lon == 1, east, west)
        near[tile] = jnp.where(odd_lon == 1, west, east)


def pack_columns(lane, planes, width):
    east = jnp.zeros((8, 128), F32)
    west = jnp.zeros((8, 128), F32)
    slots = 128 // width
    slot_of = lane // width
    for j, load in enumerate(planes):
        x = load()
        x = lroll(x, j * width) if j else x
        west = jnp.where(slot_of == j, x, west)
        east = jnp.where(slot_of == (j - 1) % slots, x, east)
    return east, west


def lon_planes(state, visc, flat, rows, row_x):
    def plane(n):
        if n < 96:
            return state[n * 8 : n * 8 + 8, :]
        if n < 143:
            return visc[n - 96]
        if n < 146:
            return flat[n - 143]
        if n < HALO:
            return flat[0]
        if n < CROSS:
            return rows[n - HALO]
        return row_x[n - CROSS]

    lane = lane_iota()
    for tile in range(LON_WIDE):
        planes = [functools.partial(plane, n) for n in range(32 * tile, min(32 * tile + 32, CROSS + 6))]
        east, west = pack_columns(lane, planes, 4)
        yield tile, (lroll(east, 64), west)


def pack_lon(
    state, visc, flat, rec_b, rec_a, far_tracers, near_tracers, rows, row_x, far, near
):
    odd, _, odd_lon = whereabouts()
    sub = sub_iota()
    keep = (sub < 4).astype(jnp.int32) != odd

    def unpair(tile):
        a, b = rec_a[tile], rec_b[tile]
        return jnp.where(keep, a, b), sroll(jnp.where(keep, b, a), 4)

    for k in range(48):
        first, second = unpair(k)
        rows[PL_U + k] = first
        rows[PL_V + k] = second
    for m in range(24):
        first, second = unpair(PAIR_VISC + m)
        rows[PL_VISC + 2 * m] = first
        rows[PL_VISC + 2 * m + 1] = second
    first, second = unpair(PAIR_SURF)
    rows[PL_STO] = first
    rows[PL_SUR] = second
    for m in range(6):
        row_x[m] = rec_b[ROW_X + m]
    for tile, (east, west) in lon_planes(state, visc, flat, rows, row_x):
        far[tile] = jnp.where(odd_lon == 1, east, west)
        near[tile] = jnp.where(odd_lon == 1, west, east)
    for tile in range(3):
        far[LON_WIDE + tile] = far_tracers[tile]
        near[LON_WIDE + tile] = near_tracers[tile]


def each(fn, *lists):
    return [fn(*items) for items in zip(*lists)]


def north_pair(q):
    sub = sub_iota()
    return [sroll(jnp.where(sub == 0, q[1], q[0]), 7), sroll(jnp.where(sub == 0, q[0], q[1]), 7)]


def south_pair(q):
    sub = sub_iota()
    return [sroll(jnp.where(sub == 7, q[1], q[0]), 1), sroll(jnp.where(sub == 7, q[0], q[1]), 1)]


def east_within(q):
    return [lroll(x, 127) for x in q]


def west_within(q):
    return [lroll(x, 1) for x in q]


def columns(load, cross_row, coefficient_at, level_count, top, counts, gain, done, keep):
    sub = sub_iota()
    zero = jnp.zeros((8, 128), F32)
    cross = jnp.logical_and(top, sub == 3)
    ghost = jnp.logical_and(top, sub < 4)
    face_east = each(jnp.minimum, level_count, east_within(level_count))
    face_west = each(jnp.minimum, level_count, west_within(level_count))
    face_north = each(jnp.minimum, level_count, north_pair(level_count))
    face_south = each(jnp.minimum, level_count, south_pair(level_count))
    sums = [
        face_east[0], jnp.where(ghost, face_west[1], face_east[1]),
        face_north[0], jnp.where(ghost, face_south[1], face_north[1]),
    ]
    for i, tile in enumerate(face_east + face_north + level_count + sums):
        counts[i] = tile

    def blend(field, chunk, i, open_east, open_north):
        q = load(field, chunk, i)
        over_east = each(lambda o, a, b: jnp.where(o, a - b, 0.0), open_east, east_within(q), q)
        over_north = each(lambda o, a, b: jnp.where(o, a - b, 0.0), open_north, north_pair(q), q)
        if field == 1:
            over_north[1] = jnp.where(cross, cross_row(chunk, i), over_north[1])
        return each(
            lambda c, a, b, d, e: c + HORIZONTAL_RATE * (a - b + d - e),
            q, over_east, west_within(over_east), over_north, south_pair(over_north),
        )

    def forward(chunk, carry):
        above, prev_gain, prev = carry
        for i in range(CHUNK):
            kf = (CHUNK * chunk + i).astype(F32)
            thick = thickness_at(kf)
            space = spacing_at(kf)
            coefficient = coefficient_at(chunk, i)
            below = [jnp.where(kf + 1.0 < counts[4 + j], coefficient[j] * space, 0.0) for j in range(2)]
            open_east = [kf < counts[j] for j in range(2)]
            open_north = [kf < counts[2 + j] for j in range(2)]
            inverse = [1.0 / (thick + above[j] + below[j] - above[j] * prev_gain[j]) for j in range(2)]
            new_gain = [below[j] * inverse[j] for j in range(2)]
            new = []
            for field in range(2):
                value = blend(field, chunk, i, open_east, open_north)
                new.append([(thick * value[j] + above[j] * prev[field][j]) * inverse[j] for j in range(2)])
            for j in range(2):
                gain[chunk, i, j] = new_gain[j]
                done[0, chunk, i, j] = new[0][j]
                done[1, chunk, i, j] = new[1][j]
            above, prev_gain, prev = below, new_gain, new
        return above, prev_gain, prev

    zeros = [zero, zero]
    lax.fori_loop(0, K // CHUNK, forward, (zeros, zeros, [zeros, zeros]))

    def backward(step, carry):
        chunk = K // CHUNK - 1 - step
        low, flux = carry
        for i in reversed(range(CHUNK)):
            k = CHUNK * chunk + i
            kf = k.astype(F32)
            thick = thickness_at(kf)
            low = [
                [done[field, chunk, i, j] + gain[chunk, i, j] * low[field][j] for j in range(2)] for field in range(2)
            ]
            flux = [
                [
                    flux[field][j] + jnp.where(kf < counts[6 + 2 * field + j], thick * low[field][j], 0.0)
                    for j in range(2)
                ]
                for field in range(2)
            ]
            for field in range(2):
                keep(field, k, low[field][0])
        return low, flux

    _, flux = lax.fori_loop(0, K // CHUNK, backward, ([zeros, zeros], [zeros, zeros]))
    return flux


def momentum_inner(state, visc, flat, rows, row_x, mixed, flux_out, gain, done, counts):
    _, top, _ = whereabouts()

    def load(field, chunk, i):
        n = 48 * field + CHUNK * chunk + i
        return [state[pl.ds(n * 8, 8), :], rows[n]]

    def coefficient_at(chunk, i):
        k = CHUNK * chunk + i
        return [visc[jnp.minimum(k, 46)], rows[PL_VISC + k]]

    def cross_row(chunk, i):
        return jnp.broadcast_to(row_x[chunk, i : i + 1, :], (8, 128))

    def keep(field, k, tile):
        mixed[48 * field + k] = tile

    flux = columns(load, cross_row, coefficient_at, [flat[0], rows[PL_WET]], top, counts, gain, done, keep)
    for field in range(2):
        for j in range(2):
            flux_out[2 * field + j] = flux[field][j]


def momentum(
    state, visc, flat, rows, row_x, flux_inner, far, near,
    mixed, moments,
    gain, done, counts, planes2, xs, sides,
):
    _, top, odd_lon = whereabouts()
    lane = lane_iota()
    sub = sub_iota()
    slot_of = lane // 4
    from_halo = jnp.logical_or(lane < 4, slot_of == 15)
    from_start = slot_of == 16
    zero = jnp.zeros((8, 128), F32)

    for tile in range(LON_WIDE):
        a, b = far[tile], near[tile]
        sides[0, tile] = jnp.where(odd_lon == 1, a, b)
        sides[1, tile] = jnp.where(odd_lon == 1, b, a)

    def strip_at(tile, j):
        return lroll(jnp.where(slot_of == j, sides[0, tile], sides[1, tile]), (128 - 4 * j) & 127)

    def strip(n):
        return strip_at(n // 32, n % 32)

    def around_edges(own, halo):
        return jnp.where(from_halo, halo, jnp.where(from_start, lroll(own, 64), own))

    def edges_at(own, chunk, first, i):
        base = first + CHUNK * chunk
        return around_edges(own, strip_at(base >> 5, (base & 31) + i))

    def spread_out(x):
        return jnp.where(lane < 64, x, lroll(x, 64))

    for m in range(6):
        xs[m] = around_edges(row_x[m], strip(m + CROSS))

    def load(field, chunk, i):
        n = 48 * field + CHUNK * chunk + i
        return [
            edges_at(state[pl.ds(n * 8, 8), :], chunk, 48 * field, i),
            edges_at(rows[n], chunk, 48 * field + HALO, i),
        ]

    def coefficient_at(chunk, i):
        k = CHUNK * chunk + i
        return [
            edges_at(visc[jnp.minimum(k, 46)], chunk, PL_VISC, i),
            edges_at(rows[PL_VISC + k], chunk, PL_VISC + HALO, i),
        ]

    def cross_row(chunk, i):
        return jnp.broadcast_to(xs[chunk, i : i + 1, :], (8, 128))

    def keep(field, k, tile):
        mixed[48 * field + k] = tile

    here = jnp.logical_or(from_halo, jnp.logical_or(from_start, lane >= 124))
    wet_edges = [
        jnp.where(here, around_edges(flat[0], strip(PL_WET)), 0.0),
        jnp.where(here, around_edges(rows[PL_WET], strip(PL_WET + HALO)), 0.0),
    ]
    edge_flux = columns(load, cross_row, coefficient_at, wet_edges, top, counts, gain, done, keep)

    def put_together(inner, edge):
        own = [
            jnp.where(lane == 127, e, jnp.where(lane == 0, lroll(e, 64), q)) for q, e in zip(inner, edge)
        ]
        return own + [spread_out(e) for e in edge]

    flux_u = put_together([flux_inner[0], flux_inner[1]], edge_flux[0])
    flux_v = put_together([flux_inner[2], flux_inner[3]], edge_flux[1])

    valid = jnp.logical_or(lane < 4, lane >= 124)

    def four(n, own):
        halo = [jnp.where(valid, spread_out(strip(m)), 0.0) for m in (n, n + HALO)]
        return [own, rows[n]] + halo

    def east(q):
        return [
            lroll(jnp.where(lane == 0, q[2], q[0]), 127),
            lroll(jnp.where(lane == 0, q[3], q[1]), 127),
            lroll(jnp.where(lane == 0, q[0], q[2]), 127),
            lroll(jnp.where(lane == 0, q[1], q[3]), 127),
        ]

    def west(q):
        return [
            lroll(jnp.where(lane == 127, q[2], q[0]), 1),
            lroll(jnp.where(lane == 127, q[3], q[1]), 1),
            lroll(jnp.where(lane == 127, q[0], q[2]), 1),
            lroll(jnp.where(lane == 127, q[1], q[3]), 1),
        ]

    def north(q):
        return north_pair(q[:2]) + north_pair(q[2:])

    def south(q):
        return south_pair(q[:2]) + south_pair(q[2:])

    level_count = four(PL_WET, flat[0])
    around = [each(jnp.minimum, level_count, shift(level_count)) for shift in (east, west, north, south)]
    for i, c in enumerate(around):
        for j in range(4):
            planes2[4 * i + j] = c[j]
    for j in range(4):
        planes2[16 + j] = level_count[j]
    ghost = jnp.logical_and(top, sub < 4)

    last = jnp.logical_and(top, sub == 7)
    first_ghost = jnp.logical_and(top, sub == 0)
    flux_v = [
        jnp.where(last, 0.0, flux_v[0]),
        jnp.where(first_ghost, 0.0, flux_v[1]),
        jnp.where(last, 0.0, flux_v[2]),
        jnp.where(first_ghost, 0.0, flux_v[3]),
    ]
    plain = each(
        lambda a, b, c, d: a - b + c - d, flux_u, west(flux_u), flux_v, south(flux_v)
    )
    mirrored = each(
        lambda a, b, c, d: a - b + c - d, east(flux_u), flux_u, north(flux_v), flux_v
    )
    divergence = [
        plain[0],
        jnp.where(ghost, mirrored[1], plain[1]),
        plain[2],
        jnp.where(ghost, mirrored[3], plain[3]),
    ]
    sto = four(PL_STO, flat[1])
    old = four(PL_SUR, flat[2])
    faces = [[FACE_SCALE * depth_of(planes2[4 * i + j]) for j in range(4)] for i in range(4)]
    diagonal = [
        jnp.maximum(sto[j] + faces[0][j] + faces[1][j] + faces[2][j] + faces[3][j], 0.1) for j in range(4)
    ]
    ocean = [planes2[16 + j] > 0.0 for j in range(4)]
    start = [jnp.where(ocean[j], old[j], 0.0) for j in range(4)]
    around = [east(start), west(start), north(start), south(start)]
    inverse = [1.0 / diagonal[j] for j in range(4)]
    basis = []
    for j in range(4):
        forcing = jnp.where(ocean[j], sto[j] * old[j] - FLUX_SCALE * divergence[j], 0.0)
        image = sto[j] * start[j]
        for i in range(4):
            image = image + faces[i][j] * (start[j] - around[i][j])
        basis.append((forcing - image) / diagonal[j])
    z0 = basis

    def spread(z):
        nb = [east(z), west(z), north(z), south(z)]
        return [
            (faces[0][j] * nb[0][j] + faces[1][j] * nb[1][j] + faces[2][j] * nb[2][j] + faces[3][j] * nb[3][j])
            * inverse[j]
            for j in range(4)
        ]

    z1 = spread(z0)
    z2 = spread(z1)
    mixed[ZED + 0] = start[0]
    mixed[ZED + 1] = z0[0]
    mixed[ZED + 2] = z1[0]
    mixed[ZED + 3] = z2[0]
    weighted = [diagonal[0] * z[0] for z in (z0, z1, z2)]
    north_weight = jnp.where(last, 1.0, 2.0)
    edge = z2[0] * (
        2.0 * faces[0][0] * east(z2)[0] + north_weight * faces[2][0] * north(z2)[0]
    )
    products = [
        weighted[0] * z0[0],
        weighted[0] * z1[0],
        weighted[1] * z1[0],
        weighted[1] * z2[0],
        weighted[2] * z2[0],
        edge,
    ]
    row = jnp.zeros((1, 128), F32)
    for i, product in enumerate(products):
        total = jnp.sum(jnp.sum(product, axis=0, keepdims=True), axis=1, keepdims=True)
        row = jnp.where(lane[:1] == i, total, row)
    moments[...] = jnp.broadcast_to(row, moments.shape)


def tracers_down(state, diff, flat, mixed, rec_b, rec_a, far, near, gain, done):
    odd, _, odd_lon = whereabouts()
    lane = lane_iota()
    sub = sub_iota()
    level_count = flat[0]
    zero = jnp.zeros((8, 128), F32)

    def forward(chunk, carry):
        above, prev_gain, prev = carry
        for i in range(CHUNK):
            k = CHUNK * chunk + i
            kf = k.astype(F32)
            thick = thickness_at(kf)
            coefficient = diff[jnp.minimum(k, 46)]
            below = jnp.where(kf + 1.0 < level_count, coefficient * spacing_at(kf), 0.0)
            inverse = 1.0 / (thick + above + below - above * prev_gain)
            new_gain = below * inverse
            gain[chunk, i] = new_gain
            open_face = [kf < mixed[AROUND + face] for face in range(4)]
            new = []
            for f in range(6):
                first = f * 48 + CHUNK * chunk
                q = state[pl.ds((first + i) * 8, 8), :]
                row_a = rec_a[f * 6 + chunk, i : i + 1, :]
                row_b = rec_b[f * 6 + chunk, i : i + 1, :]
                row_n = jnp.broadcast_to(jnp.where(odd == 1, row_b, row_a), (8, 128))
                row_s = jnp.broadcast_to(jnp.where(odd == 1, row_a, row_b), (8, 128))
                tile, j = first >> 7, (first & 127) + i
                a, b = far[LON_WIDE + tile], near[LON_WIDE + tile]
                side = lroll(jnp.where((lane == j).astype(jnp.int32) == odd_lon, a, b), (128 - j) & 127)
                change = jnp.where(open_face[0], lroll(jnp.where(lane == 0, side, q), 127) - q, 0.0)
                change += jnp.where(open_face[1], lroll(jnp.where(lane == 127, side, q), 1) - q, 0.0)
                change += jnp.where(open_face[2], sroll(jnp.where(sub == 0, row_n, q), 7) - q, 0.0)
                change += jnp.where(open_face[3], sroll(jnp.where(sub == 7, row_s, q), 1) - q, 0.0)
                value = (thick * (q + HORIZONTAL_RATE * change) + above * prev[f]) * inverse
                done[f, chunk, i] = value
                new.append(value)
            above, prev_gain, prev = below, new_gain, new
        return above, prev_gain, prev

    lax.fori_loop(0, K // CHUNK, forward, (zero, zero, [zero] * 6))


def tracers_up(gain, done, inner, mixed, after, out):
    del after
    lane = lane_iota()
    for n in range(96):
        edge = mixed[n]
        out[n] = jnp.where(lane == 127, edge, jnp.where(lane == 0, lroll(edge, 64), inner[n]))
    zero = jnp.zeros((8, 128), F32)

    def backward(step, low):
        chunk = K // CHUNK - 1 - step
        for i in reversed(range(CHUNK)):
            g = gain[chunk, i]
            low = [done[f, chunk, i] + g * low[f] for f in range(6)]
            for f in range(6):
                out[96 + f * 48 + CHUNK * chunk + i] = low[f]
        return low

    lax.fori_loop(0, K // CHUNK, backward, [zero] * 6)


def combine(parts, after, out):
    del after
    out[...] = jnp.broadcast_to(jnp.sum(parts[...], axis=0, keepdims=True), out.shape)


def finish(parts, mixed, surface):
    total = jnp.sum(parts[...], axis=0, keepdims=True)
    nu = [jnp.broadcast_to(total[:, i : i + 1], (8, 128)) for i in range(6)]

    def inner(p, q, shift):
        out = None
        for i, a in enumerate(p):
            for j, b in enumerate(q):
                term = a * b * nu[i + j + shift]
                out = term if out is None else out + term
        return out

    one = jnp.ones((8, 128), F32)
    scaled = [one]
    direction = [one]
    product = nu[0]
    move = [jnp.zeros((8, 128), F32)] * 3
    for iteration in range(ITERS):
        curvature = inner(direction, direction, 0) - inner(direction, direction, 1)
        alpha = jnp.where(curvature > 0.0, product / curvature, 0.0)
        for i, d in enumerate(direction):
            move[i] = move[i] + alpha * d
        if iteration + 1 < ITERS:
            longer = scaled + [jnp.zeros((8, 128), F32)]
            for i, d in enumerate(direction):
                longer[i] = longer[i] - alpha * d
                longer[i + 1] = longer[i + 1] + alpha * d
            scaled = longer
            following = inner(scaled, scaled, 0)
            beta = jnp.where(product > 0.0, following / product, 0.0)
            direction = [
                scaled[i] + (beta * direction[i] if i < len(direction) else 0.0) for i in range(len(scaled))
            ]
            product = following
    surface[...] = sum((move[i] * mixed[ZED + 1 + i] for i in range(3)), mixed[ZED])


VMEM_LIMIT = 24 * 1024 * 1024
FIRST_LIMIT = 60 * 1024 * 1024
VMEM = pl.BlockSpec(memory_space=pltpu.VMEM)
ANY = pl.BlockSpec(memory_space=pl.ANY)


def kernel(body, ins, outs, scratch=(), flops=0, nbytes=0, limit=VMEM_LIMIT, out_spec=VMEM):
    return pl.pallas_call(
        body,
        out_shape=[jax.ShapeDtypeStruct(s, F32) for s in outs],
        in_specs=ins,
        out_specs=[out_spec] * len(outs),
        scratch_shapes=[pltpu.VMEM(s, F32) if isinstance(s, tuple) else s for s in scratch],
        compiler_params=pltpu.CompilerParams(vmem_limit_bytes=limit),
        cost_estimate=pl.CostEstimate(flops=flops, bytes_accessed=nbytes, transcendentals=0),
    )


def lat_pairs(lat, lon):
    first, second = [], []
    for l in range(lat):
        for p in range(lon):
            here = l * lon + p
            first.append((here, (l ^ 1) * lon + p))
            if l == lat - 1:
                second.append((here, l * lon + lon - 1 - p))
            elif l % 2 == 1:
                second.append((here, here + lon))
            elif l > 0:
                second.append((here, here - lon))
    return first, second


def lon_pairs(lon):
    far, near = [], []
    for p in range(lon):
        step = 1 if p % 2 else -1
        far.append((p, (p + step) % lon))
        near.append((p, p ^ 1))
    return far, near


def make_local(mesh_shape):
    lat, lon = mesh_shape["lat"], mesh_shape["lon"]
    pairs_a, pairs_b = lat_pairs(lat, lon)
    pairs_far, pairs_near = lon_pairs(lon)
    both = ("lat", "lon")
    stages = reduction_stages(lat, lon)

    def local(ocean_state, viscosity, diffusivity, wet_levels, storage, surface_old):
        state = ocean_state.reshape(8 * K * 8, 128)
        pay_b, pay_a, uv, visc, flat = kernel(
            pack_lat,
            [ANY] * 5,
            [(LAT_TILES, 8, 128), (ROW_X, 8, 128), (96 * 8, 128), (47, 8, 128), (3, 8, 128)],
            scratch=[
                (LAT_TILES, 8, 128), (ROW_X, 8, 128),
                (96 * 8, 128), (47, 8, 128), (3, 8, 128),
                pltpu.VMEM((8, 128), jnp.int32), pltpu.SemaphoreType.DMA((6,)), pltpu.SemaphoreType.DMA((7,)),
            ],
            out_spec=ANY,
            limit=FIRST_LIMIT,
        )(state, viscosity, wet_levels, storage, surface_old)
        own = (uv, visc, flat)
        rec_b = lax.ppermute(pay_b, both, pairs_b)
        rec_a = lax.ppermute(pay_a, both, pairs_a)
        row_b, row_a, far_tracers, near_tracers, tracer = kernel(
            pack_tracers,
            [ANY],
            [(ROW_TILES, 8, 128)] * 2 + [(3, 8, 128)] * 2 + [(288 * 8, 128)],
            scratch=[pltpu.SemaphoreType.DMA((2,))],
            flops=1_000_000,
            nbytes=2_000_000,
        )(state)
        rec_row_b = lax.ppermute(row_b, both, pairs_b)
        rec_row_a = lax.ppermute(row_a, both, pairs_a)
        rows, row_x, pay_far, pay_near = kernel(
            pack_lon,
            [VMEM] * 7,
            [(PLANES, 8, 128), (6, 8, 128), (LON_TILES, 8, 128), (LON_TILES, 8, 128)],
        )(*own, rec_b, rec_a, far_tracers, near_tracers)
        rec_far = lax.ppermute(pay_far, "lon", pairs_far)
        rec_near = lax.ppermute(pay_near, "lon", pairs_near)
        chunked = (K // CHUNK, CHUNK)
        scratch = [(*chunked, 2, 8, 128), (2, *chunked, 2, 8, 128), (10, 8, 128)]
        inner, flux_inner = kernel(
            momentum_inner,
            [VMEM] * 5,
            [(2 * K, 8, 128), (4, 8, 128)],
            scratch=scratch,
            flops=10_000_000,
            nbytes=6_000_000,
        )(*own, rows, row_x)
        mixed, moments = kernel(
            momentum_entry,
            [VMEM] * 8 + [ANY] * 2,
            [(2 * K + 8, 8, 128), (stages[0][1], 128)],
            scratch=scratch + [(20, 8, 128), (6, 8, 128), (2, LON_WIDE, 8, 128)],
        )(*own, rows, row_x, flux_inner, rec_far, rec_near, rec_row_b, rec_row_a)
        (first_groups, _), (second_groups, second_size) = stages
        parts = lax.all_to_all(moments, both, 0, 0, axis_index_groups=first_groups, tiled=True)
        gain, done = kernel(
            tracers_down,
            [VMEM] * 8,
            [(*chunked, 8, 128), (6, *chunked, 8, 128)],
            flops=10_000_000,
            nbytes=6_000_000,
        )(tracer, diffusivity, flat, mixed, rec_row_b, rec_row_a, rec_far, rec_near)
        (parts,) = kernel(combine, [VMEM, ANY], [(second_size, 128)])(parts, gain)
        sent = parts
        parts = lax.all_to_all(parts, both, 0, 0, axis_index_groups=second_groups, tiled=True)
        (state_out,) = kernel(
            tracers_up, [VMEM] * 4 + [ANY], [(8 * K, 8, 128)], flops=10_000_000, nbytes=6_000_000
        )(gain, done, inner, mixed, sent)
        (surface,) = kernel(finish, [VMEM] * 2, [(8, 128)])(parts, mixed)
        return state_out.reshape(8, K, 8, 128), surface

    return local


def momentum_entry(*refs):
    inputs, outputs, scratch = refs[:8], refs[10:12], refs[12:]
    mixed, moments = outputs
    momentum(*inputs, mixed, moments, *scratch)
    planes2 = scratch[3]
    for face in range(4):
        mixed[AROUND + face] = planes2[4 * face]


def reduction_stages(lat, lon):
    index = np.arange(lat * lon)
    if lat == 32 and lon == 16:
        grid = index.reshape(8, 4, 4, 2, 2)
        along_z = grid.transpose(1, 2, 4, 3, 0).reshape(32, 16)
        rest = grid.transpose(0, 3, 1, 2, 4).reshape(16, 32)
    else:
        grid = index.reshape(lat, lon)
        along_z, rest = grid.T, grid
    return [(g.tolist(), g.shape[1]) for g in (rest, along_z)]


def solution(mesh):
    placed = (
        P(None, None, "lat", "lon"),
        P(None, "lat", "lon"),
        P(None, "lat", "lon"),
        P("lat", "lon"),
        P("lat", "lon"),
        P("lat", "lon"),
    )
    return jax.shard_map(
        make_local(dict(mesh.shape)),
        mesh=mesh,
        in_specs=placed,
        out_specs=(P(None, None, "lat", "lon"), P("lat", "lon")),
        check_vma=False,
    )
```

```python
import functools

import jax
import jax.numpy as jnp
import numpy as np
from jax import lax
from jax.experimental import pallas as pl
from jax.experimental.pallas import tpu as pltpu
from jax.sharding import PartitionSpec as P

ITERS = 3
K = 48
HORIZONTAL_RATE = 0.2
FLUX_SCALE = 0.02
FACE_SCALE = 0.25
F32 = jnp.float32

PAIR_UV = 0
PAIR_VISC = 48
PAIR_SURF = 72
ROW_X = 73
LAT_TILES = 79
ROW_TILES = 36
PL_U, PL_V, PL_VISC, PL_WET, PL_STO, PL_SUR = 0, 48, 96, 143, 144, 145
PLANES = 146
HALO, CROSS = 152, 298
GROUPS = 38
LON_WIDE = 10
LON_TILES = LON_WIDE + 3
CHUNK = 8
ZED, AROUND = 96, 100


def whereabouts():
    band = lax.axis_index("lat")
    return lax.rem(band, 2), band == lax.axis_size("lat") - 1, lax.rem(lax.axis_index("lon"), 2)


def sub_iota():
    return lax.broadcasted_iota(jnp.int32, (8, 128), 0)


def lane_iota():
    return lax.broadcasted_iota(jnp.int32, (8, 128), 1)


def lroll(x, shift):
    return pltpu.roll(x, shift, 1)


def sroll(x, shift):
    return pltpu.roll(x, shift, 0)


def flip_lanes(x):
    return jnp.take_along_axis(x, 127 - lane_iota(), axis=1)


def flip_rows(x):
    sub = sub_iota()
    x = sroll(x, 4)
    x = jnp.where((sub & 2) == 0, sroll(x, 6), sroll(x, 2))
    return jnp.where((sub & 1) == 0, sroll(x, 7), sroll(x, 1))


def thickness_at(level):
    return 0.5 + level * (1.0 / 48.0)


def spacing_at(level):
    return 96.0 / jnp.full((8, 128), 49.0 + 2.0 * level, F32)


def depth_of(count):
    return 0.5 * count + count * (count - 1.0) * (1.0 / 96.0)


def pack_lat(
    state_any, visc_any, wet_any, storage_any, surf_any,
    out_b, out_a, out_state, out_visc, out_flat,
    pay_b, pay_a, state, visc, flat, wet, sems, out_sems,
):
    odd, top, _ = whereabouts()
    half = 48 * 8
    copies = [
        pltpu.make_async_copy(state_any.at[pl.ds(0, half)], state.at[pl.ds(0, half)], sems.at[0]),
        pltpu.make_async_copy(state_any.at[pl.ds(half, half)], state.at[pl.ds(half, half)], sems.at[1]),
        pltpu.make_async_copy(visc_any, visc, sems.at[2]),
        pltpu.make_async_copy(wet_any, wet, sems.at[3]),
        pltpu.make_async_copy(storage_any, flat.at[1], sems.at[4]),
        pltpu.make_async_copy(surf_any, flat.at[2], sems.at[5]),
    ]
    for copy in copies:
        copy.start()
    sub = sub_iota()
    keep = (sub < 4).astype(jnp.int32) == odd

    def pack(tiles):
        @pl.when(jnp.logical_not(top))
        def _():
            for tile, first, second, _ in tiles():
                rolled = sroll(second, 4)
                pay_a[tile] = jnp.where(keep, first, rolled)
                pay_b[tile] = jnp.where(keep, rolled, first)

        @pl.when(top)
        def _():
            for tile, first, second, sign in tiles():
                rolled = sroll(second, 4)
                pay_a[tile] = jnp.where(keep, first, rolled)
                turned = flip_rows(flip_lanes(jnp.where(keep, rolled, first)))
                pay_b[tile] = -turned if sign < 0 else turned

    def velocities():
        for k in range(48):
            yield k, state[k * 8 : k * 8 + 8, :], state[(k + 48) * 8 : (k + 48) * 8 + 8, :], -1.0

    def others():
        for m in range(23):
            yield PAIR_VISC + m, visc[2 * m], visc[2 * m + 1], 1.0
        yield PAIR_VISC + 23, visc[46], flat[0], 1.0
        yield PAIR_SURF, flat[1], flat[2], 1.0

    def send(source, target, sem):
        copy = pltpu.make_async_copy(source, target, out_sems.at[sem])
        copy.start()
        return copy

    copies[0].wait()
    copies[1].wait()
    leaving = [send(state, out_state, 0)]
    pack(velocities)
    first = pl.ds(0, PAIR_VISC)
    leaving += [send(pay_b.at[first], out_b.at[first], 1), send(pay_a.at[first], out_a.at[first], 2)]
    for copy in copies[2:]:
        copy.wait()
    flat[0] = wet[...].astype(F32)
    leaving += [send(visc, out_visc, 3), send(flat, out_flat, 4)]
    pack(others)
    least = jnp.broadcast_to(jnp.minimum(flat[0, 3:4, :], flat[0, 4:5, :]), (8, 128))
    for m in range(6):
        start = (48 + 8 * m) * 8
        row3 = state[pl.ds(start + 3, 8, stride=8), :]
        row4 = state[pl.ds(start + 4, 8, stride=8), :]
        level = (sub + 8 * m).astype(F32)
        diff = jnp.where(level < least, row3 - row4, 0.0)
        pay_b[ROW_X + m] = -flip_lanes(diff)
    rest_b, rest_a = (pl.ds(PAIR_VISC, count - PAIR_VISC) for count in (LAT_TILES, ROW_X))
    leaving += [send(pay_b.at[rest_b], out_b.at[rest_b], 5), send(pay_a.at[rest_a], out_a.at[rest_a], 6)]
    for copy in leaving:
        copy.wait()


def pack_tracers(state_any, pay_b, pay_a, far, near, tracer, sems):
    half = 144 * 8
    copies = [
        pltpu.make_async_copy(
            state_any.at[pl.ds((96 + 144 * i) * 8, half)], tracer.at[pl.ds(i * half, half)], sems.at[i]
        )
        for i in range(2)
    ]
    for copy in copies:
        copy.start()
    for copy in copies:
        copy.wait()
    odd, top, odd_lon = whereabouts()
    lane = lane_iota()

    def rows_of(t):
        start = 8 * t * 8
        return tracer[pl.ds(start, 8, stride=8), :], tracer[pl.ds(start + 7, 8, stride=8), :]

    for t in range(ROW_TILES):
        row0, row7 = rows_of(t)
        pay_a[t] = jnp.where(odd == 1, row0, row7)
        pay_b[t] = jnp.where(odd == 1, row7, row0)

    @pl.when(top)
    def _():
        for t in range(ROW_TILES):
            pay_b[t] = flip_lanes(rows_of(t)[1])

    def scalar(n):
        return tracer[n * 8 : n * 8 + 8, :]

    for tile in range(3):
        planes = [functools.partial(scalar, n) for n in range(128 * tile, min(128 * tile + 128, 288))]
        east, west = pack_columns(lane, planes, 1)
        far[tile] = jnp.where(odd_lon == 1, east, west)
        near[tile] = jnp.where(odd_lon == 1, west, east)


def pack_columns(lane, planes, width):
    east = jnp.zeros((8, 128), F32)
    west = jnp.zeros((8, 128), F32)
    slots = 128 // width
    slot_of = lane // width
    for j, load in enumerate(planes):
        if load is None:
            continue
        x = load()
        x = lroll(x, j * width) if j else x
        west = jnp.where(slot_of == j, x, west)
        east = jnp.where(slot_of == (j - 1) % slots, x, east)
    return east, west


def lon_planes(state, visc, flat, rows, row_x):
    def plane(n):
        if n < 96:
            return state[n * 8 : n * 8 + 8, :]
        if n < 143:
            return visc[n - 96]
        if n < 146:
            return flat[n - 143]
        if n < HALO:
            return flat[0]
        if n < CROSS:
            return rows[n - HALO]
        return row_x[n - CROSS]

    lane = lane_iota()
    for tile in range(LON_WIDE):
        order = [32 * tile + 8 * (j % 4) + j // 4 for j in range(32)]
        planes = [functools.partial(plane, n) if n < CROSS + 6 else None for n in order]
        yield tile, pack_columns(lane, planes, 4)


def pack_lon(
    state, visc, flat, rec_b, rec_a, far_tracers, near_tracers, rows, row_x, far, near
):
    odd, _, odd_lon = whereabouts()
    sub = sub_iota()
    keep = (sub < 4).astype(jnp.int32) != odd

    def unpair(tile):
        a, b = rec_a[tile], rec_b[tile]
        return jnp.where(keep, a, b), sroll(jnp.where(keep, b, a), 4)

    for k in range(48):
        first, second = unpair(k)
        rows[PL_U + k] = first
        rows[PL_V + k] = second
    for m in range(24):
        first, second = unpair(PAIR_VISC + m)
        rows[PL_VISC + 2 * m] = first
        rows[PL_VISC + 2 * m + 1] = second
    first, second = unpair(PAIR_SURF)
    rows[PL_STO] = first
    rows[PL_SUR] = second
    for m in range(6):
        row_x[m] = rec_b[ROW_X + m]
    for tile, (east, west) in lon_planes(state, visc, flat, rows, row_x):
        far[tile] = jnp.where(odd_lon == 1, east, west)
        near[tile] = jnp.where(odd_lon == 1, west, east)
    for tile in range(3):
        far[LON_WIDE + tile] = far_tracers[tile]
        near[LON_WIDE + tile] = near_tracers[tile]


def each(fn, *lists):
    return [fn(*items) for items in zip(*lists)]


def north_pair(q):
    sub = sub_iota()
    return [sroll(jnp.where(sub == 0, q[1], q[0]), 7), sroll(jnp.where(sub == 0, q[0], q[1]), 7)]


def south_pair(q):
    sub = sub_iota()
    return [sroll(jnp.where(sub == 7, q[1], q[0]), 1), sroll(jnp.where(sub == 7, q[0], q[1]), 1)]


def east_within(q):
    return [lroll(x, 127) for x in q]


def west_within(q):
    return [lroll(x, 1) for x in q]


def columns(load, cross_row, coefficient_at, level_count, top, counts, gain, done, keep):
    sub = sub_iota()
    zero = jnp.zeros((8, 128), F32)
    cross = jnp.logical_and(top, sub == 3)
    ghost = jnp.logical_and(top, sub < 4)
    face_east = each(jnp.minimum, level_count, east_within(level_count))
    face_west = each(jnp.minimum, level_count, west_within(level_count))
    face_north = each(jnp.minimum, level_count, north_pair(level_count))
    face_south = each(jnp.minimum, level_count, south_pair(level_count))
    sums = [
        face_east[0], jnp.where(ghost, face_west[1], face_east[1]),
        face_north[0], jnp.where(ghost, face_south[1], face_north[1]),
    ]
    for i, tile in enumerate(face_east + face_north + level_count + sums):
        counts[i] = tile

    def blend(field, chunk, i, open_east, open_north):
        q = load(field, chunk, i)
        over_east = each(lambda o, a, b: jnp.where(o, a - b, 0.0), open_east, east_within(q), q)
        over_north = each(lambda o, a, b: jnp.where(o, a - b, 0.0), open_north, north_pair(q), q)
        if field == 1:
            over_north[1] = jnp.where(cross, cross_row(chunk, i), over_north[1])
        return each(
            lambda c, a, b, d, e: c + HORIZONTAL_RATE * (a - b + d - e),
            q, over_east, west_within(over_east), over_north, south_pair(over_north),
        )

    def forward(chunk, carry):
        above, prev_gain, prev = carry
        for i in range(CHUNK):
            kf = (CHUNK * chunk + i).astype(F32)
            thick = thickness_at(kf)
            space = spacing_at(kf)
            coefficient = coefficient_at(chunk, i)
            below = [jnp.where(kf + 1.0 < counts[4 + j], coefficient[j] * space, 0.0) for j in range(2)]
            open_east = [kf < counts[j] for j in range(2)]
            open_north = [kf < counts[2 + j] for j in range(2)]
            inverse = [1.0 / (thick + above[j] + below[j] - above[j] * prev_gain[j]) for j in range(2)]
            new_gain = [below[j] * inverse[j] for j in range(2)]
            new = []
            for field in range(2):
                value = blend(field, chunk, i, open_east, open_north)
                new.append([(thick * value[j] + above[j] * prev[field][j]) * inverse[j] for j in range(2)])
            for j in range(2):
                gain[chunk, i, j] = new_gain[j]
                done[0, chunk, i, j] = new[0][j]
                done[1, chunk, i, j] = new[1][j]
            above, prev_gain, prev = below, new_gain, new
        return above, prev_gain, prev

    zeros = [zero, zero]
    lax.fori_loop(0, K // CHUNK, forward, (zeros, zeros, [zeros, zeros]))

    def backward(step, carry):
        chunk = K // CHUNK - 1 - step
        low, flux = carry
        for i in reversed(range(CHUNK)):
            k = CHUNK * chunk + i
            kf = k.astype(F32)
            thick = thickness_at(kf)
            low = [
                [done[field, chunk, i, j] + gain[chunk, i, j] * low[field][j] for j in range(2)] for field in range(2)
            ]
            flux = [
                [
                    flux[field][j] + jnp.where(kf < counts[6 + 2 * field + j], thick * low[field][j], 0.0)
                    for j in range(2)
                ]
                for field in range(2)
            ]
            for field in range(2):
                keep(field, k, low[field][0])
        return low, flux

    _, flux = lax.fori_loop(0, K // CHUNK, backward, ([zeros, zeros], [zeros, zeros]))
    return flux


def momentum_inner(state, visc, flat, rows, row_x, mixed, flux_out, gain, done, counts):
    _, top, _ = whereabouts()

    def load(field, chunk, i):
        n = 48 * field + CHUNK * chunk + i
        return [state[pl.ds(n * 8, 8), :], rows[n]]

    def coefficient_at(chunk, i):
        k = CHUNK * chunk + i
        return [visc[jnp.minimum(k, 46)], rows[PL_VISC + k]]

    def cross_row(chunk, i):
        return jnp.broadcast_to(row_x[chunk, i : i + 1, :], (8, 128))

    def keep(field, k, tile):
        mixed[48 * field + k] = tile

    flux = columns(load, cross_row, coefficient_at, [flat[0], rows[PL_WET]], top, counts, gain, done, keep)
    for field in range(2):
        for j in range(2):
            flux_out[2 * field + j] = flux[field][j]


def to_last(x):
    return lroll(x, 124)


def to_first(x):
    return lroll(x, 116)


def momentum(
    flat, rows, flux_inner, pay_far, pay_near, far, near,
    mixed, moments,
    windows, below_all, scaled_all, gain, done, planes2,
):
    _, top, odd_lon = whereabouts()
    lane = lane_iota()
    sub = sub_iota()
    zero = jnp.zeros((8, 128), F32)
    ghost = jnp.logical_and(top, sub < 4)

    for tile in range(LON_WIDE):
        sent = [pay_far[tile], pay_near[tile]]
        came = [far[tile], near[tile]]
        own_east, own_west = (jnp.where(odd_lon == 1, *pair) for pair in (sent, sent[::-1]))
        halo_east, halo_west = (jnp.where(odd_lon == 1, *pair) for pair in (came, came[::-1]))
        for g in range(min(4, GROUPS - 4 * tile)):
            here = ((lane - 4 * g) & 15) < 4
            first = lroll(jnp.where(here, halo_east, own_east), (4 - 4 * g) & 127)
            second = lroll(jnp.where(here, own_west, halo_west), (12 - 4 * g) & 127)
            windows[4 * tile + g] = jnp.where((lane & 15) < 8, first, second)

    def window(n):
        shift = (128 - 16 * (n % 8)) & 127
        return lroll(windows[n // 8], shift) if shift else windows[n // 8]

    def everywhere(x):
        x = jnp.where(lane < 16, x, 0.0)
        for step in (16, 32, 64):
            x = x + lroll(x, step)
        return x

    wet_window = [everywhere(window(PL_WET)), everywhere(window(PL_WET + HALO))]
    face_east = each(jnp.minimum, wet_window, east_within(wet_window))
    face_west = each(jnp.minimum, wet_window, west_within(wet_window))
    face_north = each(jnp.minimum, wet_window, north_pair(wet_window))
    face_south = each(jnp.minimum, wet_window, south_pair(wet_window))
    sum_u = [face_east[0], jnp.where(ghost, face_west[1], face_east[1])]
    sum_v = [face_north[0], jnp.where(ghost, face_south[1], face_north[1])]
    cross = jnp.logical_and(top, sub == 3)
    part = lane // 16

    for chunk in range(K // CHUNK):
        level = (part + CHUNK * chunk).astype(F32)
        thick = thickness_at(level)
        space = 96.0 / (49.0 + 2.0 * level)
        open_east = [level < c for c in face_east]
        open_north = [level < c for c in face_north]
        group = PL_VISC // CHUNK + chunk
        for j, shift in enumerate((0, HALO // CHUNK)):
            below_all[chunk, j] = jnp.where(level + 1.0 < wet_window[j], windows[group + shift] * space, 0.0)
        for field in range(2):
            group = K // CHUNK * field + chunk
            q = [windows[group], windows[group + HALO // CHUNK]]
            over_east = each(lambda o, a, b: jnp.where(o, a - b, 0.0), open_east, east_within(q), q)
            over_north = each(lambda o, a, b: jnp.where(o, a - b, 0.0), open_north, north_pair(q), q)
            if field == 1:
                levels = jnp.where(part == sub, everywhere(window(CROSS + chunk)), 0.0)
                extra = jnp.broadcast_to(jnp.sum(levels, axis=0, keepdims=True), (8, 128))
                over_north[1] = jnp.where(cross, extra, over_north[1])
            blended = each(
                lambda c, a, b, d, e: c + HORIZONTAL_RATE * (a - b + d - e),
                q, over_east, west_within(over_east), over_north, south_pair(over_north),
            )
            for j in range(2):
                scaled_all[field, chunk, j] = thick * blended[j]

    def at_level(tile, k):
        shift = (128 - 16 * (k % CHUNK)) & 127
        return lroll(tile, shift) if shift else tile

    above = prev_gain = [zero, zero]
    prev = [[zero, zero], [zero, zero]]
    for k in range(K):
        thick = 0.5 + k / 48.0
        below = [at_level(below_all[k // CHUNK, j], k) for j in range(2)]
        inverse = [1.0 / (thick + above[j] + below[j] - above[j] * prev_gain[j]) for j in range(2)]
        prev_gain = [below[j] * inverse[j] for j in range(2)]
        prev = [
            [
                (at_level(scaled_all[field, k // CHUNK, j], k) + above[j] * prev[field][j]) * inverse[j]
                for j in range(2)
            ]
            for field in range(2)
        ]
        for j in range(2):
            gain[k, j] = prev_gain[j]
            for field in range(2):
                done[field, k, j] = prev[field][j]
        above = below
    low = flux = [[zero, zero], [zero, zero]]
    for k in reversed(range(K)):
        thick = 0.5 + k / 48.0
        low = [[done[field, k, j] + gain[k, j] * low[field][j] for j in range(2)] for field in range(2)]
        flux = [
            [flux[field][j] + jnp.where(k < counts[j], thick * low[field][j], 0.0) for j in range(2)]
            for field, counts in enumerate((sum_u, sum_v))
        ]
        for field in range(2):
            mixed[48 * field + k] = low[field][0]

    def put_together(inner, edge):
        own = [
            jnp.where(lane == 127, to_last(e), jnp.where(lane == 0, to_first(e), q)) for q, e in zip(inner, edge)
        ]
        return own + [jnp.where(lane < 64, to_last(e), to_first(e)) for e in edge]

    flux_u = put_together([flux_inner[0], flux_inner[1]], flux[0])
    flux_v = put_together([flux_inner[2], flux_inner[3]], flux[1])

    valid = jnp.logical_or(lane < 4, lane >= 124)

    def four(n, own):
        pair = [window(n), window(n + HALO)]
        return [own, rows[n]] + [
            jnp.where(valid, jnp.where(lane < 64, to_last(e), to_first(e)), 0.0) for e in pair
        ]

    def east(q):
        return [
            lroll(jnp.where(lane == 0, q[2], q[0]), 127),
            lroll(jnp.where(lane == 0, q[3], q[1]), 127),
            lroll(jnp.where(lane == 0, q[0], q[2]), 127),
            lroll(jnp.where(lane == 0, q[1], q[3]), 127),
        ]

    def west(q):
        return [
            lroll(jnp.where(lane == 127, q[2], q[0]), 1),
            lroll(jnp.where(lane == 127, q[3], q[1]), 1),
            lroll(jnp.where(lane == 127, q[0], q[2]), 1),
            lroll(jnp.where(lane == 127, q[1], q[3]), 1),
        ]

    def north(q):
        return north_pair(q[:2]) + north_pair(q[2:])

    def south(q):
        return south_pair(q[:2]) + south_pair(q[2:])

    level_count = four(PL_WET, flat[0])
    around = [each(jnp.minimum, level_count, shift(level_count)) for shift in (east, west, north, south)]
    for i, c in enumerate(around):
        for j in range(4):
            planes2[4 * i + j] = c[j]
    for j in range(4):
        planes2[16 + j] = level_count[j]
    last = jnp.logical_and(top, sub == 7)
    first_ghost = jnp.logical_and(top, sub == 0)
    flux_v = [
        jnp.where(last, 0.0, flux_v[0]),
        jnp.where(first_ghost, 0.0, flux_v[1]),
        jnp.where(last, 0.0, flux_v[2]),
        jnp.where(first_ghost, 0.0, flux_v[3]),
    ]
    plain = each(
        lambda a, b, c, d: a - b + c - d, flux_u, west(flux_u), flux_v, south(flux_v)
    )
    mirrored = each(
        lambda a, b, c, d: a - b + c - d, east(flux_u), flux_u, north(flux_v), flux_v
    )
    divergence = [
        plain[0],
        jnp.where(ghost, mirrored[1], plain[1]),
        plain[2],
        jnp.where(ghost, mirrored[3], plain[3]),
    ]
    sto = four(PL_STO, flat[1])
    old = four(PL_SUR, flat[2])
    faces = [[FACE_SCALE * depth_of(planes2[4 * i + j]) for j in range(4)] for i in range(4)]
    diagonal = [
        jnp.maximum(sto[j] + faces[0][j] + faces[1][j] + faces[2][j] + faces[3][j], 0.1) for j in range(4)
    ]
    ocean = [planes2[16 + j] > 0.0 for j in range(4)]
    start = [jnp.where(ocean[j], old[j], 0.0) for j in range(4)]
    around = [east(start), west(start), north(start), south(start)]
    inverse = [1.0 / diagonal[j] for j in range(4)]
    basis = []
    for j in range(4):
        forcing = jnp.where(ocean[j], sto[j] * old[j] - FLUX_SCALE * divergence[j], 0.0)
        image = sto[j] * start[j]
        for i in range(4):
            image = image + faces[i][j] * (start[j] - around[i][j])
        basis.append((forcing - image) / diagonal[j])
    z0 = basis

    def spread(z):
        nb = [east(z), west(z), north(z), south(z)]
        return [
            (faces[0][j] * nb[0][j] + faces[1][j] * nb[1][j] + faces[2][j] * nb[2][j] + faces[3][j] * nb[3][j])
            * inverse[j]
            for j in range(4)
        ]

    z1 = spread(z0)
    z2 = spread(z1)
    mixed[ZED + 0] = start[0]
    mixed[ZED + 1] = z0[0]
    mixed[ZED + 2] = z1[0]
    mixed[ZED + 3] = z2[0]
    weighted = [diagonal[0] * z[0] for z in (z0, z1, z2)]
    north_weight = jnp.where(last, 1.0, 2.0)
    edge = z2[0] * (
        2.0 * faces[0][0] * east(z2)[0] + north_weight * faces[2][0] * north(z2)[0]
    )
    products = [
        weighted[0] * z0[0],
        weighted[0] * z1[0],
        weighted[1] * z1[0],
        weighted[1] * z2[0],
        weighted[2] * z2[0],
        edge,
    ]
    row = jnp.zeros((1, 128), F32)
    for i, product in enumerate(products):
        total = jnp.sum(jnp.sum(product, axis=0, keepdims=True), axis=1, keepdims=True)
        row = jnp.where(lane[:1] == i, total, row)
    moments[...] = jnp.broadcast_to(row, moments.shape)


def tracers_down(state, diff, flat, mixed, rec_b, rec_a, far, near, after, gain, done):
    del after
    odd, _, odd_lon = whereabouts()
    lane = lane_iota()
    sub = sub_iota()
    level_count = flat[0]
    zero = jnp.zeros((8, 128), F32)

    def forward(chunk, carry):
        above, prev_gain, prev = carry
        for i in range(CHUNK):
            k = CHUNK * chunk + i
            kf = k.astype(F32)
            thick = thickness_at(kf)
            coefficient = diff[jnp.minimum(k, 46)]
            below = jnp.where(kf + 1.0 < level_count, coefficient * spacing_at(kf), 0.0)
            inverse = 1.0 / (thick + above + below - above * prev_gain)
            new_gain = below * inverse
            gain[chunk, i] = new_gain
            open_face = [kf < mixed[AROUND + face] for face in range(4)]
            new = []
            for f in range(6):
                first = f * 48 + CHUNK * chunk
                q = state[pl.ds((first + i) * 8, 8), :]
                row_a = rec_a[f * 6 + chunk, i : i + 1, :]
                row_b = rec_b[f * 6 + chunk, i : i + 1, :]
                row_n = jnp.broadcast_to(jnp.where(odd == 1, row_b, row_a), (8, 128))
                row_s = jnp.broadcast_to(jnp.where(odd == 1, row_a, row_b), (8, 128))
                tile, j = first >> 7, (first & 127) + i
                a, b = far[LON_WIDE + tile], near[LON_WIDE + tile]
                side = lroll(jnp.where((lane == j).astype(jnp.int32) == odd_lon, a, b), (128 - j) & 127)
                change = jnp.where(open_face[0], lroll(jnp.where(lane == 0, side, q), 127) - q, 0.0)
                change += jnp.where(open_face[1], lroll(jnp.where(lane == 127, side, q), 1) - q, 0.0)
                change += jnp.where(open_face[2], sroll(jnp.where(sub == 0, row_n, q), 7) - q, 0.0)
                change += jnp.where(open_face[3], sroll(jnp.where(sub == 7, row_s, q), 1) - q, 0.0)
                value = (thick * (q + HORIZONTAL_RATE * change) + above * prev[f]) * inverse
                done[f, chunk, i] = value
                new.append(value)
            above, prev_gain, prev = below, new_gain, new
        return above, prev_gain, prev

    lax.fori_loop(0, K // CHUNK, forward, (zero, zero, [zero] * 6))


def tracers_up(gain, done, inner, mixed, out):
    lane = lane_iota()
    for n in range(96):
        edge = mixed[n]
        out[n] = jnp.where(lane == 127, to_last(edge), jnp.where(lane == 0, to_first(edge), inner[n]))
    zero = jnp.zeros((8, 128), F32)

    def backward(step, low):
        chunk = K // CHUNK - 1 - step
        for i in reversed(range(CHUNK)):
            g = gain[chunk, i]
            low = [done[f, chunk, i] + g * low[f] for f in range(6)]
            for f in range(6):
                out[96 + f * 48 + CHUNK * chunk + i] = low[f]
        return low

    lax.fori_loop(0, K // CHUNK, backward, [zero] * 6)


def combine(parts, out):
    out[...] = jnp.broadcast_to(jnp.sum(parts[...], axis=0, keepdims=True), out.shape)


def finish(parts, mixed, surface):
    total = jnp.sum(parts[...], axis=0, keepdims=True)
    nu = [jnp.broadcast_to(total[:, i : i + 1], (8, 128)) for i in range(6)]

    def inner(p, q, shift):
        out = None
        for i, a in enumerate(p):
            for j, b in enumerate(q):
                term = a * b * nu[i + j + shift]
                out = term if out is None else out + term
        return out

    one = jnp.ones((8, 128), F32)
    scaled = [one]
    direction = [one]
    product = nu[0]
    move = [jnp.zeros((8, 128), F32)] * 3
    for iteration in range(ITERS):
        curvature = inner(direction, direction, 0) - inner(direction, direction, 1)
        alpha = jnp.where(curvature > 0.0, product / curvature, 0.0)
        for i, d in enumerate(direction):
            move[i] = move[i] + alpha * d
        if iteration + 1 < ITERS:
            longer = scaled + [jnp.zeros((8, 128), F32)]
            for i, d in enumerate(direction):
                longer[i] = longer[i] - alpha * d
                longer[i + 1] = longer[i + 1] + alpha * d
            scaled = longer
            following = inner(scaled, scaled, 0)
            beta = jnp.where(product > 0.0, following / product, 0.0)
            direction = [
                scaled[i] + (beta * direction[i] if i < len(direction) else 0.0) for i in range(len(scaled))
            ]
            product = following
    surface[...] = sum((move[i] * mixed[ZED + 1 + i] for i in range(3)), mixed[ZED])


VMEM_LIMIT = 24 * 1024 * 1024
FIRST_LIMIT = 60 * 1024 * 1024
VMEM = pl.BlockSpec(memory_space=pltpu.VMEM)
ANY = pl.BlockSpec(memory_space=pl.ANY)


def kernel(body, ins, outs, scratch=(), flops=0, nbytes=0, limit=VMEM_LIMIT, out_spec=VMEM):
    return pl.pallas_call(
        body,
        out_shape=[jax.ShapeDtypeStruct(s, F32) for s in outs],
        in_specs=ins,
        out_specs=[out_spec] * len(outs),
        scratch_shapes=[pltpu.VMEM(s, F32) if isinstance(s, tuple) else s for s in scratch],
        compiler_params=pltpu.CompilerParams(vmem_limit_bytes=limit),
        cost_estimate=pl.CostEstimate(flops=flops, bytes_accessed=nbytes, transcendentals=0),
    )


def lat_pairs(lat, lon):
    first, second = [], []
    for l in range(lat):
        for p in range(lon):
            here = l * lon + p
            first.append((here, (l ^ 1) * lon + p))
            if l == lat - 1:
                second.append((here, l * lon + lon - 1 - p))
            elif l % 2 == 1:
                second.append((here, here + lon))
            elif l > 0:
                second.append((here, here - lon))
    return first, second


def lon_pairs(lon):
    far, near = [], []
    for p in range(lon):
        step = 1 if p % 2 else -1
        far.append((p, (p + step) % lon))
        near.append((p, p ^ 1))
    return far, near


def make_local(mesh_shape):
    lat, lon = mesh_shape["lat"], mesh_shape["lon"]
    pairs_a, pairs_b = lat_pairs(lat, lon)
    pairs_far, pairs_near = lon_pairs(lon)
    both = ("lat", "lon")
    stages = reduction_stages(lat, lon)

    def local(ocean_state, viscosity, diffusivity, wet_levels, storage, surface_old):
        state = ocean_state.reshape(8 * K * 8, 128)
        pay_b, pay_a, uv, visc, flat = kernel(
            pack_lat,
            [ANY] * 5,
            [(LAT_TILES, 8, 128), (ROW_X, 8, 128), (96 * 8, 128), (47, 8, 128), (3, 8, 128)],
            scratch=[
                (LAT_TILES, 8, 128), (ROW_X, 8, 128),
                (96 * 8, 128), (47, 8, 128), (3, 8, 128),
                pltpu.VMEM((8, 128), jnp.int32), pltpu.SemaphoreType.DMA((6,)), pltpu.SemaphoreType.DMA((7,)),
            ],
            out_spec=ANY,
            limit=FIRST_LIMIT,
        )(state, viscosity, wet_levels, storage, surface_old)
        own = (uv, visc, flat)
        rec_b = lax.ppermute(pay_b, both, pairs_b)
        rec_a = lax.ppermute(pay_a, both, pairs_a)
        row_b, row_a, far_tracers, near_tracers, tracer = kernel(
            pack_tracers,
            [ANY],
            [(ROW_TILES, 8, 128)] * 2 + [(3, 8, 128)] * 2 + [(288 * 8, 128)],
            scratch=[pltpu.SemaphoreType.DMA((2,))],
            flops=1_000_000,
            nbytes=2_000_000,
        )(state)
        rec_row_b = lax.ppermute(row_b, both, pairs_b)
        rec_row_a = lax.ppermute(row_a, both, pairs_a)
        rows, row_x, pay_far, pay_near = kernel(
            pack_lon,
            [VMEM] * 7,
            [(PLANES, 8, 128), (6, 8, 128), (LON_TILES, 8, 128), (LON_TILES, 8, 128)],
        )(*own, rec_b, rec_a, far_tracers, near_tracers)
        rec_far = lax.ppermute(pay_far, "lon", pairs_far)
        rec_near = lax.ppermute(pay_near, "lon", pairs_near)
        chunked = (K // CHUNK, CHUNK)
        inner, flux_inner = kernel(
            momentum_inner,
            [VMEM] * 5,
            [(2 * K, 8, 128), (4, 8, 128)],
            scratch=[(*chunked, 2, 8, 128), (2, *chunked, 2, 8, 128), (10, 8, 128)],
            flops=10_000_000,
            nbytes=6_000_000,
        )(*own, rows, row_x)
        mixed, moments = kernel(
            momentum_entry,
            [VMEM] * 7 + [ANY] * 2,
            [(2 * K + 8, 8, 128), (stages[0][1], 128)],
            scratch=[
                (GROUPS, 8, 128), (K // CHUNK, 2, 8, 128), (2, K // CHUNK, 2, 8, 128),
                (K, 2, 8, 128), (2, K, 2, 8, 128), (20, 8, 128),
            ],
        )(flat, rows, flux_inner, pay_far, pay_near, rec_far, rec_near, rec_row_b, rec_row_a)
        (first_groups, _), (second_groups, second_size) = stages
        parts = lax.all_to_all(moments, both, 0, 0, axis_index_groups=first_groups, tiled=True)
        (parts,) = kernel(combine, [VMEM], [(second_size, 128)])(parts)
        sent = parts
        parts = lax.all_to_all(parts, both, 0, 0, axis_index_groups=second_groups, tiled=True)
        gain, done = kernel(
            tracers_down,
            [VMEM] * 8 + [ANY],
            [(*chunked, 8, 128), (6, *chunked, 8, 128)],
            flops=10_000_000,
            nbytes=6_000_000,
        )(tracer, diffusivity, flat, mixed, rec_row_b, rec_row_a, rec_far, rec_near, sent)
        (state_out,) = kernel(
            tracers_up, [VMEM] * 4, [(8 * K, 8, 128)], flops=10_000_000, nbytes=6_000_000
        )(gain, done, inner, mixed)
        (surface,) = kernel(finish, [VMEM] * 2, [(8, 128)])(parts, mixed)
        return state_out.reshape(8, K, 8, 128), surface

    return local


def momentum_entry(*refs):
    inputs, outputs, scratch = refs[:7], refs[9:11], refs[11:]
    mixed, moments = outputs
    momentum(*inputs, mixed, moments, *scratch)
    planes2 = scratch[5]
    for face in range(4):
        mixed[AROUND + face] = planes2[4 * face]


def reduction_stages(lat, lon):
    index = np.arange(lat * lon)
    if lat == 32 and lon == 16:
        grid = index.reshape(8, 4, 4, 2, 2)
        along_z = grid.transpose(1, 2, 4, 3, 0).reshape(32, 16)
        rest = grid.transpose(0, 3, 1, 2, 4).reshape(16, 32)
    else:
        grid = index.reshape(lat, lon)
        along_z, rest = grid.T, grid
    return [(g.tolist(), g.shape[1]) for g in (rest, along_z)]


def solution(mesh):
    placed = (
        P(None, None, "lat", "lon"),
        P(None, "lat", "lon"),
        P(None, "lat", "lon"),
        P("lat", "lon"),
        P("lat", "lon"),
        P("lat", "lon"),
    )
    return jax.shard_map(
        make_local(dict(mesh.shape)),
        mesh=mesh,
        in_specs=placed,
        out_specs=(P(None, None, "lat", "lon"), P("lat", "lon")),
        check_vma=False,
    )
```

```python
import functools

import jax
import jax.numpy as jnp
import numpy as np
from jax import lax
from jax.experimental import pallas as pl
from jax.experimental.pallas import tpu as pltpu
from jax.sharding import PartitionSpec as P

ITERS = 3
K = 48
HORIZONTAL_RATE = 0.2
FLUX_SCALE = 0.02
FACE_SCALE = 0.25
F32 = jnp.float32

PAIR_UV = 0
PAIR_STRIP = 48
PAIR_SURF = 50
ROW_X = 51
LAT_TILES = 57
ROW_TILES = 36
PAIR_VISC = 36
SECOND_TILES = 60
PL_U, PL_V, PL_VISC, PL_WET, PL_STO, PL_SUR = 0, 48, 96, 143, 144, 145
BESIDE, BESIDE_WET = 99, 96
HALO, CROSS = 152, 298
GROUPS = 38
LON_WIDE = 10
LON_TILES = LON_WIDE + 3
CHUNK = 8
ZED, AROUND = 96, 100


def whereabouts():
    band = lax.axis_index("lat")
    return lax.rem(band, 2), band == lax.axis_size("lat") - 1, lax.rem(lax.axis_index("lon"), 2)


def sub_iota():
    return lax.broadcasted_iota(jnp.int32, (8, 128), 0)


def lane_iota():
    return lax.broadcasted_iota(jnp.int32, (8, 128), 1)


def lroll(x, shift):
    return pltpu.roll(x, shift, 1)


def sroll(x, shift):
    return pltpu.roll(x, shift, 0)


def strip_slot():
    return ((lane_iota() + 4) >> 3) & 15


def flip_lanes(x):
    return jnp.take_along_axis(x, 127 - lane_iota(), axis=1)


def flip_rows(x):
    sub = sub_iota()
    x = sroll(x, 4)
    x = jnp.where((sub & 2) == 0, sroll(x, 6), sroll(x, 2))
    return jnp.where((sub & 1) == 0, sroll(x, 7), sroll(x, 1))


def thickness_at(level):
    return 0.5 + level * (1.0 / 48.0)


def spacing_at(level):
    return 96.0 / jnp.full((8, 128), 49.0 + 2.0 * level, F32)


def depth_of(count):
    return 0.5 * count + count * (count - 1.0) * (1.0 / 96.0)


def pack_lat(
    state_any, visc_any, wet_any, storage_any, surf_any,
    out_b, out_a, out_state, out_flat,
    pay_b, pay_a, state, visc, flat, wet, sems, out_sems,
):
    odd, top, _ = whereabouts()
    half = 48 * 8
    copies = [
        pltpu.make_async_copy(state_any.at[pl.ds(0, half)], state.at[pl.ds(0, half)], sems.at[0]),
        pltpu.make_async_copy(state_any.at[pl.ds(half, half)], state.at[pl.ds(half, half)], sems.at[1]),
        pltpu.make_async_copy(visc_any, visc, sems.at[2]),
        pltpu.make_async_copy(wet_any, wet, sems.at[3]),
        pltpu.make_async_copy(storage_any, flat.at[1], sems.at[4]),
        pltpu.make_async_copy(surf_any, flat.at[2], sems.at[5]),
    ]
    for copy in copies:
        copy.start()
    sub = sub_iota()
    keep = (sub < 4).astype(jnp.int32) == odd

    def pack(tiles):
        @pl.when(jnp.logical_not(top))
        def _():
            for tile, first, second, _ in tiles(False):
                rolled = sroll(second, 4)
                pay_a[tile] = jnp.where(keep, first, rolled)
                pay_b[tile] = jnp.where(keep, rolled, first)

        @pl.when(top)
        def _():
            for tile, first, second, _ in tiles(False):
                pay_a[tile] = jnp.where(keep, first, sroll(second, 4))
            for tile, first, second, sign in tiles(True):
                turned = flip_rows(flip_lanes(jnp.where(keep, sroll(second, 4), first)))
                pay_b[tile] = -turned if sign < 0 else turned

    def velocities(mirrored):
        del mirrored
        for k in range(48):
            yield k, state[k * 8 : k * 8 + 8, :], state[(k + 48) * 8 : (k + 48) * 8 + 8, :], -1.0

    def strip(t, mirrored):
        tile = jnp.zeros((8, 128), F32)
        for i in range(16 if t < 2 else 15):
            slot = (16 - i) % 16 if mirrored else i
            tile = jnp.where(strip_slot() == slot, lroll(visc[16 * t + i], 8 * slot) if slot else visc[16 * t + i], tile)
        return tile

    def others(mirrored):
        yield PAIR_STRIP, strip(0, mirrored), strip(1, mirrored), 1.0
        yield PAIR_STRIP + 1, strip(2, mirrored), flat[0], 1.0
        yield PAIR_SURF, flat[1], flat[2], 1.0

    def send(source, target, sem):
        copy = pltpu.make_async_copy(source, target, out_sems.at[sem])
        copy.start()
        return copy

    copies[0].wait()
    copies[1].wait()
    leaving = [send(state, out_state, 0)]
    pack(velocities)
    first = pl.ds(0, PAIR_VISC)
    leaving += [send(pay_b.at[first], out_b.at[first], 1), send(pay_a.at[first], out_a.at[first], 2)]
    for copy in copies[2:]:
        copy.wait()
    flat[0] = wet[...].astype(F32)
    leaving.append(send(flat, out_flat, 3))
    pack(others)
    least = jnp.broadcast_to(jnp.minimum(flat[0, 3:4, :], flat[0, 4:5, :]), (8, 128))
    for m in range(6):
        start = (48 + 8 * m) * 8
        row3 = state[pl.ds(start + 3, 8, stride=8), :]
        row4 = state[pl.ds(start + 4, 8, stride=8), :]
        level = (sub + 8 * m).astype(F32)
        diff = jnp.where(level < least, row3 - row4, 0.0)
        pay_b[ROW_X + m] = -flip_lanes(diff)
    rest_b, rest_a = (pl.ds(PAIR_VISC, count - PAIR_VISC) for count in (LAT_TILES, ROW_X))
    leaving += [send(pay_b.at[rest_b], out_b.at[rest_b], 4), send(pay_a.at[rest_a], out_a.at[rest_a], 5)]
    for copy in leaving:
        copy.wait()


def pack_tracers(state_any, visc, pay_b, pay_a, far, near, tracer, sems):
    half = 144 * 8
    copies = [
        pltpu.make_async_copy(
            state_any.at[pl.ds((96 + 144 * i) * 8, half)], tracer.at[pl.ds(i * half, half)], sems.at[i]
        )
        for i in range(2)
    ]
    for copy in copies:
        copy.start()
    for copy in copies:
        copy.wait()
    odd, top, odd_lon = whereabouts()
    lane = lane_iota()
    keep = (sub_iota() < 4).astype(jnp.int32) == odd

    def rows_of(t):
        start = 8 * t * 8
        return tracer[pl.ds(start, 8, stride=8), :], tracer[pl.ds(start + 7, 8, stride=8), :]

    for t in range(ROW_TILES):
        row0, row7 = rows_of(t)
        pay_a[t] = jnp.where(odd == 1, row0, row7)
        pay_b[t] = jnp.where(odd == 1, row7, row0)
    for m in range(24):
        first, rolled = visc[2 * m], sroll(visc[min(2 * m + 1, 46)], 4)
        pay_a[PAIR_VISC + m] = jnp.where(keep, first, rolled)
        pay_b[PAIR_VISC + m] = jnp.where(keep, rolled, first)

    @pl.when(top)
    def _():
        for t in range(ROW_TILES):
            pay_b[t] = flip_lanes(rows_of(t)[1])
        for m in range(24):
            first, rolled = visc[2 * m], sroll(visc[min(2 * m + 1, 46)], 4)
            pay_b[PAIR_VISC + m] = flip_rows(flip_lanes(jnp.where(keep, rolled, first)))

    def scalar(n):
        return tracer[n * 8 : n * 8 + 8, :], 0

    for tile in range(3):
        planes = [functools.partial(scalar, n) for n in range(128 * tile, min(128 * tile + 128, 288))]
        east, west = pack_columns(lane, planes, 1)
        far[tile] = jnp.where(odd_lon == 1, east, west)
        near[tile] = jnp.where(odd_lon == 1, west, east)


def pack_columns(lane, planes, width):
    east = jnp.zeros((8, 128), F32)
    west = jnp.zeros((8, 128), F32)
    slots = 128 // width
    slot_of = lane // width
    for j, load in enumerate(planes):
        if load is None:
            continue
        x, offset = load()
        shift = (j * width - offset) & 127
        x = lroll(x, shift) if shift else x
        west = jnp.where(slot_of == j, x, west)
        east = jnp.where(slot_of == (j - 1) % slots, x, east)
    return east, west


def lon_planes(state, visc, flat, rows, strips, row_x):
    def plane(n):
        if n < 96:
            return state[n * 8 : n * 8 + 8, :], 0
        if n < 143:
            return visc[n - 96], 0
        if n < 146:
            return flat[n - 143], 0
        if n < HALO:
            return flat[0], 0
        if n < HALO + 96:
            return rows[n - HALO], 0
        if n < HALO + PL_WET:
            k = n - HALO - PL_VISC
            return strips[k // 16], 8 * (k % 16)
        if n < CROSS:
            return rows[n - HALO - PL_WET + BESIDE_WET], 0
        return row_x[n - CROSS], 0

    lane = lane_iota()
    for tile in range(LON_WIDE):
        order = [32 * tile + 8 * (j % 4) + j // 4 for j in range(32)]
        planes = [functools.partial(plane, n) if n < CROSS + 6 else None for n in order]
        yield tile, pack_columns(lane, planes, 4)


def pack_lon(
    state, visc, flat, rec_b, rec_a, far_tracers, near_tracers, rows, row_x, far, near, strips
):
    odd, _, odd_lon = whereabouts()
    sub = sub_iota()
    keep = (sub < 4).astype(jnp.int32) != odd

    def unpair(tile):
        a, b = rec_a[tile], rec_b[tile]
        return jnp.where(keep, a, b), sroll(jnp.where(keep, b, a), 4)

    for k in range(48):
        first, second = unpair(k)
        rows[PL_U + k] = first
        rows[PL_V + k] = second
    strips[0], strips[1] = unpair(PAIR_STRIP)
    strips[2], rows[BESIDE_WET] = unpair(PAIR_STRIP + 1)
    rows[BESIDE_WET + 1], rows[BESIDE_WET + 2] = unpair(PAIR_SURF)
    for m in range(6):
        row_x[m] = rec_b[ROW_X + m]
    for tile, (east, west) in lon_planes(state, visc, flat, rows, strips, row_x):
        far[tile] = jnp.where(odd_lon == 1, east, west)
        near[tile] = jnp.where(odd_lon == 1, west, east)
    for tile in range(3):
        far[LON_WIDE + tile] = far_tracers[tile]
        near[LON_WIDE + tile] = near_tracers[tile]


def each(fn, *lists):
    return [fn(*items) for items in zip(*lists)]


def north_pair(q):
    sub = sub_iota()
    return [sroll(jnp.where(sub == 0, q[1], q[0]), 7), sroll(jnp.where(sub == 0, q[0], q[1]), 7)]


def south_pair(q):
    sub = sub_iota()
    return [sroll(jnp.where(sub == 7, q[1], q[0]), 1), sroll(jnp.where(sub == 7, q[0], q[1]), 1)]


def east_within(q):
    return [lroll(x, 127) for x in q]


def west_within(q):
    return [lroll(x, 1) for x in q]


def columns(load, cross_row, coefficient_at, level_count, top, counts, gain, done, keep):
    sub = sub_iota()
    zero = jnp.zeros((8, 128), F32)
    cross = jnp.logical_and(top, sub == 3)
    ghost = jnp.logical_and(top, sub < 4)
    face_east = each(jnp.minimum, level_count, east_within(level_count))
    face_west = each(jnp.minimum, level_count, west_within(level_count))
    face_north = each(jnp.minimum, level_count, north_pair(level_count))
    face_south = each(jnp.minimum, level_count, south_pair(level_count))
    sums = [
        face_east[0], jnp.where(ghost, face_west[1], face_east[1]),
        face_north[0], jnp.where(ghost, face_south[1], face_north[1]),
    ]
    for i, tile in enumerate(face_east + face_north + level_count + sums):
        counts[i] = tile

    def blend(field, chunk, i, open_east, open_north):
        q = load(field, chunk, i)
        over_east = each(lambda o, a, b: jnp.where(o, a - b, 0.0), open_east, east_within(q), q)
        over_north = each(lambda o, a, b: jnp.where(o, a - b, 0.0), open_north, north_pair(q), q)
        if field == 1:
            over_north[1] = jnp.where(cross, cross_row(chunk, i), over_north[1])
        return each(
            lambda c, a, b, d, e: c + HORIZONTAL_RATE * (a - b + d - e),
            q, over_east, west_within(over_east), over_north, south_pair(over_north),
        )

    def forward(chunk, carry):
        above, prev_gain, prev = carry
        for i in range(CHUNK):
            kf = (CHUNK * chunk + i).astype(F32)
            thick = thickness_at(kf)
            space = spacing_at(kf)
            coefficient = coefficient_at(chunk, i)
            below = [jnp.where(kf + 1.0 < counts[4 + j], coefficient[j] * space, 0.0) for j in range(2)]
            open_east = [kf < counts[j] for j in range(2)]
            open_north = [kf < counts[2 + j] for j in range(2)]
            inverse = [1.0 / (thick + above[j] + below[j] - above[j] * prev_gain[j]) for j in range(2)]
            new_gain = [below[j] * inverse[j] for j in range(2)]
            new = []
            for field in range(2):
                value = blend(field, chunk, i, open_east, open_north)
                new.append([(thick * value[j] + above[j] * prev[field][j]) * inverse[j] for j in range(2)])
            for j in range(2):
                gain[chunk, i, j] = new_gain[j]
                done[0, chunk, i, j] = new[0][j]
                done[1, chunk, i, j] = new[1][j]
            above, prev_gain, prev = below, new_gain, new
        return above, prev_gain, prev

    zeros = [zero, zero]
    lax.fori_loop(0, K // CHUNK, forward, (zeros, zeros, [zeros, zeros]))

    def backward(step, carry):
        chunk = K // CHUNK - 1 - step
        low, flux = carry
        for i in reversed(range(CHUNK)):
            k = CHUNK * chunk + i
            kf = k.astype(F32)
            thick = thickness_at(kf)
            low = [
                [done[field, chunk, i, j] + gain[chunk, i, j] * low[field][j] for j in range(2)] for field in range(2)
            ]
            flux = [
                [
                    flux[field][j] + jnp.where(kf < counts[6 + 2 * field + j], thick * low[field][j], 0.0)
                    for j in range(2)
                ]
                for field in range(2)
            ]
            for field in range(2):
                keep(field, k, low[field][0])
        return low, flux

    _, flux = lax.fori_loop(0, K // CHUNK, backward, ([zeros, zeros], [zeros, zeros]))
    return flux


def momentum_inner(state, visc, flat, rows, row_x, rec_b, rec_a, mixed, flux_out, gain, done, counts):
    odd, top, _ = whereabouts()
    keep_rows = (sub_iota() < 4).astype(jnp.int32) != odd

    def load(field, chunk, i):
        n = 48 * field + CHUNK * chunk + i
        return [state[pl.ds(n * 8, 8), :], rows[n]]

    def coefficient_at(chunk, i):
        tile = PAIR_VISC + CHUNK // 2 * chunk + i // 2
        a, b = rec_a[tile], rec_b[tile]
        beside = sroll(jnp.where(keep_rows, b, a), 4) if i % 2 else jnp.where(keep_rows, a, b)
        return [visc[jnp.minimum(CHUNK * chunk + i, 46)], beside]

    def cross_row(chunk, i):
        return jnp.broadcast_to(row_x[chunk, i : i + 1, :], (8, 128))

    def keep(field, k, tile):
        mixed[48 * field + k] = tile

    flux = columns(load, cross_row, coefficient_at, [flat[0], rows[BESIDE_WET]], top, counts, gain, done, keep)
    for field in range(2):
        for j in range(2):
            flux_out[2 * field + j] = flux[field][j]


def to_last(x):
    return lroll(x, 124)


def to_first(x):
    return lroll(x, 116)


def momentum(
    flat, rows, flux_inner, pay_far, pay_near, far, near,
    mixed, moments,
    windows, below_all, scaled_all, gain, done, planes2,
):
    _, top, odd_lon = whereabouts()
    lane = lane_iota()
    sub = sub_iota()
    zero = jnp.zeros((8, 128), F32)
    ghost = jnp.logical_and(top, sub < 4)

    for tile in range(LON_WIDE):
        sent = [pay_far[tile], pay_near[tile]]
        came = [far[tile], near[tile]]
        own_east, own_west = (jnp.where(odd_lon == 1, *pair) for pair in (sent, sent[::-1]))
        halo_east, halo_west = (jnp.where(odd_lon == 1, *pair) for pair in (came, came[::-1]))
        for g in range(min(4, GROUPS - 4 * tile)):
            here = ((lane - 4 * g) & 15) < 4
            first = lroll(jnp.where(here, halo_east, own_east), (4 - 4 * g) & 127)
            second = lroll(jnp.where(here, own_west, halo_west), (12 - 4 * g) & 127)
            windows[4 * tile + g] = jnp.where((lane & 15) < 8, first, second)

    def window(n):
        shift = (128 - 16 * (n % 8)) & 127
        return lroll(windows[n // 8], shift) if shift else windows[n // 8]

    def everywhere(x):
        x = jnp.where(lane < 16, x, 0.0)
        for step in (16, 32, 64):
            x = x + lroll(x, step)
        return x

    wet_window = [everywhere(window(PL_WET)), everywhere(window(PL_WET + HALO))]
    face_east = each(jnp.minimum, wet_window, east_within(wet_window))
    face_west = each(jnp.minimum, wet_window, west_within(wet_window))
    face_north = each(jnp.minimum, wet_window, north_pair(wet_window))
    face_south = each(jnp.minimum, wet_window, south_pair(wet_window))
    sum_u = [face_east[0], jnp.where(ghost, face_west[1], face_east[1])]
    sum_v = [face_north[0], jnp.where(ghost, face_south[1], face_north[1])]
    cross = jnp.logical_and(top, sub == 3)
    part = lane // 16

    for chunk in range(K // CHUNK):
        level = (part + CHUNK * chunk).astype(F32)
        thick = thickness_at(level)
        space = 96.0 / (49.0 + 2.0 * level)
        open_east = [level < c for c in face_east]
        open_north = [level < c for c in face_north]
        group = PL_VISC // CHUNK + chunk
        for j, shift in enumerate((0, HALO // CHUNK)):
            below_all[chunk, j] = jnp.where(level + 1.0 < wet_window[j], windows[group + shift] * space, 0.0)
        for field in range(2):
            group = K // CHUNK * field + chunk
            q = [windows[group], windows[group + HALO // CHUNK]]
            over_east = each(lambda o, a, b: jnp.where(o, a - b, 0.0), open_east, east_within(q), q)
            over_north = each(lambda o, a, b: jnp.where(o, a - b, 0.0), open_north, north_pair(q), q)
            if field == 1:
                levels = jnp.where(part == sub, everywhere(window(CROSS + chunk)), 0.0)
                extra = jnp.broadcast_to(jnp.sum(levels, axis=0, keepdims=True), (8, 128))
                over_north[1] = jnp.where(cross, extra, over_north[1])
            blended = each(
                lambda c, a, b, d, e: c + HORIZONTAL_RATE * (a - b + d - e),
                q, over_east, west_within(over_east), over_north, south_pair(over_north),
            )
            for j in range(2):
                scaled_all[field, chunk, j] = thick * blended[j]

    def at_level(tile, k):
        shift = (128 - 16 * (k % CHUNK)) & 127
        return lroll(tile, shift) if shift else tile

    above = prev_gain = [zero, zero]
    prev = [[zero, zero], [zero, zero]]
    for k in range(K):
        thick = 0.5 + k / 48.0
        below = [at_level(below_all[k // CHUNK, j], k) for j in range(2)]
        inverse = [1.0 / (thick + above[j] + below[j] - above[j] * prev_gain[j]) for j in range(2)]
        prev_gain = [below[j] * inverse[j] for j in range(2)]
        prev = [
            [
                (at_level(scaled_all[field, k // CHUNK, j], k) + above[j] * prev[field][j]) * inverse[j]
                for j in range(2)
            ]
            for field in range(2)
        ]
        for j in range(2):
            gain[k, j] = prev_gain[j]
            for field in range(2):
                done[field, k, j] = prev[field][j]
        above = below
    low = flux = [[zero, zero], [zero, zero]]
    for k in reversed(range(K)):
        thick = 0.5 + k / 48.0
        low = [[done[field, k, j] + gain[k, j] * low[field][j] for j in range(2)] for field in range(2)]
        flux = [
            [flux[field][j] + jnp.where(k < counts[j], thick * low[field][j], 0.0) for j in range(2)]
            for field, counts in enumerate((sum_u, sum_v))
        ]
        for field in range(2):
            mixed[48 * field + k] = low[field][0]

    def put_together(inner, edge):
        own = [
            jnp.where(lane == 127, to_last(e), jnp.where(lane == 0, to_first(e), q)) for q, e in zip(inner, edge)
        ]
        return own + [jnp.where(lane < 64, to_last(e), to_first(e)) for e in edge]

    flux_u = put_together([flux_inner[0], flux_inner[1]], flux[0])
    flux_v = put_together([flux_inner[2], flux_inner[3]], flux[1])

    valid = jnp.logical_or(lane < 4, lane >= 124)

    def four(n, own):
        pair = [window(n), window(n + HALO)]
        return [own, rows[n - PL_WET + BESIDE_WET]] + [
            jnp.where(valid, jnp.where(lane < 64, to_last(e), to_first(e)), 0.0) for e in pair
        ]

    def east(q):
        return [
            lroll(jnp.where(lane == 0, q[2], q[0]), 127),
            lroll(jnp.where(lane == 0, q[3], q[1]), 127),
            lroll(jnp.where(lane == 0, q[0], q[2]), 127),
            lroll(jnp.where(lane == 0, q[1], q[3]), 127),
        ]

    def west(q):
        return [
            lroll(jnp.where(lane == 127, q[2], q[0]), 1),
            lroll(jnp.where(lane == 127, q[3], q[1]), 1),
            lroll(jnp.where(lane == 127, q[0], q[2]), 1),
            lroll(jnp.where(lane == 127, q[1], q[3]), 1),
        ]

    def north(q):
        return north_pair(q[:2]) + north_pair(q[2:])

    def south(q):
        return south_pair(q[:2]) + south_pair(q[2:])

    level_count = four(PL_WET, flat[0])
    around = [each(jnp.minimum, level_count, shift(level_count)) for shift in (east, west, north, south)]
    for i, c in enumerate(around):
        for j in range(4):
            planes2[4 * i + j] = c[j]
    for j in range(4):
        planes2[16 + j] = level_count[j]
    last = jnp.logical_and(top, sub == 7)
    first_ghost = jnp.logical_and(top, sub == 0)
    flux_v = [
        jnp.where(last, 0.0, flux_v[0]),
        jnp.where(first_ghost, 0.0, flux_v[1]),
        jnp.where(last, 0.0, flux_v[2]),
        jnp.where(first_ghost, 0.0, flux_v[3]),
    ]
    plain = each(
        lambda a, b, c, d: a - b + c - d, flux_u, west(flux_u), flux_v, south(flux_v)
    )
    mirrored = each(
        lambda a, b, c, d: a - b + c - d, east(flux_u), flux_u, north(flux_v), flux_v
    )
    divergence = [
        plain[0],
        jnp.where(ghost, mirrored[1], plain[1]),
        plain[2],
        jnp.where(ghost, mirrored[3], plain[3]),
    ]
    sto = four(PL_STO, flat[1])
    old = four(PL_SUR, flat[2])
    faces = [[FACE_SCALE * depth_of(planes2[4 * i + j]) for j in range(4)] for i in range(4)]
    diagonal = [
        jnp.maximum(sto[j] + faces[0][j] + faces[1][j] + faces[2][j] + faces[3][j], 0.1) for j in range(4)
    ]
    ocean = [planes2[16 + j] > 0.0 for j in range(4)]
    start = [jnp.where(ocean[j], old[j], 0.0) for j in range(4)]
    around = [east(start), west(start), north(start), south(start)]
    inverse = [1.0 / diagonal[j] for j in range(4)]
    basis = []
    for j in range(4):
        forcing = jnp.where(ocean[j], sto[j] * old[j] - FLUX_SCALE * divergence[j], 0.0)
        image = sto[j] * start[j]
        for i in range(4):
            image = image + faces[i][j] * (start[j] - around[i][j])
        basis.append((forcing - image) / diagonal[j])
    z0 = basis

    def spread(z):
        nb = [east(z), west(z), north(z), south(z)]
        return [
            (faces[0][j] * nb[0][j] + faces[1][j] * nb[1][j] + faces[2][j] * nb[2][j] + faces[3][j] * nb[3][j])
            * inverse[j]
            for j in range(4)
        ]

    z1 = spread(z0)
    z2 = spread(z1)
    mixed[ZED + 0] = start[0]
    mixed[ZED + 1] = z0[0]
    mixed[ZED + 2] = z1[0]
    mixed[ZED + 3] = z2[0]
    weighted = [diagonal[0] * z[0] for z in (z0, z1, z2)]
    north_weight = jnp.where(last, 1.0, 2.0)
    edge = z2[0] * (
        2.0 * faces[0][0] * east(z2)[0] + north_weight * faces[2][0] * north(z2)[0]
    )
    products = [
        weighted[0] * z0[0],
        weighted[0] * z1[0],
        weighted[1] * z1[0],
        weighted[1] * z2[0],
        weighted[2] * z2[0],
        edge,
    ]
    row = jnp.zeros((1, 128), F32)
    for i, product in enumerate(products):
        total = jnp.sum(jnp.sum(product, axis=0, keepdims=True), axis=1, keepdims=True)
        row = jnp.where(lane[:1] == i, total, row)
    moments[...] = jnp.broadcast_to(row, moments.shape)


def tracers_down(state, diff, flat, mixed, rec_b, rec_a, far, near, after, gain, done):
    del after
    odd, _, odd_lon = whereabouts()
    lane = lane_iota()
    sub = sub_iota()
    level_count = flat[0]
    zero = jnp.zeros((8, 128), F32)

    def forward(chunk, carry):
        above, prev_gain, prev = carry
        for i in range(CHUNK):
            k = CHUNK * chunk + i
            kf = k.astype(F32)
            thick = thickness_at(kf)
            coefficient = diff[jnp.minimum(k, 46)]
            below = jnp.where(kf + 1.0 < level_count, coefficient * spacing_at(kf), 0.0)
            inverse = 1.0 / (thick + above + below - above * prev_gain)
            new_gain = below * inverse
            gain[chunk, i] = new_gain
            open_face = [kf < mixed[AROUND + face] for face in range(4)]
            new = []
            for f in range(6):
                first = f * 48 + CHUNK * chunk
                q = state[pl.ds((first + i) * 8, 8), :]
                row_a = rec_a[f * 6 + chunk, i : i + 1, :]
                row_b = rec_b[f * 6 + chunk, i : i + 1, :]
                row_n = jnp.broadcast_to(jnp.where(odd == 1, row_b, row_a), (8, 128))
                row_s = jnp.broadcast_to(jnp.where(odd == 1, row_a, row_b), (8, 128))
                tile, j = first >> 7, (first & 127) + i
                a, b = far[LON_WIDE + tile], near[LON_WIDE + tile]
                side = lroll(jnp.where((lane == j).astype(jnp.int32) == odd_lon, a, b), (128 - j) & 127)
                change = jnp.where(open_face[0], lroll(jnp.where(lane == 0, side, q), 127) - q, 0.0)
                change += jnp.where(open_face[1], lroll(jnp.where(lane == 127, side, q), 1) - q, 0.0)
                change += jnp.where(open_face[2], sroll(jnp.where(sub == 0, row_n, q), 7) - q, 0.0)
                change += jnp.where(open_face[3], sroll(jnp.where(sub == 7, row_s, q), 1) - q, 0.0)
                value = (thick * (q + HORIZONTAL_RATE * change) + above * prev[f]) * inverse
                done[f, chunk, i] = value
                new.append(value)
            above, prev_gain, prev = below, new_gain, new
        return above, prev_gain, prev

    lax.fori_loop(0, K // CHUNK, forward, (zero, zero, [zero] * 6))


def tracers_up(gain, done, inner, mixed, out):
    lane = lane_iota()
    for n in range(96):
        edge = mixed[n]
        out[n] = jnp.where(lane == 127, to_last(edge), jnp.where(lane == 0, to_first(edge), inner[n]))
    zero = jnp.zeros((8, 128), F32)

    def backward(step, low):
        chunk = K // CHUNK - 1 - step
        for i in reversed(range(CHUNK)):
            g = gain[chunk, i]
            low = [done[f, chunk, i] + g * low[f] for f in range(6)]
            for f in range(6):
                out[96 + f * 48 + CHUNK * chunk + i] = low[f]
        return low

    lax.fori_loop(0, K // CHUNK, backward, [zero] * 6)


def combine(parts, out):
    out[...] = jnp.broadcast_to(jnp.sum(parts[...], axis=0, keepdims=True), out.shape)


def finish(parts, mixed, surface):
    total = jnp.sum(parts[...], axis=0, keepdims=True)
    nu = [jnp.broadcast_to(total[:, i : i + 1], (8, 128)) for i in range(6)]

    def inner(p, q, shift):
        out = None
        for i, a in enumerate(p):
            for j, b in enumerate(q):
                term = a * b * nu[i + j + shift]
                out = term if out is None else out + term
        return out

    one = jnp.ones((8, 128), F32)
    scaled = [one]
    direction = [one]
    product = nu[0]
    move = [jnp.zeros((8, 128), F32)] * 3
    for iteration in range(ITERS):
        curvature = inner(direction, direction, 0) - inner(direction, direction, 1)
        alpha = jnp.where(curvature > 0.0, product / curvature, 0.0)
        for i, d in enumerate(direction):
            move[i] = move[i] + alpha * d
        if iteration + 1 < ITERS:
            longer = scaled + [jnp.zeros((8, 128), F32)]
            for i, d in enumerate(direction):
                longer[i] = longer[i] - alpha * d
                longer[i + 1] = longer[i + 1] + alpha * d
            scaled = longer
            following = inner(scaled, scaled, 0)
            beta = jnp.where(product > 0.0, following / product, 0.0)
            direction = [
                scaled[i] + (beta * direction[i] if i < len(direction) else 0.0) for i in range(len(scaled))
            ]
            product = following
    surface[...] = sum((move[i] * mixed[ZED + 1 + i] for i in range(3)), mixed[ZED])


VMEM_LIMIT = 24 * 1024 * 1024
FIRST_LIMIT = 60 * 1024 * 1024
VMEM = pl.BlockSpec(memory_space=pltpu.VMEM)
ANY = pl.BlockSpec(memory_space=pl.ANY)


def kernel(body, ins, outs, scratch=(), flops=0, nbytes=0, limit=VMEM_LIMIT, out_spec=VMEM):
    return pl.pallas_call(
        body,
        out_shape=[jax.ShapeDtypeStruct(s, F32) for s in outs],
        in_specs=ins,
        out_specs=[out_spec] * len(outs),
        scratch_shapes=[pltpu.VMEM(s, F32) if isinstance(s, tuple) else s for s in scratch],
        compiler_params=pltpu.CompilerParams(vmem_limit_bytes=limit),
        cost_estimate=pl.CostEstimate(flops=flops, bytes_accessed=nbytes, transcendentals=0),
    )


def lat_pairs(lat, lon):
    first, second = [], []
    for l in range(lat):
        for p in range(lon):
            here = l * lon + p
            first.append((here, (l ^ 1) * lon + p))
            if l == lat - 1:
                second.append((here, l * lon + lon - 1 - p))
            elif l % 2 == 1:
                second.append((here, here + lon))
            elif l > 0:
                second.append((here, here - lon))
    return first, second


def lon_pairs(lon):
    far, near = [], []
    for p in range(lon):
        step = 1 if p % 2 else -1
        far.append((p, (p + step) % lon))
        near.append((p, p ^ 1))
    return far, near


def make_local(mesh_shape):
    lat, lon = mesh_shape["lat"], mesh_shape["lon"]
    pairs_a, pairs_b = lat_pairs(lat, lon)
    pairs_far, pairs_near = lon_pairs(lon)
    both = ("lat", "lon")
    stages = reduction_stages(lat, lon)

    def local(ocean_state, viscosity, diffusivity, wet_levels, storage, surface_old):
        state = ocean_state.reshape(8 * K * 8, 128)
        pay_b, pay_a, uv, flat = kernel(
            pack_lat,
            [ANY] * 5,
            [(LAT_TILES, 8, 128), (ROW_X, 8, 128), (96 * 8, 128), (3, 8, 128)],
            scratch=[
                (LAT_TILES, 8, 128), (ROW_X, 8, 128),
                (96 * 8, 128), (47, 8, 128), (3, 8, 128),
                pltpu.VMEM((8, 128), jnp.int32), pltpu.SemaphoreType.DMA((6,)), pltpu.SemaphoreType.DMA((6,)),
            ],
            out_spec=ANY,
            limit=FIRST_LIMIT,
        )(state, viscosity, wet_levels, storage, surface_old)
        own = (uv, viscosity, flat)
        rec_b = lax.ppermute(pay_b, both, pairs_b)
        rec_a = lax.ppermute(pay_a, both, pairs_a)
        row_b, row_a, far_tracers, near_tracers, tracer = kernel(
            pack_tracers,
            [ANY, VMEM],
            [(SECOND_TILES, 8, 128)] * 2 + [(3, 8, 128)] * 2 + [(288 * 8, 128)],
            scratch=[pltpu.SemaphoreType.DMA((2,))],
            flops=1_000_000,
            nbytes=2_000_000,
        )(state, viscosity)
        rec_row_b = lax.ppermute(row_b, both, pairs_b)
        rec_row_a = lax.ppermute(row_a, both, pairs_a)
        rows, row_x, pay_far, pay_near = kernel(
            pack_lon,
            [VMEM] * 7,
            [(BESIDE, 8, 128), (6, 8, 128), (LON_TILES, 8, 128), (LON_TILES, 8, 128)],
            scratch=[(3, 8, 128)],
        )(*own, rec_b, rec_a, far_tracers, near_tracers)
        rec_far = lax.ppermute(pay_far, "lon", pairs_far)
        rec_near = lax.ppermute(pay_near, "lon", pairs_near)
        chunked = (K // CHUNK, CHUNK)
        inner, flux_inner = kernel(
            momentum_inner,
            [VMEM] * 7,
            [(2 * K, 8, 128), (4, 8, 128)],
            scratch=[(*chunked, 2, 8, 128), (2, *chunked, 2, 8, 128), (10, 8, 128)],
            flops=10_000_000,
            nbytes=6_000_000,
        )(*own, rows, row_x, rec_row_b, rec_row_a)
        mixed, moments = kernel(
            momentum_entry,
            [VMEM] * 7,
            [(2 * K + 8, 8, 128), (stages[0][1], 128)],
            scratch=[
                (GROUPS, 8, 128), (K // CHUNK, 2, 8, 128), (2, K // CHUNK, 2, 8, 128),
                (K, 2, 8, 128), (2, K, 2, 8, 128), (20, 8, 128),
            ],
        )(flat, rows, flux_inner, pay_far, pay_near, rec_far, rec_near)
        (first_groups, _), (second_groups, second_size) = stages
        parts = lax.all_to_all(moments, both, 0, 0, axis_index_groups=first_groups, tiled=True)
        (parts,) = kernel(combine, [VMEM], [(second_size, 128)])(parts)
        sent = parts
        parts = lax.all_to_all(parts, both, 0, 0, axis_index_groups=second_groups, tiled=True)
        gain, done = kernel(
            tracers_down,
            [VMEM] * 8 + [ANY],
            [(*chunked, 8, 128), (6, *chunked, 8, 128)],
            flops=10_000_000,
            nbytes=6_000_000,
        )(tracer, diffusivity, flat, mixed, rec_row_b, rec_row_a, rec_far, rec_near, sent)
        (state_out,) = kernel(
            tracers_up, [VMEM] * 4, [(8 * K, 8, 128)], flops=10_000_000, nbytes=6_000_000
        )(gain, done, inner, mixed)
        (surface,) = kernel(finish, [VMEM] * 2, [(8, 128)])(parts, mixed)
        return state_out.reshape(8, K, 8, 128), surface

    return local


def momentum_entry(*refs):
    inputs, outputs, scratch = refs[:7], refs[7:9], refs[9:]
    mixed, moments = outputs
    momentum(*inputs, mixed, moments, *scratch)
    planes2 = scratch[5]
    for face in range(4):
        mixed[AROUND + face] = planes2[4 * face]


def reduction_stages(lat, lon):
    index = np.arange(lat * lon)
    if lat == 32 and lon == 16:
        grid = index.reshape(8, 4, 4, 2, 2)
        along_z = grid.transpose(1, 2, 4, 3, 0).reshape(32, 16)
        rest = grid.transpose(0, 3, 1, 2, 4).reshape(16, 32)
    else:
        grid = index.reshape(lat, lon)
        along_z, rest = grid.T, grid
    return [(g.tolist(), g.shape[1]) for g in (rest, along_z)]


def solution(mesh):
    placed = (
        P(None, None, "lat", "lon"),
        P(None, "lat", "lon"),
        P(None, "lat", "lon"),
        P("lat", "lon"),
        P("lat", "lon"),
        P("lat", "lon"),
    )
    return jax.shard_map(
        make_local(dict(mesh.shape)),
        mesh=mesh,
        in_specs=placed,
        out_specs=(P(None, None, "lat", "lon"), P("lat", "lon")),
        check_vma=False,
    )
```

```python
import functools

import jax
import jax.numpy as jnp
import numpy as np
from jax import lax
from jax.experimental import pallas as pl
from jax.experimental.pallas import tpu as pltpu
from jax.sharding import PartitionSpec as P

ITERS = 3
K = 48
HORIZONTAL_RATE = 0.2
FLUX_SCALE = 0.02
FACE_SCALE = 0.25
F32 = jnp.float32

PAIR_UV = 0
PAIR_STRIP = 48
PAIR_SURF = 50
ROW_X = 51
LAT_TILES = 57
ROW_TILES = 36
PAIR_VISC = 36
SECOND_TILES = 60
PL_U, PL_V, PL_VISC, PL_WET, PL_STO, PL_SUR = 0, 48, 96, 143, 144, 145
BESIDE, BESIDE_WET = 99, 96
HALO, CROSS = 152, 298
GROUPS = 38
LON_WIDE = 10
LON_TILES = LON_WIDE + 3
CHUNK = 8
ZED, AROUND = 96, 100


def whereabouts():
    band = lax.axis_index("lat")
    return lax.rem(band, 2), band == lax.axis_size("lat") - 1, lax.rem(lax.axis_index("lon"), 2)


def sub_iota():
    return lax.broadcasted_iota(jnp.int32, (8, 128), 0)


def lane_iota():
    return lax.broadcasted_iota(jnp.int32, (8, 128), 1)


def lroll(x, shift):
    return pltpu.roll(x, shift, 1)


def sroll(x, shift):
    return pltpu.roll(x, shift, 0)


def strip_slot():
    return ((lane_iota() + 4) >> 3) & 15


def flip_lanes(x):
    return jnp.take_along_axis(x, 127 - lane_iota(), axis=1)


def flip_rows(x):
    sub = sub_iota()
    x = sroll(x, 4)
    x = jnp.where((sub & 2) == 0, sroll(x, 6), sroll(x, 2))
    return jnp.where((sub & 1) == 0, sroll(x, 7), sroll(x, 1))


def thickness_at(level):
    return 0.5 + level * (1.0 / 48.0)


def spacing_at(level):
    return 96.0 / jnp.full((8, 128), 49.0 + 2.0 * level, F32)


def depth_of(count):
    return 0.5 * count + count * (count - 1.0) * (1.0 / 96.0)


def pack_lat(
    state_any, visc_any, wet_any, storage_any, surf_any,
    out_b, out_a, out_state, out_flat,
    pay_b, pay_a, state, visc, flat, wet, sems, out_sems,
):
    odd, top, _ = whereabouts()
    half = 48 * 8
    copies = [
        pltpu.make_async_copy(state_any.at[pl.ds(0, half)], state.at[pl.ds(0, half)], sems.at[0]),
        pltpu.make_async_copy(state_any.at[pl.ds(half, half)], state.at[pl.ds(half, half)], sems.at[1]),
        pltpu.make_async_copy(visc_any, visc, sems.at[2]),
        pltpu.make_async_copy(wet_any, wet, sems.at[3]),
        pltpu.make_async_copy(storage_any, flat.at[1], sems.at[4]),
        pltpu.make_async_copy(surf_any, flat.at[2], sems.at[5]),
    ]
    for copy in copies:
        copy.start()
    sub = sub_iota()
    keep = (sub < 4).astype(jnp.int32) == odd

    def pack(tiles):
        @pl.when(jnp.logical_not(top))
        def _():
            for tile, first, second, _ in tiles(False):
                rolled = sroll(second, 4)
                pay_a[tile] = jnp.where(keep, first, rolled)
                pay_b[tile] = jnp.where(keep, rolled, first)

        @pl.when(top)
        def _():
            for tile, first, second, _ in tiles(False):
                pay_a[tile] = jnp.where(keep, first, sroll(second, 4))
            for tile, first, second, sign in tiles(True):
                turned = flip_rows(flip_lanes(jnp.where(keep, sroll(second, 4), first)))
                pay_b[tile] = -turned if sign < 0 else turned

    def velocities(mirrored):
        del mirrored
        for k in range(48):
            yield k, state[k * 8 : k * 8 + 8, :], state[(k + 48) * 8 : (k + 48) * 8 + 8, :], -1.0

    def strip(t, mirrored):
        tile = jnp.zeros((8, 128), F32)
        for i in range(16 if t < 2 else 15):
            slot = (16 - i) % 16 if mirrored else i
            tile = jnp.where(strip_slot() == slot, lroll(visc[16 * t + i], 8 * slot) if slot else visc[16 * t + i], tile)
        return tile

    def others(mirrored):
        yield PAIR_STRIP, strip(0, mirrored), strip(1, mirrored), 1.0
        yield PAIR_STRIP + 1, strip(2, mirrored), flat[0], 1.0
        yield PAIR_SURF, flat[1], flat[2], 1.0

    def send(source, target, sem):
        copy = pltpu.make_async_copy(source, target, out_sems.at[sem])
        copy.start()
        return copy

    copies[0].wait()
    copies[1].wait()
    leaving = [send(state, out_state, 0)]
    pack(velocities)
    first = pl.ds(0, PAIR_VISC)
    leaving += [send(pay_b.at[first], out_b.at[first], 1), send(pay_a.at[first], out_a.at[first], 2)]
    for copy in copies[2:]:
        copy.wait()
    flat[0] = wet[...].astype(F32)
    leaving.append(send(flat, out_flat, 3))
    pack(others)
    least = jnp.broadcast_to(jnp.minimum(flat[0, 3:4, :], flat[0, 4:5, :]), (8, 128))
    for m in range(6):
        start = (48 + 8 * m) * 8
        row3 = state[pl.ds(start + 3, 8, stride=8), :]
        row4 = state[pl.ds(start + 4, 8, stride=8), :]
        level = (sub + 8 * m).astype(F32)
        diff = jnp.where(level < least, row3 - row4, 0.0)
        pay_b[ROW_X + m] = -flip_lanes(diff)
    rest_b, rest_a = (pl.ds(PAIR_VISC, count - PAIR_VISC) for count in (LAT_TILES, ROW_X))
    leaving += [send(pay_b.at[rest_b], out_b.at[rest_b], 4), send(pay_a.at[rest_a], out_a.at[rest_a], 5)]
    for copy in leaving:
        copy.wait()


def pack_tracers(state, visc, pay_b, pay_a, far, near):
    odd, top, odd_lon = whereabouts()
    lane = lane_iota()
    keep = (sub_iota() < 4).astype(jnp.int32) == odd

    def rows_of(t):
        start = (96 + 8 * t) * 8
        return state[pl.ds(start, 8, stride=8), :], state[pl.ds(start + 7, 8, stride=8), :]

    for t in range(ROW_TILES):
        row0, row7 = rows_of(t)
        pay_a[t] = jnp.where(odd == 1, row0, row7)
        pay_b[t] = jnp.where(odd == 1, row7, row0)
    for m in range(24):
        first, rolled = visc[2 * m], sroll(visc[min(2 * m + 1, 46)], 4)
        pay_a[PAIR_VISC + m] = jnp.where(keep, first, rolled)
        pay_b[PAIR_VISC + m] = jnp.where(keep, rolled, first)

    @pl.when(top)
    def _():
        for t in range(ROW_TILES):
            pay_b[t] = flip_lanes(rows_of(t)[1])
        for m in range(24):
            first, rolled = visc[2 * m], sroll(visc[min(2 * m + 1, 46)], 4)
            pay_b[PAIR_VISC + m] = flip_rows(flip_lanes(jnp.where(keep, rolled, first)))

    def scalar(n):
        return state[(96 + n) * 8 : (96 + n) * 8 + 8, :], 0

    for tile in range(3):
        planes = [functools.partial(scalar, n) for n in range(128 * tile, min(128 * tile + 128, 288))]
        east, west = pack_columns(lane, planes, 1)
        far[tile] = jnp.where(odd_lon == 1, east, west)
        near[tile] = jnp.where(odd_lon == 1, west, east)


def pack_columns(lane, planes, width):
    east = jnp.zeros((8, 128), F32)
    west = jnp.zeros((8, 128), F32)
    slots = 128 // width
    slot_of = lane // width
    for j, load in enumerate(planes):
        if load is None:
            continue
        x, offset = load()
        shift = (j * width - offset) & 127
        x = lroll(x, shift) if shift else x
        west = jnp.where(slot_of == j, x, west)
        east = jnp.where(slot_of == (j - 1) % slots, x, east)
    return east, west


def lon_planes(state, visc, flat, rows, strips, row_x):
    def plane(n):
        if n < 96:
            return state[n * 8 : n * 8 + 8, :], 0
        if n < 143:
            return visc[n - 96], 0
        if n < 146:
            return flat[n - 143], 0
        if n < HALO:
            return flat[0], 0
        if n < HALO + 96:
            return rows[n - HALO], 0
        if n < HALO + PL_WET:
            k = n - HALO - PL_VISC
            return strips[k // 16], 8 * (k % 16)
        if n < CROSS:
            return rows[n - HALO - PL_WET + BESIDE_WET], 0
        return row_x[n - CROSS], 0

    lane = lane_iota()
    for tile in range(LON_WIDE):
        order = [32 * tile + 8 * (j % 4) + j // 4 for j in range(32)]
        planes = [functools.partial(plane, n) if n < CROSS + 6 else None for n in order]
        yield tile, pack_columns(lane, planes, 4)


def pack_lon(
    state, visc, flat, rec_b, rec_a, far_tracers, near_tracers, rows, row_x, far, near, strips
):
    odd, _, odd_lon = whereabouts()
    sub = sub_iota()
    keep = (sub < 4).astype(jnp.int32) != odd

    def unpair(tile):
        a, b = rec_a[tile], rec_b[tile]
        return jnp.where(keep, a, b), sroll(jnp.where(keep, b, a), 4)

    for k in range(48):
        first, second = unpair(k)
        rows[PL_U + k] = first
        rows[PL_V + k] = second
    strips[0], strips[1] = unpair(PAIR_STRIP)
    strips[2], rows[BESIDE_WET] = unpair(PAIR_STRIP + 1)
    rows[BESIDE_WET + 1], rows[BESIDE_WET + 2] = unpair(PAIR_SURF)
    for m in range(6):
        row_x[m] = rec_b[ROW_X + m]
    for tile, (east, west) in lon_planes(state, visc, flat, rows, strips, row_x):
        far[tile] = jnp.where(odd_lon == 1, east, west)
        near[tile] = jnp.where(odd_lon == 1, west, east)
    for tile in range(3):
        far[LON_WIDE + tile] = far_tracers[tile]
        near[LON_WIDE + tile] = near_tracers[tile]


def each(fn, *lists):
    return [fn(*items) for items in zip(*lists)]


def north_pair(q):
    sub = sub_iota()
    return [sroll(jnp.where(sub == 0, q[1], q[0]), 7), sroll(jnp.where(sub == 0, q[0], q[1]), 7)]


def south_pair(q):
    sub = sub_iota()
    return [sroll(jnp.where(sub == 7, q[1], q[0]), 1), sroll(jnp.where(sub == 7, q[0], q[1]), 1)]


def east_within(q):
    return [lroll(x, 127) for x in q]


def west_within(q):
    return [lroll(x, 1) for x in q]


def columns(load, cross_row, coefficient_at, level_count, top, counts, gain, done, keep):
    sub = sub_iota()
    zero = jnp.zeros((8, 128), F32)
    cross = jnp.logical_and(top, sub == 3)
    ghost = jnp.logical_and(top, sub < 4)
    face_east = each(jnp.minimum, level_count, east_within(level_count))
    face_west = each(jnp.minimum, level_count, west_within(level_count))
    face_north = each(jnp.minimum, level_count, north_pair(level_count))
    face_south = each(jnp.minimum, level_count, south_pair(level_count))
    sums = [
        face_east[0], jnp.where(ghost, face_west[1], face_east[1]),
        face_north[0], jnp.where(ghost, face_south[1], face_north[1]),
    ]
    for i, tile in enumerate(face_east + face_north + level_count + sums):
        counts[i] = tile

    def blend(field, chunk, i, open_east, open_north):
        q = load(field, chunk, i)
        over_east = each(lambda o, a, b: jnp.where(o, a - b, 0.0), open_east, east_within(q), q)
        over_north = each(lambda o, a, b: jnp.where(o, a - b, 0.0), open_north, north_pair(q), q)
        if field == 1:
            over_north[1] = jnp.where(cross, cross_row(chunk, i), over_north[1])
        return each(
            lambda c, a, b, d, e: c + HORIZONTAL_RATE * (a - b + d - e),
            q, over_east, west_within(over_east), over_north, south_pair(over_north),
        )

    def forward(chunk, carry):
        above, prev_gain, prev = carry
        for i in range(CHUNK):
            kf = (CHUNK * chunk + i).astype(F32)
            thick = thickness_at(kf)
            space = spacing_at(kf)
            coefficient = coefficient_at(chunk, i)
            below = [jnp.where(kf + 1.0 < counts[4 + j], coefficient[j] * space, 0.0) for j in range(2)]
            open_east = [kf < counts[j] for j in range(2)]
            open_north = [kf < counts[2 + j] for j in range(2)]
            inverse = [1.0 / (thick + above[j] + below[j] - above[j] * prev_gain[j]) for j in range(2)]
            new_gain = [below[j] * inverse[j] for j in range(2)]
            new = []
            for field in range(2):
                value = blend(field, chunk, i, open_east, open_north)
                new.append([(thick * value[j] + above[j] * prev[field][j]) * inverse[j] for j in range(2)])
            for j in range(2):
                gain[chunk, i, j] = new_gain[j]
                done[0, chunk, i, j] = new[0][j]
                done[1, chunk, i, j] = new[1][j]
            above, prev_gain, prev = below, new_gain, new
        return above, prev_gain, prev

    zeros = [zero, zero]
    lax.fori_loop(0, K // CHUNK, forward, (zeros, zeros, [zeros, zeros]))

    def backward(step, carry):
        chunk = K // CHUNK - 1 - step
        low, flux = carry
        for i in reversed(range(CHUNK)):
            k = CHUNK * chunk + i
            kf = k.astype(F32)
            thick = thickness_at(kf)
            low = [
                [done[field, chunk, i, j] + gain[chunk, i, j] * low[field][j] for j in range(2)] for field in range(2)
            ]
            flux = [
                [
                    flux[field][j] + jnp.where(kf < counts[6 + 2 * field + j], thick * low[field][j], 0.0)
                    for j in range(2)
                ]
                for field in range(2)
            ]
            for field in range(2):
                keep(field, k, low[field][0])
        return low, flux

    _, flux = lax.fori_loop(0, K // CHUNK, backward, ([zeros, zeros], [zeros, zeros]))
    return flux


def momentum_inner(state, visc, flat, rows, row_x, rec_b, rec_a, mixed, flux_out, gain, done, counts):
    odd, top, _ = whereabouts()
    keep_rows = (sub_iota() < 4).astype(jnp.int32) != odd

    def load(field, chunk, i):
        n = 48 * field + CHUNK * chunk + i
        return [state[pl.ds(n * 8, 8), :], rows[n]]

    def coefficient_at(chunk, i):
        tile = PAIR_VISC + CHUNK // 2 * chunk + i // 2
        a, b = rec_a[tile], rec_b[tile]
        beside = sroll(jnp.where(keep_rows, b, a), 4) if i % 2 else jnp.where(keep_rows, a, b)
        return [visc[jnp.minimum(CHUNK * chunk + i, 46)], beside]

    def cross_row(chunk, i):
        return jnp.broadcast_to(row_x[chunk, i : i + 1, :], (8, 128))

    def keep(field, k, tile):
        mixed[48 * field + k] = tile

    flux = columns(load, cross_row, coefficient_at, [flat[0], rows[BESIDE_WET]], top, counts, gain, done, keep)
    for field in range(2):
        for j in range(2):
            flux_out[2 * field + j] = flux[field][j]


def to_last(x):
    return lroll(x, 124)


def to_first(x):
    return lroll(x, 116)


def momentum(
    flat, rows, flux_inner, pay_far, pay_near, far, near,
    mixed, moments,
    windows, below_all, scaled_all, gain, done, planes2,
):
    _, top, odd_lon = whereabouts()
    lane = lane_iota()
    sub = sub_iota()
    zero = jnp.zeros((8, 128), F32)
    ghost = jnp.logical_and(top, sub < 4)

    for tile in range(LON_WIDE):
        sent = [pay_far[tile], pay_near[tile]]
        came = [far[tile], near[tile]]
        own_east, own_west = (jnp.where(odd_lon == 1, *pair) for pair in (sent, sent[::-1]))
        halo_east, halo_west = (jnp.where(odd_lon == 1, *pair) for pair in (came, came[::-1]))
        for g in range(min(4, GROUPS - 4 * tile)):
            here = ((lane - 4 * g) & 15) < 4
            first = lroll(jnp.where(here, halo_east, own_east), (4 - 4 * g) & 127)
            second = lroll(jnp.where(here, own_west, halo_west), (12 - 4 * g) & 127)
            windows[4 * tile + g] = jnp.where((lane & 15) < 8, first, second)

    def window(n):
        shift = (128 - 16 * (n % 8)) & 127
        return lroll(windows[n // 8], shift) if shift else windows[n // 8]

    def everywhere(x):
        x = jnp.where(lane < 16, x, 0.0)
        for step in (16, 32, 64):
            x = x + lroll(x, step)
        return x

    wet_window = [everywhere(window(PL_WET)), everywhere(window(PL_WET + HALO))]
    face_east = each(jnp.minimum, wet_window, east_within(wet_window))
    face_west = each(jnp.minimum, wet_window, west_within(wet_window))
    face_north = each(jnp.minimum, wet_window, north_pair(wet_window))
    face_south = each(jnp.minimum, wet_window, south_pair(wet_window))
    sum_u = [face_east[0], jnp.where(ghost, face_west[1], face_east[1])]
    sum_v = [face_north[0], jnp.where(ghost, face_south[1], face_north[1])]
    cross = jnp.logical_and(top, sub == 3)
    part = lane // 16

    for chunk in range(K // CHUNK):
        level = (part + CHUNK * chunk).astype(F32)
        thick = thickness_at(level)
        space = 96.0 / (49.0 + 2.0 * level)
        open_east = [level < c for c in face_east]
        open_north = [level < c for c in face_north]
        group = PL_VISC // CHUNK + chunk
        for j, shift in enumerate((0, HALO // CHUNK)):
            below_all[chunk, j] = jnp.where(level + 1.0 < wet_window[j], windows[group + shift] * space, 0.0)
        for field in range(2):
            group = K // CHUNK * field + chunk
            q = [windows[group], windows[group + HALO // CHUNK]]
            over_east = each(lambda o, a, b: jnp.where(o, a - b, 0.0), open_east, east_within(q), q)
            over_north = each(lambda o, a, b: jnp.where(o, a - b, 0.0), open_north, north_pair(q), q)
            if field == 1:
                levels = jnp.where(part == sub, everywhere(window(CROSS + chunk)), 0.0)
                extra = jnp.broadcast_to(jnp.sum(levels, axis=0, keepdims=True), (8, 128))
                over_north[1] = jnp.where(cross, extra, over_north[1])
            blended = each(
                lambda c, a, b, d, e: c + HORIZONTAL_RATE * (a - b + d - e),
                q, over_east, west_within(over_east), over_north, south_pair(over_north),
            )
            for j in range(2):
                scaled_all[field, chunk, j] = thick * blended[j]

    def at_level(tile, k):
        shift = (128 - 16 * (k % CHUNK)) & 127
        return lroll(tile, shift) if shift else tile

    above = prev_gain = [zero, zero]
    prev = [[zero, zero], [zero, zero]]
    for k in range(K):
        thick = 0.5 + k / 48.0
        below = [at_level(below_all[k // CHUNK, j], k) for j in range(2)]
        inverse = [1.0 / (thick + above[j] + below[j] - above[j] * prev_gain[j]) for j in range(2)]
        prev_gain = [below[j] * inverse[j] for j in range(2)]
        prev = [
            [
                (at_level(scaled_all[field, k // CHUNK, j], k) + above[j] * prev[field][j]) * inverse[j]
                for j in range(2)
            ]
            for field in range(2)
        ]
        for j in range(2):
            gain[k, j] = prev_gain[j]
            for field in range(2):
                done[field, k, j] = prev[field][j]
        above = below
    low = flux = [[zero, zero], [zero, zero]]
    for k in reversed(range(K)):
        thick = 0.5 + k / 48.0
        low = [[done[field, k, j] + gain[k, j] * low[field][j] for j in range(2)] for field in range(2)]
        flux = [
            [flux[field][j] + jnp.where(k < counts[j], thick * low[field][j], 0.0) for j in range(2)]
            for field, counts in enumerate((sum_u, sum_v))
        ]
        for field in range(2):
            mixed[48 * field + k] = low[field][0]

    def put_together(inner, edge):
        own = [
            jnp.where(lane == 127, to_last(e), jnp.where(lane == 0, to_first(e), q)) for q, e in zip(inner, edge)
        ]
        return own + [jnp.where(lane < 64, to_last(e), to_first(e)) for e in edge]

    flux_u = put_together([flux_inner[0], flux_inner[1]], flux[0])
    flux_v = put_together([flux_inner[2], flux_inner[3]], flux[1])

    valid = jnp.logical_or(lane < 4, lane >= 124)

    def four(n, own):
        pair = [window(n), window(n + HALO)]
        return [own, rows[n - PL_WET + BESIDE_WET]] + [
            jnp.where(valid, jnp.where(lane < 64, to_last(e), to_first(e)), 0.0) for e in pair
        ]

    def east(q):
        return [
            lroll(jnp.where(lane == 0, q[2], q[0]), 127),
            lroll(jnp.where(lane == 0, q[3], q[1]), 127),
            lroll(jnp.where(lane == 0, q[0], q[2]), 127),
            lroll(jnp.where(lane == 0, q[1], q[3]), 127),
        ]

    def west(q):
        return [
            lroll(jnp.where(lane == 127, q[2], q[0]), 1),
            lroll(jnp.where(lane == 127, q[3], q[1]), 1),
            lroll(jnp.where(lane == 127, q[0], q[2]), 1),
            lroll(jnp.where(lane == 127, q[1], q[3]), 1),
        ]

    def north(q):
        return north_pair(q[:2]) + north_pair(q[2:])

    def south(q):
        return south_pair(q[:2]) + south_pair(q[2:])

    level_count = four(PL_WET, flat[0])
    around = [each(jnp.minimum, level_count, shift(level_count)) for shift in (east, west, north, south)]
    for i, c in enumerate(around):
        for j in range(4):
            planes2[4 * i + j] = c[j]
    for j in range(4):
        planes2[16 + j] = level_count[j]
    last = jnp.logical_and(top, sub == 7)
    first_ghost = jnp.logical_and(top, sub == 0)
    flux_v = [
        jnp.where(last, 0.0, flux_v[0]),
        jnp.where(first_ghost, 0.0, flux_v[1]),
        jnp.where(last, 0.0, flux_v[2]),
        jnp.where(first_ghost, 0.0, flux_v[3]),
    ]
    plain = each(
        lambda a, b, c, d: a - b + c - d, flux_u, west(flux_u), flux_v, south(flux_v)
    )
    mirrored = each(
        lambda a, b, c, d: a - b + c - d, east(flux_u), flux_u, north(flux_v), flux_v
    )
    divergence = [
        plain[0],
        jnp.where(ghost, mirrored[1], plain[1]),
        plain[2],
        jnp.where(ghost, mirrored[3], plain[3]),
    ]
    sto = four(PL_STO, flat[1])
    old = four(PL_SUR, flat[2])
    faces = [[FACE_SCALE * depth_of(planes2[4 * i + j]) for j in range(4)] for i in range(4)]
    diagonal = [
        jnp.maximum(sto[j] + faces[0][j] + faces[1][j] + faces[2][j] + faces[3][j], 0.1) for j in range(4)
    ]
    ocean = [planes2[16 + j] > 0.0 for j in range(4)]
    start = [jnp.where(ocean[j], old[j], 0.0) for j in range(4)]
    around = [east(start), west(start), north(start), south(start)]
    inverse = [1.0 / diagonal[j] for j in range(4)]
    basis = []
    for j in range(4):
        forcing = jnp.where(ocean[j], sto[j] * old[j] - FLUX_SCALE * divergence[j], 0.0)
        image = sto[j] * start[j]
        for i in range(4):
            image = image + faces[i][j] * (start[j] - around[i][j])
        basis.append((forcing - image) / diagonal[j])
    z0 = basis

    def spread(z):
        nb = [east(z), west(z), north(z), south(z)]
        return [
            (faces[0][j] * nb[0][j] + faces[1][j] * nb[1][j] + faces[2][j] * nb[2][j] + faces[3][j] * nb[3][j])
            * inverse[j]
            for j in range(4)
        ]

    z1 = spread(z0)
    z2 = spread(z1)
    mixed[ZED + 0] = start[0]
    mixed[ZED + 1] = z0[0]
    mixed[ZED + 2] = z1[0]
    mixed[ZED + 3] = z2[0]
    weighted = [diagonal[0] * z[0] for z in (z0, z1, z2)]
    north_weight = jnp.where(last, 1.0, 2.0)
    edge = z2[0] * (
        2.0 * faces[0][0] * east(z2)[0] + north_weight * faces[2][0] * north(z2)[0]
    )
    products = [
        weighted[0] * z0[0],
        weighted[0] * z1[0],
        weighted[1] * z1[0],
        weighted[1] * z2[0],
        weighted[2] * z2[0],
        edge,
    ]
    row = jnp.zeros((1, 128), F32)
    for i, product in enumerate(products):
        total = jnp.sum(jnp.sum(product, axis=0, keepdims=True), axis=1, keepdims=True)
        row = jnp.where(lane[:1] == i, total, row)
    moments[...] = jnp.broadcast_to(row, moments.shape)


def tracers_down(state, diff, flat, mixed, rec_b, rec_a, far, near, after, gain, done):
    del after
    odd, _, odd_lon = whereabouts()
    lane = lane_iota()
    sub = sub_iota()
    level_count = flat[0]
    zero = jnp.zeros((8, 128), F32)

    def forward(chunk, carry):
        above, prev_gain, prev = carry
        for i in range(CHUNK):
            k = CHUNK * chunk + i
            kf = k.astype(F32)
            thick = thickness_at(kf)
            coefficient = diff[jnp.minimum(k, 46)]
            below = jnp.where(kf + 1.0 < level_count, coefficient * spacing_at(kf), 0.0)
            inverse = 1.0 / (thick + above + below - above * prev_gain)
            new_gain = below * inverse
            gain[chunk, i] = new_gain
            open_face = [kf < mixed[AROUND + face] for face in range(4)]
            new = []
            for f in range(6):
                first = f * 48 + CHUNK * chunk
                q = state[pl.ds((96 + first + i) * 8, 8), :]
                row_a = rec_a[f * 6 + chunk, i : i + 1, :]
                row_b = rec_b[f * 6 + chunk, i : i + 1, :]
                row_n = jnp.broadcast_to(jnp.where(odd == 1, row_b, row_a), (8, 128))
                row_s = jnp.broadcast_to(jnp.where(odd == 1, row_a, row_b), (8, 128))
                tile, j = first >> 7, (first & 127) + i
                a, b = far[LON_WIDE + tile], near[LON_WIDE + tile]
                side = lroll(jnp.where((lane == j).astype(jnp.int32) == odd_lon, a, b), (128 - j) & 127)
                change = jnp.where(open_face[0], lroll(jnp.where(lane == 0, side, q), 127) - q, 0.0)
                change += jnp.where(open_face[1], lroll(jnp.where(lane == 127, side, q), 1) - q, 0.0)
                change += jnp.where(open_face[2], sroll(jnp.where(sub == 0, row_n, q), 7) - q, 0.0)
                change += jnp.where(open_face[3], sroll(jnp.where(sub == 7, row_s, q), 1) - q, 0.0)
                value = (thick * (q + HORIZONTAL_RATE * change) + above * prev[f]) * inverse
                done[f, chunk, i] = value
                new.append(value)
            above, prev_gain, prev = below, new_gain, new
        return above, prev_gain, prev

    lax.fori_loop(0, K // CHUNK, forward, (zero, zero, [zero] * 6))


def tracers_up(gain, done, inner, mixed, out):
    lane = lane_iota()
    for n in range(96):
        edge = mixed[n]
        out[n] = jnp.where(lane == 127, to_last(edge), jnp.where(lane == 0, to_first(edge), inner[n]))
    zero = jnp.zeros((8, 128), F32)

    def backward(step, low):
        chunk = K // CHUNK - 1 - step
        for i in reversed(range(CHUNK)):
            g = gain[chunk, i]
            low = [done[f, chunk, i] + g * low[f] for f in range(6)]
            for f in range(6):
                out[96 + f * 48 + CHUNK * chunk + i] = low[f]
        return low

    lax.fori_loop(0, K // CHUNK, backward, [zero] * 6)


def combine(parts, out):
    out[...] = jnp.broadcast_to(jnp.sum(parts[...], axis=0, keepdims=True), out.shape)


def finish(parts, mixed, surface):
    total = jnp.sum(parts[...], axis=0, keepdims=True)
    nu = [jnp.broadcast_to(total[:, i : i + 1], (8, 128)) for i in range(6)]

    def inner(p, q, shift):
        out = None
        for i, a in enumerate(p):
            for j, b in enumerate(q):
                term = a * b * nu[i + j + shift]
                out = term if out is None else out + term
        return out

    one = jnp.ones((8, 128), F32)
    scaled = [one]
    direction = [one]
    product = nu[0]
    move = [jnp.zeros((8, 128), F32)] * 3
    for iteration in range(ITERS):
        curvature = inner(direction, direction, 0) - inner(direction, direction, 1)
        alpha = jnp.where(curvature > 0.0, product / curvature, 0.0)
        for i, d in enumerate(direction):
            move[i] = move[i] + alpha * d
        if iteration + 1 < ITERS:
            longer = scaled + [jnp.zeros((8, 128), F32)]
            for i, d in enumerate(direction):
                longer[i] = longer[i] - alpha * d
                longer[i + 1] = longer[i + 1] + alpha * d
            scaled = longer
            following = inner(scaled, scaled, 0)
            beta = jnp.where(product > 0.0, following / product, 0.0)
            direction = [
                scaled[i] + (beta * direction[i] if i < len(direction) else 0.0) for i in range(len(scaled))
            ]
            product = following
    surface[...] = sum((move[i] * mixed[ZED + 1 + i] for i in range(3)), mixed[ZED])


VMEM_LIMIT = 24 * 1024 * 1024
FIRST_LIMIT = 60 * 1024 * 1024
VMEM = pl.BlockSpec(memory_space=pltpu.VMEM)
ANY = pl.BlockSpec(memory_space=pl.ANY)


def kernel(body, ins, outs, scratch=(), flops=0, nbytes=0, limit=VMEM_LIMIT, out_spec=VMEM):
    return pl.pallas_call(
        body,
        out_shape=[jax.ShapeDtypeStruct(s, F32) for s in outs],
        in_specs=ins,
        out_specs=[out_spec] * len(outs),
        scratch_shapes=[pltpu.VMEM(s, F32) if isinstance(s, tuple) else s for s in scratch],
        compiler_params=pltpu.CompilerParams(vmem_limit_bytes=limit),
        cost_estimate=pl.CostEstimate(flops=flops, bytes_accessed=nbytes, transcendentals=0),
    )


def lat_pairs(lat, lon):
    first, second = [], []
    for l in range(lat):
        for p in range(lon):
            here = l * lon + p
            first.append((here, (l ^ 1) * lon + p))
            if l == lat - 1:
                second.append((here, l * lon + lon - 1 - p))
            elif l % 2 == 1:
                second.append((here, here + lon))
            elif l > 0:
                second.append((here, here - lon))
    return first, second


def lon_pairs(lon):
    far, near = [], []
    for p in range(lon):
        step = 1 if p % 2 else -1
        far.append((p, (p + step) % lon))
        near.append((p, p ^ 1))
    return far, near


def make_local(mesh_shape):
    lat, lon = mesh_shape["lat"], mesh_shape["lon"]
    pairs_a, pairs_b = lat_pairs(lat, lon)
    pairs_far, pairs_near = lon_pairs(lon)
    both = ("lat", "lon")
    stages = reduction_stages(lat, lon)

    def local(ocean_state, viscosity, diffusivity, wet_levels, storage, surface_old):
        state = ocean_state.reshape(8 * K * 8, 128)
        pay_b, pay_a, uv, flat = kernel(
            pack_lat,
            [ANY] * 5,
            [(LAT_TILES, 8, 128), (ROW_X, 8, 128), (96 * 8, 128), (3, 8, 128)],
            scratch=[
                (LAT_TILES, 8, 128), (ROW_X, 8, 128),
                (96 * 8, 128), (47, 8, 128), (3, 8, 128),
                pltpu.VMEM((8, 128), jnp.int32), pltpu.SemaphoreType.DMA((6,)), pltpu.SemaphoreType.DMA((6,)),
            ],
            out_spec=ANY,
            limit=FIRST_LIMIT,
        )(state, viscosity, wet_levels, storage, surface_old)
        own = (uv, viscosity, flat)
        rec_b = lax.ppermute(pay_b, both, pairs_b)
        rec_a = lax.ppermute(pay_a, both, pairs_a)
        row_b, row_a, far_tracers, near_tracers = kernel(
            pack_tracers,
            [VMEM, VMEM],
            [(SECOND_TILES, 8, 128)] * 2 + [(3, 8, 128)] * 2,
            flops=1_000_000,
            nbytes=2_000_000,
        )(state, viscosity)
        rec_row_b = lax.ppermute(row_b, both, pairs_b)
        rec_row_a = lax.ppermute(row_a, both, pairs_a)
        rows, row_x, pay_far, pay_near = kernel(
            pack_lon,
            [VMEM] * 7,
            [(BESIDE, 8, 128), (6, 8, 128), (LON_TILES, 8, 128), (LON_TILES, 8, 128)],
            scratch=[(3, 8, 128)],
        )(*own, rec_b, rec_a, far_tracers, near_tracers)
        rec_far = lax.ppermute(pay_far, "lon", pairs_far)
        rec_near = lax.ppermute(pay_near, "lon", pairs_near)
        chunked = (K // CHUNK, CHUNK)
        inner, flux_inner = kernel(
            momentum_inner,
            [VMEM] * 7,
            [(2 * K, 8, 128), (4, 8, 128)],
            scratch=[(*chunked, 2, 8, 128), (2, *chunked, 2, 8, 128), (10, 8, 128)],
            flops=10_000_000,
            nbytes=6_000_000,
        )(*own, rows, row_x, rec_row_b, rec_row_a)
        mixed, moments = kernel(
            momentum_entry,
            [VMEM] * 7,
            [(2 * K + 8, 8, 128), (stages[0][1], 128)],
            scratch=[
                (GROUPS, 8, 128), (K // CHUNK, 2, 8, 128), (2, K // CHUNK, 2, 8, 128),
                (K, 2, 8, 128), (2, K, 2, 8, 128), (20, 8, 128),
            ],
        )(flat, rows, flux_inner, pay_far, pay_near, rec_far, rec_near)
        (first_groups, _), (second_groups, second_size) = stages
        parts = lax.all_to_all(moments, both, 0, 0, axis_index_groups=first_groups, tiled=True)
        (parts,) = kernel(combine, [VMEM], [(second_size, 128)])(parts)
        sent = parts
        parts = lax.all_to_all(parts, both, 0, 0, axis_index_groups=second_groups, tiled=True)
        gain, done = kernel(
            tracers_down,
            [VMEM] * 8 + [ANY],
            [(*chunked, 8, 128), (6, *chunked, 8, 128)],
            flops=10_000_000,
            nbytes=6_000_000,
        )(state, diffusivity, flat, mixed, rec_row_b, rec_row_a, rec_far, rec_near, sent)
        (state_out,) = kernel(
            tracers_up, [VMEM] * 4, [(8 * K, 8, 128)], flops=10_000_000, nbytes=6_000_000
        )(gain, done, inner, mixed)
        (surface,) = kernel(finish, [VMEM] * 2, [(8, 128)])(parts, mixed)
        return state_out.reshape(8, K, 8, 128), surface

    return local


def momentum_entry(*refs):
    inputs, outputs, scratch = refs[:7], refs[7:9], refs[9:]
    mixed, moments = outputs
    momentum(*inputs, mixed, moments, *scratch)
    planes2 = scratch[5]
    for face in range(4):
        mixed[AROUND + face] = planes2[4 * face]


def reduction_stages(lat, lon):
    index = np.arange(lat * lon)
    if lat == 32 and lon == 16:
        grid = index.reshape(8, 4, 4, 2, 2)
        along_z = grid.transpose(1, 2, 4, 3, 0).reshape(32, 16)
        rest = grid.transpose(0, 3, 1, 2, 4).reshape(16, 32)
    else:
        grid = index.reshape(lat, lon)
        along_z, rest = grid.T, grid
    return [(g.tolist(), g.shape[1]) for g in (rest, along_z)]


def solution(mesh):
    placed = (
        P(None, None, "lat", "lon"),
        P(None, "lat", "lon"),
        P(None, "lat", "lon"),
        P("lat", "lon"),
        P("lat", "lon"),
        P("lat", "lon"),
    )
    return jax.shard_map(
        make_local(dict(mesh.shape)),
        mesh=mesh,
        in_specs=placed,
        out_specs=(P(None, None, "lat", "lon"), P("lat", "lon")),
        check_vma=False,
    )
```
